128 devices in a mesh: dp: 16 (over z, x_lo, core), mp: 8 (over x_hi, y).
Axes of the slice: x: 4 (x_hi: 2, x_lo: 2; x = x_hi * 2 + x_lo), y: 4, z: 4, core: 2. Of those that a mesh axis runs over, the one named last changes fastest.
Arguments:
- hidden_in: float32 [4096, 1024], P('dp'), may hold values from -6 to 6
- cotangent: float32 [4096, 1024], P('dp'), may hold values from -6 to 6
- scene_lengths: int32 [3], replicated, may hold values from 1 to 2048, as said below
- block_owner: int32 [16], replicated, may hold values from 0 to 15, as said below
- attn_gain: float32 [2, 1024], replicated, may hold values from 0.1 to 1.9
- attn_shift: float32 [2, 1024], replicated, may hold values from -2 to 2
- qkv_weight: bfloat16 [2, 1024, 3, 1024], P(None, None, None, 'mp'), may hold values from -0.1875 to 0.1875
- qv_bias: float32 [2, 2, 16, 64], P(None, None, 'mp'), may hold values from -0.3 to 0.3
- out_weight: bfloat16 [2, 1024, 1024], P(None, 'mp'), may hold values from -3 to 3
- out_bias: float32 [2, 1024], replicated, may hold values from -1.2 to 1.2
- mlp_gain: float32 [2, 1024], replicated, may hold values from 0.1 to 1.9
- mlp_shift: float32 [2, 1024], replicated, may hold values from -2 to 2
- mlp_in_weight: bfloat16 [2, 1024, 4096], P(None, None, 'mp'), may hold values from -0.1875 to 0.1875
- mlp_in_bias: float32 [2, 4096], P(None, 'mp'), may hold values from -0.6 to 0.6
- mlp_out_weight: bfloat16 [2, 4096, 1024], P(None, 'mp'), may hold values from -0.09375 to 0.09375
- mlp_out_bias: float32 [2, 1024], replicated, may hold values from -1.2 to 1.2
Outputs:
- output: float32 [4096, 1024], P('dp')
- input_grad: float32 [4096, 1024], P('dp')
- attn_gain_grad: float32 [2, 1024], P(None, 'dp')
- attn_shift_grad: float32 [2, 1024], P(None, 'dp')
- qkv_weight_grad: float32 [2, 1024, 3, 1024], P(None, 'dp', None, 'mp')
- qv_bias_grad: float32 [2, 2, 16, 64], P(None, None, 'mp', 'dp')
- out_weight_grad: float32 [2, 1024, 1024], P(None, 'mp', 'dp')
- out_bias_grad: float32 [2, 1024], P(None, 'dp')
- mlp_gain_grad: float32 [2, 1024], P(None, 'dp')
- mlp_shift_grad: float32 [2, 1024], P(None, 'dp')
- mlp_in_weight_grad: float32 [2, 1024, 4096], P(None, 'dp', 'mp')
- mlp_in_bias_grad: float32 [2, 64, 64], P(None, 'mp', 'dp')
- mlp_out_weight_grad: float32 [2, 4096, 1024], P(None, 'mp', 'dp')
- mlp_out_bias_grad: float32 [2, 1024], P(None, 'dp')
The draws below stay inside these ranges and needn't reach their ends.
Inputs may be any that keep to these rules, and one draw needn't show every extreme that they name: `scene_lengths`: scene lengths add up to 4096; the longest scene has exactly 2048 tokens. `block_owner`: each block number appears once.
All inputs are finite; a program needn't handle non-finite values.
Results may differ from the reference program's by a relative error of at most 0.03.
Values may be sent and summed in bfloat16 or wider, within the bound.
No kernel may reach another device: no remote copies, remote signals or barrier semaphores. Data moves between devices by JAX's collectives and lax.ppermute only.
A program may use at most 128 MiB of HBM per device.

```python
import math
import jax
import jax.numpy as jnp
from jax import lax

HEADS = 16
HEAD_DIM = 64
FF = 4096
LAYERS = 2
SCENES = 3
TOK_DEV = 256
D = 1024
TOKENS = 4096
BLOCKS = 16


def scene_plan(key):
    half = TOKENS // 2
    rest = half - (SCENES - 1)
    place_key = jax.random.fold_in(key, 101)
    cut_key = jax.random.fold_in(key, 102)
    perm_key = jax.random.fold_in(key, 103)
    pick_key = jax.random.fold_in(key, 104)
    longest = jax.random.randint(place_key, (), 0, SCENES, dtype=jnp.int32)
    cuts = jnp.sort(jax.random.randint(cut_key, (SCENES - 2,), 0, rest + 1, dtype=jnp.int32))
    edges = jnp.concatenate([jnp.zeros((1,), jnp.int32), cuts, jnp.full((1,), rest, jnp.int32)])
    others = edges[1:] - edges[:-1] + 1
    order = jnp.arange(SCENES, dtype=jnp.int32)
    other_index = jnp.clip(jnp.where(order < longest, order, order - 1), 0, SCENES - 2)
    lengths = jnp.where(order == longest, half, others[other_index]).astype(jnp.int32)
    start = jnp.sum(jnp.where(order < longest, lengths, 0))
    first_full = (start + TOK_DEV - 1) // TOK_DEV
    block_ids = jnp.arange(BLOCKS, dtype=jnp.int32)
    scores = jax.random.permutation(perm_key, BLOCKS).astype(jnp.int32)
    special_rank = jax.random.permutation(pick_key, 3).astype(jnp.int32)
    offset_block = block_ids - first_full
    is_special = (offset_block >= 0) & (offset_block < 3)
    special_score = special_rank[jnp.clip(offset_block, 0, 2)] - 3
    scores = jnp.where(is_special, special_score, scores)
    block_order = jnp.argsort(scores, stable=True).astype(jnp.int32)
    middle = BLOCKS // 2
    device_key = jnp.where(block_ids == 0, -3, jnp.where(block_ids == middle, -2, jnp.where(block_ids == BLOCKS - 1, -1, block_ids)))
    device_order = jnp.argsort(device_key, stable=True).astype(jnp.int32)
    owner = jnp.zeros((BLOCKS,), jnp.int32).at[device_order].set(block_order)
    return (lengths, owner)


def draw_scene_lengths(key, part):
    lengths, owner = scene_plan(key)
    return lengths


def draw_block_owner(key, part):
    lengths, owner = scene_plan(key)
    return owner


def steps_of(stream_key, shape, pieces, least, high):
    def one(position, blocks):
        draws = jax.random.uniform(jax.random.fold_in(jax.random.fold_in(stream_key, 6), position), (blocks,), jnp.float32, least / len(pieces), high / len(pieces))
        return jnp.repeat(jnp.exp(draws), shape[position] // blocks).reshape((-1,) + (1,) * (len(shape) - position - 1))

    loudness = one(*pieces[0])
    for cut in pieces[1:]:
        loudness = loudness * one(*cut)
    return loudness


def bell_draw(stream_key, shape, deviation, limit, pieces=(), held_as=jnp.bfloat16):
    entries = deviation * jax.random.normal(stream_key, shape, jnp.float32)
    if pieces:
        entries = entries * steps_of(stream_key, shape, pieces, -0.22, 0.18)
    return jnp.clip(entries, -limit, limit).astype(held_as)


def setup_inputs(seed: int = 0) -> dict:
    arg_keys = jax.random.split(jax.random.key(seed), 17)
    hidden_in = bell_draw(arg_keys[0], (TOKENS, D), 1.0, 6.0, ((0, 16),), jnp.float32)
    cotangent = bell_draw(arg_keys[1], (TOKENS, D), 1.0, 6.0, ((0, 16),), jnp.float32)
    scene_lengths = draw_scene_lengths(jax.random.fold_in(arg_keys[16], 71), 0)
    block_owner = draw_block_owner(jax.random.fold_in(arg_keys[16], 71), 0)
    attn_gain = jnp.clip(1.0 + 0.18 * jax.random.normal(arg_keys[4], (LAYERS, D), jnp.float32), 0.1, 1.9)
    attn_shift = bell_draw(arg_keys[5], (LAYERS, D), 0.3, 2.0, (), jnp.float32)
    qkv_weight = bell_draw(arg_keys[6], (LAYERS, D, 3, D), D ** -0.5, 0.1875, ((3, 8),))
    qv_bias = bell_draw(arg_keys[7], (LAYERS, 2, HEADS, HEAD_DIM), 0.05, 0.3, ((2, 8),), jnp.float32)
    out_weight = bell_draw(arg_keys[8], (LAYERS, D, D), (max(D // 256, 2)) ** -0.5, 3.0, ((1, 8),))
    out_bias = bell_draw(arg_keys[9], (LAYERS, D), 0.2, 1.2, (), jnp.float32)
    mlp_gain = jnp.clip(1.0 + 0.18 * jax.random.normal(arg_keys[10], (LAYERS, D), jnp.float32), 0.1, 1.9)
    mlp_shift = bell_draw(arg_keys[11], (LAYERS, D), 0.3, 2.0, (), jnp.float32)
    mlp_in_weight = bell_draw(arg_keys[12], (LAYERS, D, FF), D ** -0.5, 0.1875, ((2, 8),))
    mlp_in_bias = bell_draw(arg_keys[13], (LAYERS, FF), 0.1, 0.6, ((1, 8),), jnp.float32)
    mlp_out_weight = bell_draw(arg_keys[14], (LAYERS, FF, D), FF ** -0.5, 0.09375, ((1, 8),))
    mlp_out_bias = bell_draw(arg_keys[15], (LAYERS, D), 0.2, 1.2, (), jnp.float32)
    return dict(hidden_in=hidden_in, cotangent=cotangent, scene_lengths=scene_lengths, block_owner=block_owner, attn_gain=attn_gain, attn_shift=attn_shift, qkv_weight=qkv_weight, qv_bias=qv_bias, out_weight=out_weight, out_bias=out_bias, mlp_gain=mlp_gain, mlp_shift=mlp_shift, mlp_in_weight=mlp_in_weight, mlp_in_bias=mlp_in_bias, mlp_out_weight=mlp_out_weight, mlp_out_bias=mlp_out_bias)


@jax.custom_vjp
def low(v):
    return lax.optimization_barrier(v.astype(jnp.bfloat16)).astype(jnp.float32)

@jax.custom_vjp
def low_back(v):
    return v

def low_keep(v):
    return (low(v), None)

def low_pass(kept, grad):
    return (grad,)

def back_keep(v):
    return (v, None)

def back_low(kept, grad):
    return (low(grad),)
low.defvjp(low_keep, low_pass)
low_back.defvjp(back_keep, back_low)
norm_eps = 1e-05
highest = lax.Precision.HIGHEST

def layer_norm(inputs, gain_row, shift_row):
    average = lax.optimization_barrier(jnp.mean(inputs, axis=-1, keepdims=True))
    centered = inputs - average
    variance = lax.optimization_barrier(jnp.mean(centered * centered, axis=-1, keepdims=True))
    return centered * lax.rsqrt(variance + norm_eps) * gain_row + shift_row

def scene_labels(scene_lengths, block_owner, block_rows):
    row_index = jnp.arange(block_owner.shape[0] * block_rows, dtype=jnp.int32)
    placed = block_owner[row_index // block_rows] * block_rows + row_index % block_rows
    bounds = jnp.cumsum(scene_lengths)
    return lax.optimization_barrier(jnp.sum((placed[:, None] >= bounds[None, :]).astype(jnp.int32), axis=1))

def one_layer(hidden, weights, labels):
    attn_gain, attn_shift, qkv_weight, qv_bias, out_weight, out_bias, mlp_gain, mlp_shift, mlp_in_weight, mlp_in_bias, mlp_out_weight, mlp_out_bias = weights
    tokens_total, width = hidden.shape
    heads, head_dim = (qv_bias.shape[1], qv_bias.shape[2])
    scale = 1.0 / math.sqrt(head_dim)
    normed = low(layer_norm(hidden, attn_gain, attn_shift))
    projected = jnp.einsum('td,dje->tje', normed, qkv_weight, precision=highest)
    query = low_back(low(projected[:, 0] + qv_bias[0].reshape(width)))
    keys = low_back(low(projected[:, 1]))
    values = low_back(low(projected[:, 2] + qv_bias[1].reshape(width)))
    key_heads = keys.reshape(tokens_total, heads, head_dim)
    value_heads = values.reshape(tokens_total, heads, head_dim)

    def attend(block):
        block_query, block_labels = block
        scores = low_back(jnp.einsum('qhe,khe->hqk', block_query, key_heads, precision=highest) * scale)
        same_scene = (block_labels[:, None] == labels[None, :])[None]
        masked = jnp.where(same_scene, scores, -1e+30)
        peak = lax.optimization_barrier(jnp.max(masked, axis=-1, keepdims=True))
        exponent = jnp.where(same_scene, jnp.exp(masked - peak), 0.0)
        probs = exponent / lax.optimization_barrier(jnp.sum(exponent, axis=-1, keepdims=True))
        return jnp.einsum('hqk,khe->qhe', low(probs), value_heads, precision=highest)
    block_size = math.gcd(512, tokens_total)
    block_count = tokens_total // block_size
    attended = lax.map(jax.checkpoint(attend), (query.reshape(block_count, block_size, heads, head_dim), labels.reshape(block_count, block_size)))
    attended = low_back(low(attended.reshape(tokens_total, width)))
    branch = low_back(jnp.dot(attended, out_weight, precision=highest, preferred_element_type=jnp.float32) + out_bias)
    middle = hidden + branch
    normed_mlp = low(layer_norm(middle, mlp_gain, mlp_shift))
    before = low_back(jnp.dot(normed_mlp, mlp_in_weight, precision=highest, preferred_element_type=jnp.float32) + mlp_in_bias)
    active = low(jax.nn.gelu(before, approximate=False))
    mlp_branch = low_back(jnp.dot(active, mlp_out_weight, precision=highest, preferred_element_type=jnp.float32) + mlp_out_bias)
    return middle + mlp_branch

def reference(hidden_in, cotangent, scene_lengths, block_owner, attn_gain, attn_shift, qkv_weight, qv_bias, out_weight, out_bias, mlp_gain, mlp_shift, mlp_in_weight, mlp_in_bias, mlp_out_weight, mlp_out_bias):
    labels = scene_labels(scene_lengths, block_owner, TOK_DEV)
    params = (attn_gain, attn_shift, qkv_weight.astype(jnp.float32), qv_bias, out_weight.astype(jnp.float32), out_bias, mlp_gain, mlp_shift, mlp_in_weight.astype(jnp.float32), mlp_in_bias, mlp_out_weight.astype(jnp.float32), mlp_out_bias)

    def forward(inputs, weight_set):
        hidden = inputs
        for layer in range(LAYERS):
            hidden = one_layer(hidden, tuple((stacked[layer] for stacked in weight_set)), labels)
        return hidden
    output, pullback = jax.vjp(forward, hidden_in, params)
    input_grad, grads = pullback(cotangent)
    return (output, input_grad, grads[0], grads[1], grads[2], grads[3], grads[4], grads[5], grads[6], grads[7], grads[8], grads[9].reshape(LAYERS, FF // 64, 64), grads[10], grads[11])
```

```python
import math

import jax
import jax.numpy as jnp
from jax import lax
from jax.sharding import PartitionSpec as P

norm_eps = 1e-05
f32 = jnp.float32
bf16 = jnp.bfloat16


def row_stats(inputs):
    average = jnp.mean(inputs, axis=-1, keepdims=True)
    centered = inputs - average
    variance = jnp.mean(centered * centered, axis=-1, keepdims=True)
    return centered, lax.rsqrt(variance + norm_eps)


def layer_norm(inputs, gain_row, shift_row):
    centered, inverse = row_stats(inputs)
    return centered * inverse * gain_row + shift_row


def norm_backward(grad, inputs, gain_row):
    centered, inverse = row_stats(inputs)
    unit = centered * inverse
    scaled = grad * gain_row
    first = jnp.mean(scaled, axis=-1, keepdims=True)
    second = jnp.mean(scaled * unit, axis=-1, keepdims=True)
    into = (scaled - first - unit * second) * inverse
    return into, jnp.sum(grad * unit, axis=0), jnp.sum(grad, axis=0)


def labels_of(positions, scene_lengths):
    bounds = jnp.cumsum(scene_lengths)
    return jnp.sum((positions[:, None] >= bounds[None, :]).astype(jnp.int32), axis=1)


def exact_gelu(inner):
    return jax.nn.gelu(inner, approximate=False)


def chip_groups(count):
    return [list(range(core, count, 2)) for core in range(2)]


def other_core(count):
    return [(index, index ^ 1) for index in range(count)]


def scatter_mp(partial):
    parts = lax.axis_size("mp")
    rows = partial.shape[0] // parts
    moved = lax.all_to_all(partial, "mp", 0, 0, tiled=True)
    return jnp.sum(moved.reshape(parts, rows, -1).astype(f32), axis=0)


def gather_mp(block):
    parts = lax.axis_size("mp")
    spread = jnp.broadcast_to(block[None], (parts,) + block.shape)
    return lax.all_to_all(spread.reshape((-1,) + block.shape[1:]), "mp", 0, 0, tiled=True)


def gather_dp(block):
    count = lax.axis_size("dp")
    spread = jnp.broadcast_to(block[None], (count // 2,) + block.shape)
    spread = spread.reshape((-1,) + block.shape[1:])
    mine = lax.all_to_all(
        spread, "dp", 0, 0, tiled=True, axis_index_groups=chip_groups(count)
    )
    theirs = lax.ppermute(mine, "dp", other_core(count))
    return jnp.concatenate([mine, theirs], axis=0)


def core_order(gathered, block_rows):
    core = lax.axis_index("dp") % 2
    split = gathered.reshape((-1, 2, block_rows) + gathered.shape[1:])
    mine = lax.dynamic_index_in_dim(split, core, axis=1, keepdims=False)
    theirs = lax.dynamic_index_in_dim(split, 1 - core, axis=1, keepdims=False)
    return jnp.concatenate([mine, theirs], axis=0).reshape(gathered.shape)


def scatter_dp_rows(partial):
    count = lax.axis_size("dp")
    rows = partial.shape[0] // count
    core = lax.axis_index("dp") % 2
    split = partial.reshape(count // 2, 2, rows, partial.shape[1])
    away = lax.dynamic_index_in_dim(split, 1 - core, axis=1, keepdims=False)
    mine = lax.dynamic_index_in_dim(split, core, axis=1, keepdims=False)
    other = lax.ppermute(away.astype(bf16), "dp", other_core(count))
    both = (mine.astype(f32) + other.astype(f32)).astype(bf16)
    both = both.reshape(-1, partial.shape[1])
    moved = lax.all_to_all(both, "dp", 0, 0, tiled=True, axis_index_groups=chip_groups(count))
    return jnp.sum(moved.reshape(count // 2, rows, -1).astype(f32), axis=0)


def heads_of(rows, heads):
    return rows.reshape(rows.shape[0], heads, -1)


def attend(query, key_all, value_all, same_scene, heads):
    scale = 1.0 / math.sqrt(query.shape[1] // heads)
    scores = (
        jnp.einsum(
            "qhe,khe->hqk",
            heads_of(query, heads),
            heads_of(key_all, heads),
            preferred_element_type=f32,
        )
        * scale
    )
    masked = jnp.where(same_scene[None], scores, -1e30)
    peak = jnp.max(masked, axis=-1, keepdims=True)
    exponent = jnp.where(same_scene[None], jnp.exp(masked - peak), 0.0)
    totals = jnp.sum(exponent, axis=-1, keepdims=True)
    probs = (exponent / totals).astype(bf16)
    attended = jnp.einsum(
        "hqk,khe->qhe", probs, heads_of(value_all, heads), preferred_element_type=f32
    )
    return attended.reshape(query.shape[0], -1), (peak + jnp.log(totals))[..., 0]


def query_side(query, key_all, value_all, grad_own, delta, log_total, same_scene, heads):
    scale = 1.0 / math.sqrt(query.shape[1] // heads)
    scores = jnp.einsum(
        "qhe,khe->hqk", heads_of(query, heads), heads_of(key_all, heads), preferred_element_type=f32
    )
    probs = jnp.where(
        same_scene[None], jnp.exp(jnp.minimum(scores * scale - log_total[..., None], 1.0)), 0.0
    )
    grad_probs = jnp.einsum(
        "qhe,khe->hqk",
        heads_of(grad_own, heads),
        heads_of(value_all, heads),
        preferred_element_type=f32,
    )
    grad_scores = (probs * (grad_probs - delta[..., None])).astype(bf16)
    out = (
        jnp.einsum(
            "hqk,khe->qhe", grad_scores, heads_of(key_all, heads), preferred_element_type=f32
        )
        * scale
    )
    return out.reshape(query.shape).astype(bf16)


def key_side(query_all, keys, values, grad_all, delta_all, log_all, same_scene, heads):
    scale = 1.0 / math.sqrt(keys.shape[1] // heads)
    scores = jnp.einsum(
        "qhe,khe->hqk", heads_of(query_all, heads), heads_of(keys, heads), preferred_element_type=f32
    )
    probs = jnp.where(
        same_scene.T[None], jnp.exp(jnp.minimum(scores * scale - log_all[..., None], 1.0)), 0.0
    )
    grad_probs = jnp.einsum(
        "qhe,khe->hqk",
        heads_of(grad_all, heads),
        heads_of(values, heads),
        preferred_element_type=f32,
    )
    grad_scores = (probs * (grad_probs - delta_all[..., None])).astype(bf16)
    key_grad = (
        jnp.einsum(
            "hqk,qhe->khe", grad_scores, heads_of(query_all, heads), preferred_element_type=f32
        )
        * scale
    )
    value_grad = jnp.einsum(
        "hqk,qhe->khe", probs.astype(bf16), heads_of(grad_all, heads), preferred_element_type=f32
    )
    return key_grad.reshape(keys.shape).astype(bf16), value_grad.reshape(keys.shape).astype(bf16)


def over_tokens(left, right):
    return lax.dot_general(left, right, (((0,), (0,)), ((), ())), preferred_element_type=f32)


def times_transposed(left, right):
    return lax.dot_general(left, right, (((1,), (1,)), ((), ())), preferred_element_type=f32)


def body(
    hidden_in,
    cotangent,
    scene_lengths,
    block_owner,
    attn_gain,
    attn_shift,
    qkv_weight,
    qv_bias,
    out_weight,
    out_bias,
    mlp_gain,
    mlp_shift,
    mlp_in_weight,
    mlp_in_bias,
    mlp_out_weight,
    mlp_out_bias,
):
    block_rows, width = hidden_in.shape
    layers = attn_gain.shape[0]
    heads = qv_bias.shape[2]
    local = heads * qv_bias.shape[3]
    dp_count, mp_count = lax.axis_size("dp"), lax.axis_size("mp")
    dp_index, mp_index = lax.axis_index("dp"), lax.axis_index("mp")
    own_rows = block_rows // mp_count
    dp_columns = width // dp_count

    def own_part(rows):
        return lax.dynamic_slice_in_dim(rows, mp_index * own_rows, own_rows)

    within = jnp.arange(block_rows, dtype=jnp.int32)
    placed = (block_owner[:, None] * block_rows + within[None, :]).reshape(-1)
    own_place = block_owner[dp_index] * block_rows + within
    labels_all = core_order(labels_of(placed, scene_lengths), block_rows)
    own_labels = labels_of(own_place, scene_lengths)
    same_scene = own_labels[:, None] == labels_all[None, :]

    qkv_flat = [qkv_weight[layer].reshape(width, 3 * local) for layer in range(layers)]
    bias_flat = qv_bias.reshape(layers, 2, local)

    kept = []
    hidden = own_part(hidden_in)
    normed = layer_norm(hidden_in, attn_gain[0], attn_shift[0]).astype(bf16)
    for layer in range(layers):
        if layer:
            normed = gather_mp(layer_norm(hidden, attn_gain[layer], attn_shift[layer]).astype(bf16))
        projected = jnp.dot(normed, qkv_flat[layer], preferred_element_type=f32)
        query = (projected[:, :local] + bias_flat[layer, 0]).astype(bf16)
        keys = projected[:, local : 2 * local].astype(bf16)
        values = (projected[:, 2 * local :] + bias_flat[layer, 1]).astype(bf16)
        key_value = gather_dp(jnp.concatenate([keys, values], axis=1))
        query_all = lax.all_gather(query, "dp", axis=0, tiled=True)
        key_all, value_all = key_value[:, :local], key_value[:, local:]
        attended, log_total = attend(query, key_all, value_all, same_scene, heads)
        log_all = lax.all_gather(log_total, "dp", axis=1, tiled=True)
        attended_low = attended.astype(bf16)
        attn_part = jnp.dot(attended_low, out_weight[layer], preferred_element_type=f32)
        middle = hidden + scatter_mp(attn_part.astype(bf16)) + out_bias[layer]
        normed_mlp = gather_mp(
            layer_norm(middle, mlp_gain[layer], mlp_shift[layer]).astype(bf16)
        )
        before = (
            jnp.dot(normed_mlp, mlp_in_weight[layer], preferred_element_type=f32)
            + mlp_in_bias[layer]
        )
        active = exact_gelu(before).astype(bf16)
        mlp_part = jnp.dot(active, mlp_out_weight[layer], preferred_element_type=f32)
        after = middle + scatter_mp(mlp_part.astype(bf16)) + mlp_out_bias[layer]
        kept.append(
            dict(
                hidden=hidden,
                normed=normed,
                query=query,
                keys=keys,
                values=values,
                key_all=key_all,
                value_all=value_all,
                query_all=query_all,
                log_total=log_total,
                log_all=log_all,
                attended=attended,
                attended_low=attended_low,
                middle=middle,
                normed_mlp=normed_mlp,
                before=before,
                active=active,
            )
        )
        hidden = after
    output = lax.all_gather(hidden, "mp", axis=0, tiled=True)

    grad_full = cotangent.astype(bf16)
    grad_own = own_part(cotangent)
    large = {}
    small = {}
    bias_grads = []
    for layer in reversed(range(layers)):
        kept_now = kept[layer]
        if layer < layers - 1:
            grad_full = gather_mp(grad_own.astype(bf16))
        down_bias_grad = jnp.sum(grad_own.astype(bf16).astype(f32), axis=0)
        grad_active = times_transposed(grad_full, mlp_out_weight[layer])
        ignored, gelu_pull = jax.vjp(exact_gelu, kept_now["before"])
        grad_before = gelu_pull(grad_active)[0].astype(bf16)
        normed_partial = times_transposed(grad_before, mlp_in_weight[layer]).astype(bf16)
        mlp_normed_grad = scatter_mp(normed_partial)
        down_grad = over_tokens(grad_full, kept_now["active"])
        in_grad = over_tokens(kept_now["normed_mlp"], grad_before)
        in_bias_grad = jnp.sum(grad_before.astype(f32), axis=0)
        into, gain_two_grad, shift_two_grad = norm_backward(
            mlp_normed_grad, kept_now["middle"], mlp_gain[layer]
        )
        middle_grad = grad_own + into
        branch_own = middle_grad.astype(bf16)
        out_bias_grad = jnp.sum(branch_own.astype(f32), axis=0)
        grad_branch = gather_mp(branch_own)
        grad_attended = times_transposed(grad_branch, out_weight[layer]).astype(bf16)
        out_grad = over_tokens(grad_branch, kept_now["attended_low"])
        delta = jnp.sum(
            heads_of(grad_attended.astype(f32) * kept_now["attended"], heads), axis=-1
        ).T
        high = delta.astype(bf16)
        low = (delta - high.astype(f32)).astype(bf16)
        packed = jnp.concatenate([high, low], axis=0).reshape(-1, local)
        padded = jnp.zeros((16 - packed.shape[0], local), bf16)
        message = jnp.concatenate([grad_attended, packed, padded], axis=0)
        got = gather_dp(message).reshape(dp_count, block_rows + 16, local)
        grad_all = got[:, :block_rows].reshape(-1, local)
        split = got[:, block_rows : block_rows + packed.shape[0]].reshape(
            dp_count, 2, heads, block_rows
        )
        delta_all = (split[:, 0].astype(f32) + split[:, 1].astype(f32)).transpose(1, 0, 2)
        delta_all = delta_all.reshape(heads, -1)
        query_grad = query_side(
            kept_now["query"],
            kept_now["key_all"],
            kept_now["value_all"],
            grad_attended,
            delta,
            kept_now["log_total"],
            same_scene,
            heads,
        )
        key_grad, value_grad = key_side(
            core_order(kept_now["query_all"], block_rows),
            kept_now["keys"],
            kept_now["values"],
            grad_all,
            delta_all,
            core_order(kept_now["log_all"].T, block_rows).T,
            same_scene,
            heads,
        )
        proj_grad = jnp.concatenate([query_grad, key_grad, value_grad], axis=1)
        first_partial = times_transposed(proj_grad, qkv_flat[layer])
        first_normed_grad = scatter_mp(first_partial.astype(bf16))
        qkv_grad = over_tokens(kept_now["normed"], proj_grad)
        into, gain_one_grad, shift_one_grad = norm_backward(
            first_normed_grad, kept_now["hidden"], attn_gain[layer]
        )
        grad_own = middle_grad + into
        if layer == 0:
            centered, inverse = row_stats(hidden_in)
            rounded = first_partial.astype(bf16).astype(f32)
            gain_one_grad = jnp.sum(rounded * (centered * inverse), axis=0)
            shift_one_grad = jnp.sum(rounded, axis=0)
        small[layer] = [
            gain_one_grad,
            shift_one_grad,
            out_bias_grad,
            gain_two_grad,
            shift_two_grad,
            down_bias_grad,
        ]
        large[layer] = dict(qkv=qkv_grad, out=out_grad, inner=in_grad, down=down_grad)
        bias_grads.append(
            jnp.stack(
                [
                    jnp.sum(query_grad.astype(f32), axis=0),
                    jnp.sum(value_grad.astype(f32), axis=0),
                ]
            )
            .reshape(2 * heads, dp_count, -1)
            .transpose(1, 0, 2)
            .reshape(dp_count, -1)
        )
        bias_grads.append(
            in_bias_grad.reshape(-1, dp_count, 64 // dp_count)
            .transpose(1, 0, 2)
            .reshape(dp_count, -1)
        )

    rows_small = jnp.stack(small[0] + small[1])
    count_small = rows_small.shape[0]
    rows_small = rows_small.reshape(count_small, dp_count, dp_columns).transpose(1, 0, 2)
    message = jnp.concatenate([rows_small.reshape(dp_count, -1)] + bias_grads, axis=1)
    message_len = message.shape[1]
    message = jnp.pad(message, ((0, 0), (0, -message_len % 1024)))
    got_small = lax.all_to_all(message.reshape(-1, 128), "dp", 0, 0, tiled=True)
    got_small = jnp.sum(got_small.reshape(dp_count, -1), axis=0)
    mp_small = got_small[: count_small * dp_columns].reshape(1, -1)
    mp_small = jnp.pad(mp_small, ((0, 15), (0, width - mp_small.shape[1])))
    tail = gather_mp(jnp.concatenate([grad_own, mp_small], axis=0).astype(bf16))
    tail = tail.reshape(mp_count, own_rows + 16, width)
    input_grad = tail[:, :own_rows].reshape(block_rows, width).astype(f32)
    norm_small = jnp.sum(tail[:, own_rows, : count_small * dp_columns].astype(f32), axis=0)
    norm_small = norm_small.reshape(2, 6, dp_columns)

    first = lax.psum_scatter(
        jnp.concatenate([large[1]["inner"], large[1]["down"]], axis=1).astype(bf16),
        "dp",
        scatter_dimension=0,
        tiled=True,
    ).astype(f32)
    second = lax.psum_scatter(
        jnp.concatenate(
            [large[1]["qkv"], large[1]["out"], large[0]["inner"], large[0]["down"]], axis=1
        ).astype(bf16),
        "dp",
        scatter_dimension=0,
        tiled=True,
    ).astype(f32)
    third = scatter_dp_rows(jnp.concatenate([large[0]["out"], large[0]["qkv"]], axis=1).astype(bf16))
    ff_local = mlp_in_bias.shape[1]
    qkv_own = [third[:, local:], second[:, : 3 * local]]
    out_own = [third[:, :local], second[:, 3 * local : 4 * local]]
    in_own = [second[:, 4 * local : 4 * local + ff_local], first[:, :ff_local]]
    down_own = [second[:, 4 * local + ff_local :], first[:, ff_local:]]

    bias_start = count_small * dp_columns
    bias_len = [bias_grads[0].shape[1], bias_grads[1].shape[1]]
    pieces = []
    for piece in range(2 * layers):
        pieces.append(got_small[bias_start : bias_start + bias_len[piece % 2]])
        bias_start += bias_len[piece % 2]
    qv_own = jnp.stack([pieces[2], pieces[0]]).reshape(layers, 2, heads, -1)
    in_bias_own = jnp.stack([pieces[3], pieces[1]]).reshape(layers, ff_local // 64, -1)
    return (
        output,
        input_grad,
        norm_small[:, 0],
        norm_small[:, 1],
        jnp.stack(qkv_own).reshape(layers, dp_columns, 3, local),
        qv_own,
        jnp.stack([piece.T for piece in out_own]),
        norm_small[:, 2],
        norm_small[:, 3],
        norm_small[:, 4],
        jnp.stack(in_own),
        in_bias_own,
        jnp.stack([piece.T for piece in down_own]),
        norm_small[:, 5],
    )


def solution(mesh):
    in_specs = (
        P("dp", None),
        P("dp", None),
        P(),
        P(),
        P(),
        P(),
        P(None, None, None, "mp"),
        P(None, None, "mp", None),
        P(None, "mp", None),
        P(),
        P(),
        P(),
        P(None, None, "mp"),
        P(None, "mp"),
        P(None, "mp", None),
        P(),
    )
    out_specs = (
        P("dp", None),
        P("dp", None),
        P(None, "dp"),
        P(None, "dp"),
        P(None, "dp", None, "mp"),
        P(None, None, "mp", "dp"),
        P(None, "mp", "dp"),
        P(None, "dp"),
        P(None, "dp"),
        P(None, "dp"),
        P(None, "dp", "mp"),
        P(None, "mp", "dp"),
        P(None, "mp", "dp"),
        P(None, "dp"),
    )
    return jax.shard_map(body, mesh=mesh, in_specs=in_specs, out_specs=out_specs, check_vma=False)
```

```python
import functools
import math

import jax
import jax.numpy as jnp
from jax import lax
from jax.experimental import pallas as pl
from jax.experimental.pallas import tpu as pltpu
from jax.sharding import PartitionSpec as P

norm_eps = 1e-05
f32 = jnp.float32
bf16 = jnp.bfloat16
far = -1e30


def chip_groups(count):
    return [list(range(core, count, 2)) for core in range(2)]


def other_core(count):
    return [(index, index ^ 1) for index in range(count)]


def exchange_mp(spread):
    return lax.all_to_all(spread, "mp", 0, 0, tiled=True)


def gather_dp(block):
    count = lax.axis_size("dp")
    spread = jnp.broadcast_to(block[None], (count // 2,) + block.shape)
    mine = lax.all_to_all(
        spread, "dp", 0, 0, tiled=True, axis_index_groups=chip_groups(count)
    )
    theirs = lax.ppermute(mine, "dp", other_core(count))
    return mine, theirs


def whole(memory=pltpu.VMEM):
    return pl.BlockSpec(memory_space=memory)


def of_layer(stacked, layer):
    tail = stacked.shape[1:]
    return pl.BlockSpec((1,) + tail, lambda step: (layer,) + (0,) * len(tail))


def plain(array):
    return pl.BlockSpec(array.shape, lambda step: (0,) * len(array.shape))


def run_kernel(kernel, inputs, in_specs, outputs, flops=0, scratch=(), limit=48):
    moved = sum(math.prod(shape) * jnp.dtype(kind).itemsize for shape, kind in outputs)
    moved += sum(item.size * item.dtype.itemsize for item in inputs)
    return pl.pallas_call(
        kernel,
        grid=(1,),
        in_specs=in_specs,
        out_specs=[
            pl.BlockSpec(shape, functools.partial(lambda rank, step: (0,) * rank, len(shape)))
            for shape, kind in outputs
        ],
        out_shape=[jax.ShapeDtypeStruct(shape, kind) for shape, kind in outputs],
        scratch_shapes=list(scratch),
        compiler_params=pltpu.CompilerParams(vmem_limit_bytes=limit * 2**20),
        cost_estimate=pl.CostEstimate(flops=flops, bytes_accessed=moved, transcendentals=0),
    )(*inputs)


def dot_nn(left, right):
    return lax.dot_general(left, right, (((1,), (0,)), ((), ())), preferred_element_type=f32)


def dot_nt(left, right):
    return lax.dot_general(left, right, (((1,), (1,)), ((), ())), preferred_element_type=f32)


def dot_tn(left, right):
    return lax.dot_general(left, right, (((0,), (0,)), ((), ())), preferred_element_type=f32)


def row_stats(inputs):
    average = jnp.mean(inputs, axis=-1, keepdims=True)
    centered = inputs - average
    variance = jnp.mean(centered * centered, axis=-1, keepdims=True)
    return centered, lax.rsqrt(variance + norm_eps)


def add_parts(got_ref):
    total = got_ref[0].astype(f32)
    for part in range(1, got_ref.shape[0]):
        total += got_ref[part].astype(f32)
    return total


def residual_norm(got, residual, bias, bias_layer, gain, shift, norm_layer):
    parts, rows, width = got.shape

    def kernel(got_ref, residual_ref, bias_ref, gain_ref, shift_ref, out_ref, *spread_ref):
        total = residual_ref[...] + add_parts(got_ref) + bias_ref[bias_layer : bias_layer + 1, :]
        out_ref[...] = total
        if norm_layer is not None:
            layer = slice(norm_layer, norm_layer + 1)
            centered, inverse = row_stats(total)
            normed = centered * inverse * gain_ref[layer, :] + shift_ref[layer, :]
            for part in range(parts):
                spread_ref[0][part] = normed.astype(bf16)

    inputs = [got, residual, bias, gain, shift]
    outputs = [((rows, width), f32)]
    if norm_layer is not None:
        outputs.append(((parts, rows, width), bf16))
    return run_kernel(kernel, inputs, [plain(item) for item in inputs], outputs)


def norm_backward(got, inputs, gain, layer, grad, extra=None):
    parts, rows, width = got.shape
    more = 0 if extra is None else 16

    def kernel(got_ref, inputs_ref, gain_ref, grad_ref, *refs):
        out_ref, spread_ref, small_ref = refs[-3:]
        into = add_parts(got_ref)
        centered, inverse = row_stats(inputs_ref[...])
        unit = centered * inverse
        scaled = into * gain_ref[layer : layer + 1, :]
        first = jnp.mean(scaled, axis=-1, keepdims=True)
        second = jnp.mean(scaled * unit, axis=-1, keepdims=True)
        total = grad_ref[...] + (scaled - first - unit * second) * inverse
        out_ref[...] = total
        rounded = total.astype(bf16)
        for part in range(parts):
            spread_ref[part, :rows] = rounded
        if more:
            high = refs[0][...].astype(bf16).astype(f32)
            both = jnp.concatenate([high, refs[0][...] - high], axis=0).astype(bf16)
            for part in range(parts):
                spread_ref[part, rows:, : both.shape[1]] = both
        small_ref[0:1, :] = jnp.sum(into * unit, axis=0, keepdims=True)
        small_ref[1:2, :] = jnp.sum(into, axis=0, keepdims=True)
        small_ref[2:3, :] = jnp.sum(rounded.astype(f32), axis=0, keepdims=True)
        small_ref[3:, :] = jnp.zeros((5, width), f32)

    inputs = [got, inputs, gain, grad] + ([] if extra is None else [extra])
    outputs = [((rows, width), f32), ((parts, rows + more, width), bf16), ((8, width), f32)]
    return run_kernel(kernel, inputs, [plain(item) for item in inputs], outputs)


def label_of(position, table_ref):
    return sum((position >= table_ref[17 + scene]).astype(jnp.int32) for scene in range(3))


def scalar_label(position, table_ref):
    return sum(
        jnp.where(position >= table_ref[17 + scene], 1, 0).astype(jnp.int32) for scene in range(3)
    )


def block_kind(start, own, rows, table_ref):
    first, last = scalar_label(start, table_ref), scalar_label(start + rows - 1, table_ref)
    own_first, own_last = scalar_label(own, table_ref), scalar_label(own + rows - 1, table_ref)
    meets = jnp.logical_and(first <= own_last, own_first <= last)
    alone = jnp.logical_and(first == last, own_first == own_last)
    return meets, jnp.logical_and(meets, alone)


def over_blocks(count, rows, table_ref, step):
    own = table_ref[16]

    def one(index, carry):
        meets, alone = block_kind(table_ref[index], own, rows, table_ref)

        @pl.when(alone)
        def _():
            step(index, False)

        @pl.when(jnp.logical_and(meets, jnp.logical_not(alone)))
        def _():
            step(index, True)

        return carry

    lax.fori_loop(0, count, one, 0)


def head_stack(rows):
    lane = lax.broadcasted_iota(jnp.int32, rows.shape, 1)
    half = rows.shape[1] // 2
    zero = jnp.zeros_like(rows)
    return jnp.concatenate(
        [jnp.where(lane < half, rows, zero), jnp.where(lane >= half, rows, zero)], axis=0
    )


def heads_from_lanes(stacked):
    half, rows = stacked.shape[0] // 2, stacked.shape[1] // 2
    return jnp.concatenate([stacked[:half, :rows], stacked[half:, rows:]], axis=0)


def heads_from_rows(stacked):
    rows = stacked.shape[0] // 2
    lane = lax.broadcasted_iota(jnp.int32, (rows, stacked.shape[1]), 1)
    return jnp.where(lane < stacked.shape[1] // 2, stacked[:rows], stacked[rows:])


def row_pieces(vector, count):
    pieces = []
    rest = vector
    for piece in range(count):
        term = rest.astype(bf16).astype(f32)
        rest = rest - term
        pieces += [term[:, start : start + 128] for start in range(0, vector.shape[1], 128)]
    row = lax.broadcasted_iota(jnp.int32, (16, 128), 0)
    tile = jnp.zeros((16, 128), f32)
    for index, piece in enumerate(pieces):
        tile = jnp.where(row == index, jnp.broadcast_to(piece, (16, 128)), tile)
    return tile.astype(bf16)


def rows_back(tile, count, length):
    tile = tile.astype(f32)
    lines = length // 128
    out = []
    for line in range(lines):
        total = tile[line : line + 1]
        for piece in range(1, count):
            total = total + tile[piece * lines + line : piece * lines + line + 1]
        out.append(total)
    return jnp.concatenate(out, axis=1)


def attention_forward(query, mine, theirs, out_weight, layer, table):
    rows, local = query.shape
    count = mine.shape[0] + theirs.shape[0]
    half = mine.shape[0]
    width = out_weight.shape[2]
    scale = 1.0 / math.sqrt(local // 2)

    def kernel(
        table_ref,
        query_ref,
        mine_ref,
        theirs_ref,
        weight_ref,
        part_ref,
        low_ref,
        flat_ref,
        log_ref,
        message_ref,
        stack_ref,
        peak_ref,
        total_ref,
        sum_ref,
    ):
        scaled = (query_ref[...].astype(f32) * scale).astype(bf16)
        stack_ref[...] = head_stack(scaled)
        peak_ref[...] = jnp.full(peak_ref.shape, far, f32)
        total_ref[...] = jnp.zeros(total_ref.shape, f32)
        sum_ref[...] = jnp.zeros(sum_ref.shape, f32)
        lanes = lax.broadcasted_iota(jnp.int32, (1, 2 * rows), 1)
        place = table_ref[16] + jnp.where(lanes >= rows, lanes - rows, lanes)
        own_label = label_of(place, table_ref)

        def one(block_ref, place_block, start, masked):
            keys = block_ref[place_block, :, :local]
            values = block_ref[place_block, :, local:]
            scores = dot_nt(keys, stack_ref[...])
            if masked:
                position = start + lax.broadcasted_iota(jnp.int32, (rows, 128), 0)
                label = label_of(position, table_ref)
                label = jnp.concatenate([label] * (2 * rows // 128), axis=1)
                same = label == own_label
                scores = jnp.where(same, scores, far)
            old = peak_ref[...]
            new = jnp.maximum(old, jnp.max(scores, axis=0, keepdims=True))
            weight = jnp.exp(scores - new)
            if masked:
                weight = jnp.where(same, weight, 0.0)
            fade = jnp.exp(old - new)
            peak_ref[...] = new
            total_ref[...] = total_ref[...] * fade + jnp.sum(weight, axis=0, keepdims=True)
            sum_ref[...] = sum_ref[...] * fade + dot_tn(values, weight.astype(bf16))

        def step(index, masked):
            start = table_ref[index]

            @pl.when(index < half)
            def _():
                one(mine_ref, index, start, masked)

            @pl.when(index >= half)
            def _():
                one(theirs_ref, index - half, start, masked)

        over_blocks(count, rows, table_ref, step)
        attended = heads_from_lanes(sum_ref[...] / total_ref[...])
        flat_ref[...] = attended
        low = attended.T.astype(bf16)
        low_ref[...] = low
        part = dot_nn(low, weight_ref[0]).astype(bf16)
        part_ref[...] = part.reshape(part_ref.shape)
        log_total = peak_ref[...] + jnp.log(total_ref[...])
        log_ref[...] = log_total
        message_ref[:rows, :] = scaled
        message_ref[rows:, :] = row_pieces(log_total, 3)

    inputs = [table, query, mine, theirs, out_weight]
    mp_count = lax.axis_size("mp")
    return run_kernel(
        kernel,
        inputs,
        [whole(pltpu.SMEM), plain(query), plain(mine), plain(theirs), of_layer(out_weight, layer)],
        [
            ((mp_count, rows // mp_count, width), bf16),
            ((rows, local), bf16),
            ((local, rows), f32),
            ((1, 2 * rows), f32),
            ((rows + 16, local), bf16),
        ],
        flops=8 * rows * count * rows * local,
        scratch=[
            pltpu.VMEM((2 * rows, local), bf16),
            pltpu.VMEM((1, 2 * rows), f32),
            pltpu.VMEM((1, 2 * rows), f32),
            pltpu.VMEM((local, 2 * rows), f32),
        ],
    )


def grad_attended(branch, out_weight, layer, flat):
    rows = branch.shape[0] * branch.shape[1]
    local = out_weight.shape[1]

    def kernel(branch_ref, weight_ref, flat_ref, message_ref, delta_ref):
        grad = dot_nt(branch_ref[...].reshape(rows, -1), weight_ref[0]).astype(bf16)
        product = grad.astype(f32).T * flat_ref[...]
        half = local // 2
        delta = jnp.concatenate(
            [
                jnp.sum(product[:half], axis=0, keepdims=True),
                jnp.sum(product[half:], axis=0, keepdims=True),
            ],
            axis=1,
        )
        delta_ref[...] = delta
        message_ref[:rows, :] = grad
        message_ref[rows:, :] = row_pieces(delta, 3)

    inputs = [branch, out_weight, flat]
    return run_kernel(
        kernel,
        inputs,
        [plain(branch), of_layer(out_weight, layer), plain(flat)],
        [((rows + 16, local), bf16), ((1, 2 * rows), f32)],
        flops=2 * rows * local * branch.shape[2],
    )


def query_side(message, log_total, delta, mine, theirs, grad, table):
    rows, local = grad.shape[0] - 16, grad.shape[1]
    half = mine.shape[0]
    count = 2 * half
    scale = 1.0 / math.sqrt(local // 2)

    def kernel(
        table_ref,
        query_ref,
        log_ref,
        delta_ref,
        mine_ref,
        theirs_ref,
        grad_ref,
        out_ref,
        stack_ref,
        grad_stack_ref,
        sum_ref,
    ):
        stack_ref[...] = head_stack(query_ref[:rows, :])
        grad_stack_ref[...] = head_stack(grad_ref[:rows, :])
        sum_ref[...] = jnp.zeros(sum_ref.shape, f32)
        lanes = lax.broadcasted_iota(jnp.int32, (1, 2 * rows), 1)
        place = table_ref[16] + jnp.where(lanes >= rows, lanes - rows, lanes)
        own_label = label_of(place, table_ref)

        def one(block_ref, place_block, start, masked):
            keys = block_ref[place_block, :, :local]
            values = block_ref[place_block, :, local:]
            scores = dot_nt(keys, stack_ref[...]) - log_ref[...]
            if masked:
                position = start + lax.broadcasted_iota(jnp.int32, (rows, 128), 0)
                label = label_of(position, table_ref)
                label = jnp.concatenate([label] * (2 * rows // 128), axis=1)
                scores = jnp.where(label == own_label, scores, far)
            probs = jnp.exp(scores)
            grad_probs = dot_nt(values, grad_stack_ref[...])
            grad_scores = (probs * (grad_probs - delta_ref[...])).astype(bf16)
            sum_ref[...] += dot_tn(keys, grad_scores)

        def step(index, masked):
            start = table_ref[index]

            @pl.when(index < half)
            def _():
                one(mine_ref, index, start, masked)

            @pl.when(index >= half)
            def _():
                one(theirs_ref, index - half, start, masked)

        over_blocks(count, rows, table_ref, step)
        out_ref[...] = (heads_from_lanes(sum_ref[...]) * scale).T.astype(bf16)

    inputs = [table, message, log_total, delta, mine, theirs, grad]
    return run_kernel(
        kernel,
        inputs,
        [whole(pltpu.SMEM)] + [plain(item) for item in inputs[1:]],
        [((rows, local), bf16)],
        flops=12 * rows * count * rows * local,
        scratch=[
            pltpu.VMEM((2 * rows, local), bf16),
            pltpu.VMEM((2 * rows, local), bf16),
            pltpu.VMEM((local, 2 * rows), f32),
        ],
    )[0]


def key_side(queries, mine, theirs, key_value, query_grad, qkv, layer, table, unit):
    rows, local = key_value.shape[0], key_value.shape[1] // 2
    half = mine.shape[0]
    count = 2 * half
    width = qkv.shape[2]
    mp_count = lax.axis_size("mp")
    with_unit = unit is not None

    def kernel(table_ref, queries_ref, mine_ref, theirs_ref, own_ref, grad_ref, weight_ref, *refs):
        if with_unit:
            unit_ref, refs = refs[0], refs[1:]
        part_ref, proj_ref, bias_ref, small_ref = refs[:4]
        keys_ref, values_ref, key_sum_ref, value_sum_ref = refs[4:]
        keys_ref[...] = head_stack(own_ref[:, :local])
        values_ref[...] = head_stack(own_ref[:, local:])
        key_sum_ref[...] = jnp.zeros(key_sum_ref.shape, f32)
        value_sum_ref[...] = jnp.zeros(value_sum_ref.shape, f32)
        position = table_ref[16] + lax.broadcasted_iota(jnp.int32, (rows, 128), 0)
        own_label = label_of(position, table_ref)
        own_label = jnp.concatenate([own_label] * (rows // 128), axis=1)
        own_label = jnp.concatenate([own_label] * 2, axis=0)
        core = table_ref[20]

        def spread(row):
            return jnp.concatenate(
                [
                    jnp.broadcast_to(row[:, :rows], (rows, rows)),
                    jnp.broadcast_to(row[:, rows:], (rows, rows)),
                ],
                axis=0,
            )

        def one(block_ref, place_block, source, start, masked):
            query = queries_ref[source, :rows, :]
            grad = block_ref[place_block, :rows, :]
            log_total = rows_back(queries_ref[source, rows:, :], 3, 2 * rows)
            delta = rows_back(block_ref[place_block, rows:, :], 3, 2 * rows)
            scores = dot_nt(keys_ref[...], query) - spread(log_total)
            if masked:
                lanes = start + lax.broadcasted_iota(jnp.int32, (1, rows), 1)
                label = label_of(lanes, table_ref)
                scores = jnp.where(own_label == label, scores, far)
            probs = jnp.exp(scores)
            grad_probs = dot_nt(values_ref[...], grad)
            grad_scores = (probs * (grad_probs - spread(delta))).astype(bf16)
            value_sum_ref[...] += dot_nn(probs.astype(bf16), grad)
            key_sum_ref[...] += dot_nn(grad_scores, query)

        def step(index, masked):
            start = table_ref[index]

            @pl.when(index < half)
            def _():
                one(mine_ref, index, 2 * index + core, start, masked)

            @pl.when(index >= half)
            def _():
                one(theirs_ref, index - half, 2 * (index - half) + 1 - core, start, masked)

        over_blocks(count, rows, table_ref, step)
        key_grad = heads_from_rows(key_sum_ref[...]).astype(bf16)
        value_grad = heads_from_rows(value_sum_ref[...]).astype(bf16)
        query_grad = grad_ref[...]
        proj_ref[:, :local] = query_grad
        proj_ref[:, local : 2 * local] = key_grad
        proj_ref[:, 2 * local :] = value_grad
        bias_ref[...] = jnp.zeros(bias_ref.shape, f32)
        bias_ref[0:1, :] = jnp.sum(query_grad.astype(f32), axis=0, keepdims=True)
        bias_ref[1:2, :] = jnp.sum(value_grad.astype(f32), axis=0, keepdims=True)
        part = dot_nt(query_grad, weight_ref[0, 0])
        part += dot_nt(key_grad, weight_ref[0, 1])
        part += dot_nt(value_grad, weight_ref[0, 2])
        low = part.astype(bf16)
        part_ref[...] = low.reshape(part_ref.shape)
        small_ref[...] = jnp.zeros(small_ref.shape, f32)
        if with_unit:
            into = low.astype(f32)
            small_ref[0:1, :] = jnp.sum(into * unit_ref[...], axis=0, keepdims=True)
            small_ref[1:2, :] = jnp.sum(into, axis=0, keepdims=True)

    inputs = [table, queries, mine, theirs, key_value, query_grad, qkv]
    in_specs = [whole(pltpu.SMEM)] + [plain(item) for item in inputs[1:6]] + [of_layer(qkv, layer)]
    if with_unit:
        inputs.append(unit)
        in_specs.append(plain(unit))
    return run_kernel(
        kernel,
        inputs,
        in_specs,
        [
            ((mp_count, rows // mp_count, width), bf16),
            ((rows, 3 * local), bf16),
            ((8, local), f32),
            ((8, width), f32),
        ],
        flops=16 * rows * count * rows * local,
        scratch=[
            pltpu.VMEM((2 * rows, local), bf16),
            pltpu.VMEM((2 * rows, local), bf16),
            pltpu.VMEM((2 * rows, local), f32),
            pltpu.VMEM((2 * rows, local), f32),
        ],
    )


def first_norm(hidden, gain, shift):
    rows, width = hidden.shape

    def kernel(hidden_ref, gain_ref, shift_ref, normed_ref, unit_ref):
        centered, inverse = row_stats(hidden_ref[...])
        unit = centered * inverse
        unit_ref[...] = unit
        normed_ref[...] = (unit * gain_ref[0:1, :] + shift_ref[0:1, :]).astype(bf16)

    inputs = [hidden, gain, shift]
    return run_kernel(
        kernel,
        inputs,
        [plain(item) for item in inputs],
        [((rows, width), bf16), ((rows, width), f32)],
    )


def project(normed, qkv, bias, layer):
    rows = normed.shape[0]
    width, local = qkv.shape[2:]

    def kernel(normed_ref, weight_ref, bias_ref, query_ref, pair_ref):
        own = normed_ref[...]
        query = dot_nn(own, weight_ref[0, 0]) + bias_ref[0, 0:1, :]
        query_ref[...] = query.astype(bf16)
        pair_ref[:, :local] = dot_nn(own, weight_ref[0, 1]).astype(bf16)
        values = dot_nn(own, weight_ref[0, 2]) + bias_ref[0, 1:2, :]
        pair_ref[:, local:] = values.astype(bf16)

    inputs = [normed, qkv, bias]
    return run_kernel(
        kernel,
        inputs,
        [plain(normed), of_layer(qkv, layer), of_layer(bias, layer)],
        [((rows, local), bf16), ((rows, 2 * local), bf16)],
        flops=6 * rows * width * local,
    )


def mlp_forward(normed, inner, inner_bias, down, layer):
    parts, part_rows, width = normed.shape
    rows, units = parts * part_rows, inner.shape[2]

    def kernel(normed_ref, inner_ref, bias_ref, down_ref, before_ref, active_ref, part_ref):
        own = normed_ref[...].reshape(rows, width)
        before = dot_nn(own, inner_ref[0]) + bias_ref[layer : layer + 1, :]
        before_ref[...] = before
        active = 0.5 * before * (1.0 + lax.erf(before * math.sqrt(0.5)))
        active = active.astype(bf16)
        active_ref[...] = active
        part_ref[...] = dot_nn(active, down_ref[0]).astype(bf16).reshape(part_ref.shape)

    inputs = [normed, inner, inner_bias, down]
    return run_kernel(
        kernel,
        inputs,
        [plain(normed), of_layer(inner, layer), plain(inner_bias), of_layer(down, layer)],
        [((rows, units), f32), ((rows, units), bf16), ((parts, part_rows, width), bf16)],
        flops=4 * rows * width * units,
    )


def mlp_backward(grad, before, inner, down, layer):
    parts, part_rows, width = grad.shape
    rows, units = parts * part_rows, inner.shape[2]

    def kernel(grad_ref, before_ref, inner_ref, down_ref, out_ref, bias_ref, part_ref):
        into = dot_nt(grad_ref[...].reshape(rows, width), down_ref[0])
        before = before_ref[...]
        slope = 0.5 * (1.0 + lax.erf(before * math.sqrt(0.5)))
        slope += before * jnp.exp(-0.5 * before * before) * (1.0 / math.sqrt(2.0 * math.pi))
        out = (into * slope).astype(bf16)
        out_ref[...] = out
        bias_ref[...] = jnp.broadcast_to(
            jnp.sum(out.astype(f32), axis=0, keepdims=True), bias_ref.shape
        )
        part_ref[...] = dot_nt(out, inner_ref[0]).astype(bf16).reshape(part_ref.shape)

    inputs = [grad, before, inner, down]
    return run_kernel(
        kernel,
        inputs,
        [plain(grad), plain(before), of_layer(inner, layer), of_layer(down, layer)],
        [((rows, units), bf16), ((8, units), f32), ((parts, part_rows, width), bf16)],
        flops=4 * rows * width * units,
    )


def token_products(pairs):
    columns = [right.shape[-1] for left, right in pairs]
    width = pairs[0][0].shape[-1]
    rows = pairs[0][1].shape[0]

    def kernel(*refs):
        out_ref = refs[-1]
        at = 0
        for index, size in enumerate(columns):
            left = refs[2 * index][...].reshape(rows, width)
            out_ref[:, at : at + size] = dot_tn(left, refs[2 * index + 1][...]).astype(bf16)
            at += size

    inputs = [item for pair in pairs for item in pair]
    return run_kernel(
        kernel,
        inputs,
        [plain(item) for item in inputs],
        [((width, sum(columns)), bf16)],
        flops=2 * rows * width * sum(columns),
    )[0]


def pack_small(norm_one, norm_two, key_small, own_cotangent, proj_bias, inner_bias, dp_count):
    width = own_cotangent.shape[1]
    columns = width // dp_count

    def kernel(one_ref, two_a_ref, two_b_ref, key_ref, grad_ref, *refs):
        proj_refs, inner_refs = refs[:2], refs[2:4]
        out_ref, first_ref, second_ref = refs[4:]
        last = jnp.sum(grad_ref[...].astype(bf16).astype(f32), axis=0, keepdims=True)
        zero = jnp.zeros((2, width), f32)
        for target, two_ref, gains, bias in (
            (first_ref, two_a_ref, key_ref, one_ref[2:3, :]),
            (second_ref, two_b_ref, one_ref, last),
        ):
            target[0:2, :] = gains[0:2, :]
            target[2:3, :] = two_ref[2:3, :]
            target[3:5, :] = two_ref[0:2, :]
            target[5:6, :] = bias
            target[6:8, :] = zero
        for device in range(dp_count):
            at = slice(device * columns, (device + 1) * columns)
            out_ref[device, 0:8, :] = jnp.concatenate(
                [first_ref[:, at], second_ref[:, at]], axis=1
            )
            for layer in range(2):
                out_ref[device, 8 + 2 * layer : 10 + 2 * layer, :] = proj_refs[layer][0:2, :]
                for line in range(4):
                    row = 12 + 4 * layer + line
                    out_ref[device, row : row + 1, :] = inner_refs[layer][
                        0:1, 128 * line : 128 * line + 128
                    ]
            out_ref[device, 20:24, :] = jnp.zeros((4, 128), f32)

    inputs = [norm_one, norm_two[0], norm_two[1], key_small, own_cotangent] + proj_bias + inner_bias
    return run_kernel(
        kernel,
        inputs,
        [plain(item) for item in inputs],
        [((dp_count, 24, 128), f32)],
        scratch=[pltpu.VMEM((8, width), f32), pltpu.VMEM((8, width), f32)],
    )[0]


def finish_rows(got, rows):
    parts, own_rows, width = got.shape[0], rows, got.shape[2]

    def kernel(got_ref, out_ref, *small_refs):
        total = jnp.zeros((8, 128), f32)
        for part in range(parts):
            out_ref[part * own_rows : (part + 1) * own_rows, :] = got_ref[part, :own_rows, :].astype(
                f32
            )
            both = got_ref[part, own_rows:, :128].astype(f32)
            total += both[:8] + both[8:]
        for index, small_ref in enumerate(small_refs):
            small_ref[0:1, :] = total[index : index + 1, :64]
            small_ref[1:2, :] = total[index : index + 1, 64:]

    return run_kernel(
        kernel,
        [got],
        [plain(got)],
        [((parts * own_rows, width), f32)] + [((2, 64), f32)] * 6,
    )


def finish_weights(first, second, third, local, units):
    columns = first.shape[0]

    def kernel(first_ref, second_ref, third_ref, qkv_ref, out_ref, inner_ref, down_ref):
        last = add_parts(third_ref)
        inner_ref[1] = first_ref[:, :units].astype(f32)
        down_ref[1] = first_ref[:, units:].astype(f32)
        middle = second_ref[...].astype(f32)
        for piece in range(3):
            qkv_ref[0, piece] = last[:, local * (piece + 1) : local * (piece + 2)]
            qkv_ref[1, piece] = middle[:, local * (piece + 1) : local * (piece + 2)]
        out_ref[0] = last[:, :local]
        out_ref[1] = middle[:, :local]
        inner_ref[0] = middle[:, 4 * local : 4 * local + units]
        down_ref[0] = middle[:, 4 * local + units :]

    inputs = [first, second, third]
    return run_kernel(
        kernel,
        inputs,
        [plain(item) for item in inputs],
        [
            ((2, 3, columns, local), f32),
            ((2, columns, local), f32),
            ((2, columns, units), f32),
            ((2, columns, units), f32),
        ],
    )


def scatter_dp(partial):
    count = lax.axis_size("dp")
    rows = partial.shape[0] // count
    core = lax.axis_index("dp") % 2
    split = partial.reshape(count // 2, 2, rows, partial.shape[1])
    away = lax.dynamic_index_in_dim(split, 1 - core, axis=1, keepdims=False)
    mine = lax.dynamic_index_in_dim(split, core, axis=1, keepdims=False)
    other = lax.ppermute(away, "dp", other_core(count))
    both = (mine.astype(f32) + other.astype(f32)).astype(bf16)
    return lax.all_to_all(both, "dp", 0, 0, tiled=True, axis_index_groups=chip_groups(count))


def body(
    hidden_in,
    cotangent,
    scene_lengths,
    block_owner,
    attn_gain,
    attn_shift,
    qkv_weight,
    qv_bias,
    out_weight,
    out_bias,
    mlp_gain,
    mlp_shift,
    mlp_in_weight,
    mlp_in_bias,
    mlp_out_weight,
    mlp_out_bias,
):
    rows, width = hidden_in.shape
    layers = attn_gain.shape[0]
    local = qv_bias.shape[2] * qv_bias.shape[3]
    units = mlp_in_bias.shape[1]
    dp_count, mp_count = lax.axis_size("dp"), lax.axis_size("mp")
    dp_index, mp_index = lax.axis_index("dp"), lax.axis_index("mp")
    own_rows = rows // mp_count
    core = dp_index % 2

    def own_part(array):
        return lax.dynamic_slice_in_dim(array, mp_index * own_rows, own_rows)

    pairs = jnp.arange(dp_count // 2, dtype=jnp.int32) * 2
    order = jnp.concatenate([pairs + core, pairs + 1 - core, dp_index[None]])
    table = jnp.concatenate(
        [block_owner[order] * rows, jnp.cumsum(scene_lengths), core[None]]
    ).astype(jnp.int32)

    qkv = qkv_weight.transpose(0, 2, 1, 3)
    proj_bias = qv_bias.reshape(layers, 2, local)

    kept = []
    hidden = own_part(hidden_in)
    normed, unit = first_norm(hidden_in, attn_gain, attn_shift)
    for layer in range(layers):
        query, pair = project(normed, qkv, proj_bias, layer)
        mine, theirs = gather_dp(pair)
        part, attended_low, flat, log_total, message = attention_forward(
            query, mine, theirs, out_weight, layer, table
        )
        queries = lax.all_gather(message, "dp", axis=0, tiled=True)
        queries = queries.reshape((dp_count,) + message.shape)
        middle, spread = residual_norm(
            exchange_mp(part), hidden, out_bias, layer, mlp_gain, mlp_shift, layer
        )
        normed_mlp = exchange_mp(spread)
        before, active, part = mlp_forward(
            normed_mlp, mlp_in_weight, mlp_in_bias, mlp_out_weight, layer
        )
        kept.append(
            dict(
                hidden=hidden,
                normed=normed,
                pair=pair,
                mine=mine,
                theirs=theirs,
                attended_low=attended_low,
                flat=flat,
                log_total=log_total,
                message=message,
                queries=queries,
                middle=middle,
                normed_mlp=normed_mlp,
                before=before,
                active=active,
            )
        )
        more = layer + 1 if layer + 1 < layers else None
        after = residual_norm(
            exchange_mp(part), middle, mlp_out_bias, layer, attn_gain, attn_shift, more
        )
        hidden = after[0]
        if more is not None:
            normed = exchange_mp(after[1]).reshape(rows, width)
    output = lax.all_gather(hidden, "mp", axis=0, tiled=True)

    grad_own = own_part(cotangent)
    grad_full = cotangent.astype(bf16).reshape(mp_count, own_rows, width)
    norm_one, norm_two, bias_proj, bias_inner = {}, {}, {}, {}
    products = {}
    for layer in reversed(range(layers)):
        now = kept[layer]
        grad_before, bias_inner[layer], part = mlp_backward(
            grad_full, now["before"], mlp_in_weight, mlp_out_weight, layer
        )
        mlp_pairs = [(now["normed_mlp"], grad_before), (grad_full, now["active"])]
        middle_grad, spread, norm_two[layer] = norm_backward(
            exchange_mp(part), now["middle"], mlp_gain, layer, grad_own
        )
        branch = exchange_mp(spread)
        grad_message, delta = grad_attended(branch, out_weight, layer, now["flat"])
        grad_mine, grad_theirs = gather_dp(grad_message)
        query_grad = query_side(
            now["message"], now["log_total"], delta, now["mine"], now["theirs"], grad_message, table
        )
        part, proj_grad, bias_proj[layer], key_small = key_side(
            now["queries"],
            grad_mine,
            grad_theirs,
            now["pair"],
            query_grad,
            qkv,
            layer,
            table,
            unit if layer == 0 else None,
        )
        proj_pairs = [(branch, now["attended_low"]), (now["normed"], proj_grad)]
        if layer:
            products["first"] = token_products(mlp_pairs)
            grad_own, spread, norm_one[layer] = norm_backward(
                exchange_mp(part), now["hidden"], attn_gain, layer, middle_grad
            )
            grad_full = exchange_mp(spread)
            held = proj_pairs
        else:
            products["second"] = token_products(held + mlp_pairs)
            products["third"] = token_products(proj_pairs)
            small = pack_small(
                norm_one[1],
                norm_two,
                key_small,
                own_part(cotangent),
                [bias_proj[0], bias_proj[1]],
                [bias_inner[0], bias_inner[1]],
                dp_count,
            )
            small = jnp.sum(lax.all_to_all(small, "dp", 0, 0, tiled=True), axis=0)
            ignored, spread, ignored = norm_backward(
                exchange_mp(part), now["hidden"], attn_gain, layer, middle_grad, small[:8]
            )
            tail = exchange_mp(spread)

    first, second = (
        lax.psum_scatter(products[name], "dp", scatter_dimension=0, tiled=True)
        for name in ("first", "second")
    )
    third = scatter_dp(products["third"])
    qkv_grad, out_grad, inner_grad, down_grad = finish_weights(first, second, third, local, units)
    input_grad, gain_one, shift_one, out_bias_grad, gain_two, shift_two, down_bias_grad = (
        finish_rows(tail, own_rows)
    )
    bias_columns = qv_bias.shape[3] // dp_count
    qv_grad = lax.dynamic_slice_in_dim(
        small[8:12].reshape(qv_bias.shape), dp_index * bias_columns, bias_columns, axis=3
    )
    inner_columns = 64 // dp_count
    inner_bias_grad = lax.dynamic_slice_in_dim(
        small[12:20].reshape(layers, units // 64, 64),
        dp_index * inner_columns,
        inner_columns,
        axis=2,
    )
    return (
        output,
        input_grad,
        gain_one,
        shift_one,
        qkv_grad.transpose(0, 2, 1, 3),
        qv_grad,
        out_grad.transpose(0, 2, 1),
        out_bias_grad,
        gain_two,
        shift_two,
        inner_grad,
        inner_bias_grad,
        down_grad.transpose(0, 2, 1),
        down_bias_grad,
    )


def solution(mesh):
    in_specs = (
        P("dp", None),
        P("dp", None),
        P(),
        P(),
        P(),
        P(),
        P(None, None, None, "mp"),
        P(None, None, "mp", None),
        P(None, "mp", None),
        P(),
        P(),
        P(),
        P(None, None, "mp"),
        P(None, "mp"),
        P(None, "mp", None),
        P(),
    )
    out_specs = (
        P("dp", None),
        P("dp", None),
        P(None, "dp"),
        P(None, "dp"),
        P(None, "dp", None, "mp"),
        P(None, None, "mp", "dp"),
        P(None, "mp", "dp"),
        P(None, "dp"),
        P(None, "dp"),
        P(None, "dp"),
        P(None, "dp", "mp"),
        P(None, "mp", "dp"),
        P(None, "mp", "dp"),
        P(None, "dp"),
    )
    return jax.shard_map(body, mesh=mesh, in_specs=in_specs, out_specs=out_specs, check_vma=False)
```

```python
import functools
import math

import jax
import jax.numpy as jnp
from jax import lax
from jax.experimental import pallas as pl
from jax.experimental.pallas import tpu as pltpu
from jax.sharding import PartitionSpec as P

norm_eps = 1e-05
f32 = jnp.float32
bf16 = jnp.bfloat16
absent = -1e30


def chip_groups(count):
    return [list(range(core, count, 2)) for core in range(2)]


def other_core(count):
    return [(index, index ^ 1) for index in range(count)]


def exchange_mp(spread):
    return lax.all_to_all(spread, "mp", 0, 0, tiled=True)


def gather_chips(spread):
    groups = chip_groups(lax.axis_size("dp"))
    return lax.all_to_all(spread, "dp", 0, 0, tiled=True, axis_index_groups=groups)


def from_other_core(blocks):
    return lax.ppermute(blocks, "dp", other_core(lax.axis_size("dp")))


def after(value, *others):
    return lax.optimization_barrier((value,) + others)[0]


def whole(memory=pltpu.VMEM):
    return pl.BlockSpec(memory_space=memory)


def of_layer(stacked, layer):
    tail = stacked.shape[1:]
    return pl.BlockSpec((1,) + tail, lambda step: (layer,) + (0,) * len(tail))


def plain(array):
    return pl.BlockSpec(array.shape, lambda step: (0,) * len(array.shape))


def far(array):
    return pltpu.with_memory_space_constraint(array, pltpu.HBM)


def run_kernel(kernel, inputs, in_specs, outputs, flops=0, scratch=(), limit=12):
    moved = sum(math.prod(out[0]) * jnp.dtype(out[1]).itemsize for out in outputs)
    moved += sum(item.size * item.dtype.itemsize for item in inputs)
    return pl.pallas_call(
        kernel,
        grid=(1,),
        in_specs=in_specs,
        out_specs=[
            whole(pltpu.HBM)
            if len(out) == 4
            else pl.BlockSpec(out[0], functools.partial(lambda rank, step: (0,) * rank, len(out[0])))
            for out in outputs
        ],
        out_shape=[
            out[2](out[0], out[1]) if len(out) > 2 else jax.ShapeDtypeStruct(out[0], out[1])
            for out in outputs
        ],
        scratch_shapes=list(scratch),
        compiler_params=pltpu.CompilerParams(vmem_limit_bytes=limit * 2**20),
        cost_estimate=pl.CostEstimate(flops=flops, bytes_accessed=moved, transcendentals=0),
    )(*inputs)


def keep_in_hbm(pairs, sems):
    copies = [
        pltpu.make_async_copy(source, kept, sems.at[index])
        for index, (source, kept) in enumerate(pairs)
    ]
    for copy in copies:
        copy.start()
    return copies


def dot_nn(left, right):
    return lax.dot_general(left, right, (((1,), (0,)), ((), ())), preferred_element_type=f32)


def dot_nt(left, right):
    return lax.dot_general(left, right, (((1,), (1,)), ((), ())), preferred_element_type=f32)


def dot_tn(left, right):
    return lax.dot_general(left, right, (((0,), (0,)), ((), ())), preferred_element_type=f32)


def row_stats(inputs):
    average = jnp.mean(inputs, axis=-1, keepdims=True)
    centered = inputs - average
    variance = jnp.mean(centered * centered, axis=-1, keepdims=True)
    return centered, lax.rsqrt(variance + norm_eps)


def add_parts(got_ref):
    total = got_ref[0].astype(f32)
    for part in range(1, got_ref.shape[0]):
        total += got_ref[part].astype(f32)
    return total


def residual_norm(got, residual, bias, bias_layer, gain, shift, norm_layer):
    parts, rows, width = got.shape

    def kernel(got_ref, residual_ref, bias_ref, gain_ref, shift_ref, out_ref, spread_ref):
        total = residual_ref[...] + add_parts(got_ref) + bias_ref[bias_layer : bias_layer + 1, :]
        out_ref[...] = total
        layer = slice(norm_layer, norm_layer + 1)
        centered, inverse = row_stats(total)
        normed = (centered * inverse * gain_ref[layer, :] + shift_ref[layer, :]).astype(bf16)
        for part in range(parts):
            spread_ref[part] = normed

    inputs = [got, residual, bias, gain, shift]
    outputs = [((rows, width), f32, pltpu.HBM), ((parts, rows, width), bf16)]
    return run_kernel(kernel, inputs, [plain(item) for item in inputs], outputs)


def norm_backward(got, inputs, gain, layer, grad, extra=None, bias=None):
    parts, rows, width = got.shape
    if bias is not None:
        rows //= 2
    more = 0 if extra is None else 128

    def kernel(got_ref, inputs_ref, gain_ref, grad_ref, *refs):
        if bias is None:
            out_ref, spread_ref, small_ref = refs[-3:]
        else:
            bias_ref, out_ref, spread_ref, small_ref, output_ref = refs
        total = add_parts(got_ref)
        into = total[:rows]
        if bias is not None:
            output_ref[...] = inputs_ref[...] + total[rows:] + bias_ref[layer : layer + 1, :]
        centered, inverse = row_stats(inputs_ref[...])
        unit = centered * inverse
        scaled = into * gain_ref[layer : layer + 1, :]
        first = jnp.mean(scaled, axis=-1, keepdims=True)
        second = jnp.mean(scaled * unit, axis=-1, keepdims=True)
        total = grad_ref[...] + (scaled - first - unit * second) * inverse
        out_ref[...] = total
        rounded = total.astype(bf16)
        for part in range(parts):
            spread_ref[part, :, :width] = rounded
        if more:
            small = jnp.zeros((8, 128), f32)
            for chip in range(extra.shape[0]):
                piece = refs[0][chip, -16:, :128].astype(f32)
                small += piece[:8] + piece[8:]
            high = small.astype(bf16).astype(f32)
            zero = jnp.zeros((rows - 16, 128), f32)
            both = jnp.concatenate([high, small - high, zero], axis=0).astype(bf16)
            for part in range(parts):
                spread_ref[part, :, width:] = both
        small_ref[0:1, :] = jnp.sum(into * unit, axis=0, keepdims=True)
        small_ref[1:2, :] = jnp.sum(into, axis=0, keepdims=True)
        small_ref[2:3, :] = jnp.sum(rounded.astype(f32), axis=0, keepdims=True)
        small_ref[3:, :] = jnp.zeros((5, width), f32)

    inputs = [got, inputs, gain, grad] + [item for item in (extra, bias) if item is not None]
    outputs = [
        ((rows, width), f32, pltpu.HBM),
        ((parts, rows, width + more), bf16),
        ((8, width), f32, pltpu.HBM),
    ]
    if bias is not None:
        outputs.append(((rows, width), f32, pltpu.HBM))
    return run_kernel(kernel, inputs, [plain(item) for item in inputs], outputs)


class Places:
    def __init__(self, owner_ref, lengths_ref, rows):
        self.owner_ref, self.rows = owner_ref, rows
        self.device = lax.axis_index("dp")
        self.core = lax.rem(self.device, 2)
        self.own = owner_ref[self.device] * rows
        self.ends = []
        for scene in range(lengths_ref.shape[0]):
            before = self.ends[-1] if self.ends else 0
            self.ends.append(before + lengths_ref[scene])

    def device_of(self, index, same_core):
        return 2 * index + (self.core if same_core else 1 - self.core)

    def start(self, index, same_core):
        return self.owner_ref[self.device_of(index, same_core)] * self.rows

    def label(self, position):
        return sum((position >= end).astype(jnp.int32) for end in self.ends)

    def scalar_label(self, position):
        return sum(jnp.where(position >= end, 1, 0).astype(jnp.int32) for end in self.ends)

    def over_blocks(self, count, step):
        last = self.rows - 1
        own_first, own_last = self.scalar_label(self.own), self.scalar_label(self.own + last)
        own_alone = own_first == own_last

        for same_core in (True, False):

            def one(index, carry, same_core=same_core):
                start = self.start(index, same_core)
                first, end = self.scalar_label(start), self.scalar_label(start + last)
                meets = jnp.logical_and(first <= own_last, own_first <= end)
                alone = jnp.logical_and(first == end, own_alone)

                @pl.when(jnp.logical_and(meets, alone))
                def _():
                    step(index, same_core, start, False)

                @pl.when(jnp.logical_and(meets, jnp.logical_not(alone)))
                def _():
                    step(index, same_core, start, True)

                return carry

            lax.fori_loop(0, count, one, 0)


def scalars():
    return [whole(pltpu.SMEM), whole(pltpu.SMEM)]


def head_stack(rows):
    lane = lax.broadcasted_iota(jnp.int32, rows.shape, 1)
    half = rows.shape[1] // 2
    zero = jnp.zeros_like(rows)
    return jnp.concatenate(
        [jnp.where(lane < half, rows, zero), jnp.where(lane >= half, rows, zero)], axis=0
    )


def heads_from_lanes(stacked):
    half, rows = stacked.shape[0] // 2, stacked.shape[1] // 2
    return jnp.concatenate([stacked[:half, :rows], stacked[half:, rows:]], axis=0)


def heads_from_rows(stacked):
    rows = stacked.shape[0] // 2
    lane = lax.broadcasted_iota(jnp.int32, (rows, stacked.shape[1]), 1)
    return jnp.where(lane < stacked.shape[1] // 2, stacked[:rows], stacked[rows:])


def row_pieces(vector, count):
    pieces = []
    rest = vector
    for piece in range(count):
        term = rest.astype(bf16).astype(f32)
        rest = rest - term
        pieces += [term[:, start : start + 128] for start in range(0, vector.shape[1], 128)]
    row = lax.broadcasted_iota(jnp.int32, (16, 128), 0)
    tile = jnp.zeros((16, 128), f32)
    for index, piece in enumerate(pieces):
        tile = jnp.where(row == index, jnp.broadcast_to(piece, (16, 128)), tile)
    return tile.astype(bf16)


def rows_back(tile, count, length):
    tile = tile.astype(f32)
    lines = length // 128
    out = []
    for line in range(lines):
        total = tile[line : line + 1]
        for piece in range(1, count):
            total = total + tile[piece * lines + line : piece * lines + line + 1]
        out.append(total)
    return jnp.concatenate(out, axis=1)


def attention_forward(query, mine, theirs, out_weight, layer, owner, lengths):
    rows, local = query.shape
    count = mine.shape[0] + theirs.shape[0]
    half = mine.shape[0]
    width = out_weight.shape[2]
    scale = 1.0 / math.sqrt(local // 2)

    def kernel(
        owner_ref,
        lengths_ref,
        query_ref,
        mine_ref,
        theirs_ref,
        weight_ref,
        part_ref,
        low_ref,
        flat_ref,
        log_ref,
        message_ref,
        kept_mine_ref,
        kept_theirs_ref,
        stack_ref,
        peak_ref,
        total_ref,
        sum_ref,
        sems,
    ):
        copies = keep_in_hbm([(mine_ref, kept_mine_ref), (theirs_ref, kept_theirs_ref)], sems)
        places = Places(owner_ref, lengths_ref, rows)
        scaled = (query_ref[...].astype(f32) * scale).astype(bf16)
        stack_ref[...] = head_stack(scaled)
        peak_ref[...] = jnp.full(peak_ref.shape, absent, f32)
        total_ref[...] = jnp.zeros(total_ref.shape, f32)
        sum_ref[...] = jnp.zeros(sum_ref.shape, f32)
        lanes = lax.broadcasted_iota(jnp.int32, (1, 2 * rows), 1)
        own_label = places.label(places.own + jnp.where(lanes >= rows, lanes - rows, lanes))

        def step(index, same_core, start, masked):
            block_ref = mine_ref if same_core else theirs_ref
            keys = block_ref[index, :, :local]
            values = block_ref[index, :, local:]
            scores = dot_nt(keys, stack_ref[...])
            if masked:
                label = places.label(start + lax.broadcasted_iota(jnp.int32, (rows, 128), 0))
                label = jnp.concatenate([label] * (2 * rows // 128), axis=1)
                same = label == own_label
                scores = jnp.where(same, scores, absent)
            old = peak_ref[...]
            new = jnp.maximum(old, jnp.max(scores, axis=0, keepdims=True))
            weight = jnp.exp(scores - new)
            if masked:
                weight = jnp.where(same, weight, 0.0)
            fade = jnp.exp(old - new)
            peak_ref[...] = new
            total_ref[...] = total_ref[...] * fade + jnp.sum(weight, axis=0, keepdims=True)
            sum_ref[...] = sum_ref[...] * fade + dot_tn(values, weight.astype(bf16))

        places.over_blocks(half, step)
        attended = heads_from_lanes(sum_ref[...] / total_ref[...])
        flat_ref[...] = attended
        low = attended.T.astype(bf16)
        low_ref[...] = low
        part = dot_nn(low, weight_ref[0]).astype(bf16)
        part_ref[...] = part.reshape(part_ref.shape)
        log_total = peak_ref[...] + jnp.log(total_ref[...])
        log_ref[...] = log_total
        message_ref[:rows, :] = scaled
        message_ref[rows:, :] = row_pieces(log_total, 3)
        for copy in copies:
            copy.wait()

    inputs = [owner, lengths, query, mine, theirs, out_weight]
    mp_count = lax.axis_size("mp")
    return run_kernel(
        kernel,
        inputs,
        scalars()
        + [plain(query), plain(mine), plain(theirs), of_layer(out_weight, layer)],
        [
            ((mp_count, rows // mp_count, width), bf16),
            ((rows, local), bf16, pltpu.HBM),
            ((local, rows), f32, pltpu.HBM),
            ((1, 2 * rows), f32, pltpu.HBM),
            ((rows + 16, local), bf16, pltpu.HBM),
            (mine.shape, bf16, pltpu.HBM, True),
            (theirs.shape, bf16, pltpu.HBM, True),
        ],
        flops=8 * rows * count * rows * local,
        limit=16,
        scratch=[
            pltpu.VMEM((2 * rows, local), bf16),
            pltpu.VMEM((1, 2 * rows), f32),
            pltpu.VMEM((1, 2 * rows), f32),
            pltpu.VMEM((local, 2 * rows), f32),
            pltpu.SemaphoreType.DMA((2,)),
        ],
    )


def grad_attended(branch, out_weight, layer, flat):
    rows = branch.shape[0] * branch.shape[1]
    local = out_weight.shape[1]

    chips = lax.axis_size("dp") // 2

    def kernel(
        branch_ref, weight_ref, flat_ref, spread_ref, message_ref, delta_ref, kept_ref, sems
    ):
        copies = keep_in_hbm([(branch_ref, kept_ref)], sems)
        grad = dot_nt(branch_ref[...].reshape(rows, -1), weight_ref[0]).astype(bf16)
        product = grad.astype(f32).T * flat_ref[...]
        half = local // 2
        delta = jnp.concatenate(
            [
                jnp.sum(product[:half], axis=0, keepdims=True),
                jnp.sum(product[half:], axis=0, keepdims=True),
            ],
            axis=1,
        )
        delta_ref[...] = delta
        pieces = row_pieces(delta, 3)
        message_ref[...] = grad
        for chip in range(chips):
            spread_ref[chip, :rows, :] = grad
            spread_ref[chip, rows:, :] = pieces
        copies[0].wait()

    inputs = [branch, far(out_weight), far(flat)]
    return run_kernel(
        kernel,
        inputs,
        [plain(branch), of_layer(out_weight, layer), plain(flat)],
        [
            ((chips, rows + 16, local), bf16),
            ((rows, local), bf16),
            ((1, 2 * rows), f32),
            (branch.shape, bf16, pltpu.HBM, True),
        ],
        flops=2 * rows * local * branch.shape[2],
        scratch=[pltpu.SemaphoreType.DMA((1,))],
    )


def query_side(message, log_total, delta, mine, theirs, grad, owner, lengths):
    rows, local = grad.shape
    half = mine.shape[0]
    count = 2 * half
    scale = 1.0 / math.sqrt(local // 2)

    def kernel(
        owner_ref,
        lengths_ref,
        query_ref,
        log_ref,
        delta_ref,
        mine_ref,
        theirs_ref,
        grad_ref,
        out_ref,
        stack_ref,
        grad_stack_ref,
        sum_ref,
    ):
        places = Places(owner_ref, lengths_ref, rows)
        stack_ref[...] = head_stack(query_ref[:rows, :])
        grad_stack_ref[...] = head_stack(grad_ref[...])
        sum_ref[...] = jnp.zeros(sum_ref.shape, f32)
        lanes = lax.broadcasted_iota(jnp.int32, (1, 2 * rows), 1)
        own_label = places.label(places.own + jnp.where(lanes >= rows, lanes - rows, lanes))

        def step(index, same_core, start, masked):
            block_ref = mine_ref if same_core else theirs_ref
            keys = block_ref[index, :, :local]
            values = block_ref[index, :, local:]
            scores = dot_nt(keys, stack_ref[...]) - log_ref[...]
            if masked:
                label = places.label(start + lax.broadcasted_iota(jnp.int32, (rows, 128), 0))
                label = jnp.concatenate([label] * (2 * rows // 128), axis=1)
                scores = jnp.where(label == own_label, scores, absent)
            probs = jnp.exp(scores)
            grad_probs = dot_nt(values, grad_stack_ref[...])
            grad_scores = (probs * (grad_probs - delta_ref[...])).astype(bf16)
            sum_ref[...] += dot_tn(keys, grad_scores)

        places.over_blocks(half, step)
        out_ref[...] = (heads_from_lanes(sum_ref[...]) * scale).T.astype(bf16)

    inputs = [owner, lengths, far(message), far(log_total), delta, far(mine), far(theirs), grad]
    return run_kernel(
        kernel,
        inputs,
        scalars() + [plain(item) for item in inputs[2:]],
        [((rows, local), bf16)],
        flops=64 * rows * count * rows * local,
        limit=16,
        scratch=[
            pltpu.VMEM((2 * rows, local), bf16),
            pltpu.VMEM((2 * rows, local), bf16),
            pltpu.VMEM((local, 2 * rows), f32),
        ],
    )[0]


def key_side(
    queries, mine, theirs, key_value, query_grad, qkv, layer, owner, lengths, unit
):
    rows, local = key_value.shape[0], key_value.shape[1] // 2
    half = mine.shape[0]
    count = 2 * half
    width = qkv.shape[2]
    mp_count = lax.axis_size("mp")
    with_unit = unit is not None

    def kernel(
        owner_ref,
        lengths_ref,
        queries_ref,
        mine_ref,
        theirs_ref,
        own_ref,
        grad_ref,
        weight_ref,
        *refs,
    ):
        places = Places(owner_ref, lengths_ref, rows)
        if with_unit:
            unit_ref, refs = refs[0], refs[1:]
        part_ref, proj_ref, bias_ref, small_ref = refs[:4]
        keys_ref, values_ref, key_sum_ref, value_sum_ref = refs[4:]
        keys_ref[...] = head_stack(own_ref[:, :local])
        values_ref[...] = head_stack(own_ref[:, local:])
        key_sum_ref[...] = jnp.zeros(key_sum_ref.shape, f32)
        value_sum_ref[...] = jnp.zeros(value_sum_ref.shape, f32)
        own_label = places.label(places.own + lax.broadcasted_iota(jnp.int32, (rows, 128), 0))
        own_label = jnp.concatenate([own_label] * (rows // 128), axis=1)
        own_label = jnp.concatenate([own_label] * 2, axis=0)

        def spread(row):
            return jnp.concatenate(
                [
                    jnp.broadcast_to(row[:, :rows], (rows, rows)),
                    jnp.broadcast_to(row[:, rows:], (rows, rows)),
                ],
                axis=0,
            )

        def step(index, same_core, start, masked):
            block_ref = mine_ref if same_core else theirs_ref
            source = places.device_of(index, same_core)
            query = queries_ref[source, :rows, :]
            grad = block_ref[index, :rows, :]
            log_total = rows_back(queries_ref[source, rows:, :], 3, 2 * rows)
            delta = rows_back(block_ref[index, rows:, :], 3, 2 * rows)
            scores = dot_nt(keys_ref[...], query) - spread(log_total)
            if masked:
                lanes = start + lax.broadcasted_iota(jnp.int32, (1, rows), 1)
                label = places.label(lanes)
                scores = jnp.where(own_label == label, scores, absent)
            probs = jnp.exp(scores)
            grad_probs = dot_nt(values_ref[...], grad)
            grad_scores = (probs * (grad_probs - spread(delta))).astype(bf16)
            value_sum_ref[...] += dot_nn(probs.astype(bf16), grad)
            key_sum_ref[...] += dot_nn(grad_scores, query)

        places.over_blocks(half, step)
        key_grad = heads_from_rows(key_sum_ref[...]).astype(bf16)
        value_grad = heads_from_rows(value_sum_ref[...]).astype(bf16)
        query_grad = grad_ref[...]
        proj_ref[:, :local] = query_grad
        proj_ref[:, local : 2 * local] = key_grad
        proj_ref[:, 2 * local :] = value_grad
        bias_ref[...] = jnp.zeros(bias_ref.shape, f32)
        bias_ref[0:1, :] = jnp.sum(query_grad.astype(f32), axis=0, keepdims=True)
        bias_ref[1:2, :] = jnp.sum(value_grad.astype(f32), axis=0, keepdims=True)
        part = dot_nt(query_grad, weight_ref[0, 0])
        part += dot_nt(key_grad, weight_ref[0, 1])
        part += dot_nt(value_grad, weight_ref[0, 2])
        low = part.astype(bf16)
        part_ref[...] = low.reshape(part_ref.shape)
        small_ref[...] = jnp.zeros(small_ref.shape, f32)
        if with_unit:
            into = low.astype(f32)
            small_ref[0:1, :] = jnp.sum(into * unit_ref[...], axis=0, keepdims=True)
            small_ref[1:2, :] = jnp.sum(into, axis=0, keepdims=True)

    inputs = [owner, lengths, far(queries), mine, theirs, far(key_value), query_grad, far(qkv)]
    in_specs = scalars() + [plain(item) for item in inputs[2:7]] + [of_layer(qkv, layer)]
    if with_unit:
        inputs.append(far(unit))
        in_specs.append(plain(unit))
    return run_kernel(
        kernel,
        inputs,
        in_specs,
        [
            ((mp_count, rows // mp_count, width), bf16),
            ((rows, 3 * local), bf16, pltpu.HBM),
            ((8, local), f32, pltpu.HBM),
            ((8, width), f32, pltpu.HBM),
        ],
        flops=64 * rows * count * rows * local,
        limit=18,
        scratch=[
            pltpu.VMEM((2 * rows, local), bf16),
            pltpu.VMEM((2 * rows, local), bf16),
            pltpu.VMEM((2 * rows, local), f32),
            pltpu.VMEM((2 * rows, local), f32),
        ],
    )


def project(normed, qkv, bias, layer, first=None):
    rows, width = normed.shape
    local = qkv.shape[3]
    chips = lax.axis_size("dp") // 2
    own_rows = rows // lax.axis_size("mp")

    def kernel(normed_ref, weight_ref, bias_ref, *refs):
        if first is None:
            query_ref, pair_ref, spread_ref, kept_ref, sems = refs
            copies = keep_in_hbm([(normed_ref, kept_ref)], sems)
            normed = normed_ref[...]
        else:
            gain_ref, shift_ref, query_ref, pair_ref, spread_ref = refs[:5]
            own_ref, low_ref, unit_ref = refs[5:]
            centered, inverse = row_stats(normed_ref[...])
            unit = centered * inverse
            unit_ref[...] = unit
            normed = (unit * gain_ref[0:1, :] + shift_ref[0:1, :]).astype(bf16)
            low_ref[...] = normed
            own = pl.multiple_of(lax.axis_index("mp") * own_rows, own_rows)
            own_ref[...] = normed_ref[pl.ds(own, own_rows), :]
        query_bias, value_bias = (
            jnp.concatenate([bias_ref[0, at, 0:1, :], bias_ref[0, at, 1:2, :]], axis=1)
            for at in range(2)
        )
        query = dot_nn(normed, weight_ref[0, 0]) + query_bias
        query_ref[...] = query.astype(bf16)
        keys = dot_nn(normed, weight_ref[0, 1]).astype(bf16)
        values = (dot_nn(normed, weight_ref[0, 2]) + value_bias).astype(bf16)
        pair_ref[:, :local] = keys
        pair_ref[:, local:] = values
        for chip in range(chips):
            spread_ref[chip, :, :local] = keys
            spread_ref[chip, :, local:] = values
        if first is None:
            copies[0].wait()

    inputs = [normed, qkv, bias] if first is None else [far(normed), far(qkv), far(bias)]
    in_specs = [plain(normed), of_layer(qkv, layer), of_layer(bias, layer)]
    outputs = [
        ((rows, local), bf16),
        ((rows, 2 * local), bf16, pltpu.HBM),
        ((chips, rows, 2 * local), bf16),
    ]
    scratch = []
    if first is None:
        outputs.append((normed.shape, bf16, pltpu.HBM, True))
        scratch.append(pltpu.SemaphoreType.DMA((1,)))
    else:
        inputs += [far(item) for item in first]
        in_specs += [plain(item) for item in first]
        outputs += [
            ((own_rows, width), f32, pltpu.HBM),
            ((rows, width), bf16, pltpu.HBM),
            ((rows, width), f32, pltpu.HBM),
        ]
    return run_kernel(
        kernel, inputs, in_specs, outputs, flops=6 * rows * width * local, scratch=scratch
    )


def mlp_forward(normed, inner, inner_bias, down, layer):
    parts, part_rows, width = normed.shape
    rows, units = parts * part_rows, inner.shape[2]

    def kernel(
        normed_ref,
        inner_ref,
        bias_ref,
        down_ref,
        before_ref,
        active_ref,
        part_ref,
        kept_ref,
        sems,
    ):
        copies = keep_in_hbm([(normed_ref, kept_ref)], sems)
        own = normed_ref[...].reshape(rows, width)
        before = dot_nn(own, inner_ref[0]) + bias_ref[layer : layer + 1, :]
        before_ref[...] = before
        active = gelu(before).astype(bf16)
        active_ref[...] = active
        part_ref[...] = dot_nn(active, down_ref[0]).astype(bf16).reshape(part_ref.shape)
        copies[0].wait()

    inputs = [normed, inner, inner_bias, down]
    return run_kernel(
        kernel,
        inputs,
        [plain(normed), of_layer(inner, layer), plain(inner_bias), of_layer(down, layer)],
        [
            ((rows, units), f32, pltpu.HBM),
            ((rows, units), bf16, pltpu.HBM),
            ((parts, part_rows, width), bf16),
            (normed.shape, bf16, pltpu.HBM, True),
        ],
        flops=4 * rows * width * units,
        scratch=[pltpu.SemaphoreType.DMA((1,))],
    )


def gelu(before):
    return 0.5 * before * (1.0 + lax.erf(before * math.sqrt(0.5)))


def gelu_slope(before):
    slope = 0.5 * (1.0 + lax.erf(before * math.sqrt(0.5)))
    return slope + before * jnp.exp(-0.5 * before * before) * (1.0 / math.sqrt(2.0 * math.pi))


def mlp_last(normed, cotangent, inner, inner_bias, down):
    parts, part_rows, width = normed.shape
    layer = inner.shape[0] - 1
    rows, units = parts * part_rows, inner.shape[2]

    def kernel(
        normed_ref,
        cotangent_ref,
        inner_ref,
        inner_bias_ref,
        down_ref,
        active_ref,
        out_ref,
        bias_ref,
        part_ref,
        own_ref,
        full_ref,
        kept_ref,
        sems,
    ):
        copies = keep_in_hbm([(normed_ref, kept_ref)], sems)
        grad = cotangent_ref[...].astype(bf16)
        full_ref[...] = grad.reshape(full_ref.shape)
        own = pl.multiple_of(lax.axis_index("mp") * part_rows, part_rows)
        own_ref[...] = cotangent_ref[pl.ds(own, part_rows), :]
        before = dot_nn(normed_ref[...].reshape(rows, width), inner_ref[0])
        before += inner_bias_ref[layer : layer + 1, :]
        out = (dot_nt(grad, down_ref[0]) * gelu_slope(before)).astype(bf16)
        out_ref[...] = out
        bias_ref[...] = jnp.broadcast_to(
            jnp.sum(out.astype(f32), axis=0, keepdims=True), bias_ref.shape
        )
        part = dot_nt(out, inner_ref[0]).astype(bf16)
        part_ref[:, :part_rows, :] = part.reshape(parts, part_rows, width)
        active = gelu(before).astype(bf16)
        active_ref[...] = active
        part = dot_nn(active, down_ref[0]).astype(bf16)
        part_ref[:, part_rows:, :] = part.reshape(parts, part_rows, width)
        copies[0].wait()

    inputs = [normed, far(cotangent), inner, inner_bias, down]
    return run_kernel(
        kernel,
        inputs,
        [
            plain(normed),
            plain(cotangent),
            of_layer(inner, layer),
            plain(inner_bias),
            of_layer(down, layer),
        ],
        [
            ((rows, units), bf16, pltpu.HBM),
            ((rows, units), bf16, pltpu.HBM),
            ((8, units), f32, pltpu.HBM),
            ((parts, 2 * part_rows, width), bf16),
            ((part_rows, width), f32, pltpu.HBM),
            ((parts, part_rows, width), bf16, pltpu.HBM),
            (normed.shape, bf16, pltpu.HBM, True),
        ],
        flops=8 * rows * width * units,
        scratch=[pltpu.SemaphoreType.DMA((1,))],
    )


def mlp_backward(grad, before, inner, down, layer):
    parts, part_rows, width = grad.shape
    rows, units = parts * part_rows, inner.shape[2]

    def kernel(
        grad_ref, before_ref, inner_ref, down_ref, out_ref, bias_ref, part_ref, kept_ref, sems
    ):
        copies = keep_in_hbm([(grad_ref, kept_ref)], sems)
        into = dot_nt(grad_ref[...].reshape(rows, width), down_ref[0])
        out = (into * gelu_slope(before_ref[...])).astype(bf16)
        out_ref[...] = out
        bias_ref[...] = jnp.broadcast_to(
            jnp.sum(out.astype(f32), axis=0, keepdims=True), bias_ref.shape
        )
        part_ref[...] = dot_nt(out, inner_ref[0]).astype(bf16).reshape(part_ref.shape)
        copies[0].wait()

    inputs = [grad, before, inner, down]
    return run_kernel(
        kernel,
        inputs,
        [plain(grad), plain(before), of_layer(inner, layer), of_layer(down, layer)],
        [
            ((rows, units), bf16, pltpu.HBM),
            ((8, units), f32, pltpu.HBM),
            ((parts, part_rows, width), bf16),
            (grad.shape, bf16, pltpu.HBM, True),
        ],
        flops=4 * rows * width * units,
        scratch=[pltpu.SemaphoreType.DMA((1,))],
    )


def token_products(pairs):
    columns = [right.shape[-1] for left, right in pairs]
    width = pairs[0][0].shape[-1]
    rows = pairs[0][1].shape[0]

    def kernel(*refs):
        out_ref = refs[-1]
        at = 0
        for index, size in enumerate(columns):
            left = refs[2 * index][...].reshape(rows, width)
            out_ref[:, at : at + size] = dot_tn(left, refs[2 * index + 1][...]).astype(bf16)
            at += size

    inputs = [far(item) for pair in pairs for item in pair]
    return run_kernel(
        kernel,
        inputs,
        [plain(item) for item in inputs],
        [((width, sum(columns)), bf16, pltpu.HBM)],
        flops=2 * rows * width * sum(columns),
    )[0]


def last_products(pairs, norm_one, norm_two, key_small, own_cotangent, proj_bias, inner_bias):
    width = own_cotangent.shape[1]
    dp_count = lax.axis_size("dp")
    columns = width // dp_count
    token_rows = pairs[0][1].shape[0]
    total = sum(right.shape[-1] for left, right in pairs)
    items = [item for pair in pairs for item in pair]
    inputs = items + [norm_one, norm_two[0], norm_two[1], key_small, own_cotangent]
    inputs = [far(item) for item in inputs + proj_bias + inner_bias]

    def kernel(*refs):
        item_refs, refs = refs[: len(items)], refs[len(items) :]
        one_ref, two_a_ref, two_b_ref, key_ref, grad_ref = refs[:5]
        proj_refs, inner_refs = refs[5:7], refs[7:9]
        mine_ref, away_ref, first_ref, second_ref, product_ref = refs[9:]
        at = 0
        for left_ref, right_ref in zip(item_refs[0::2], item_refs[1::2]):
            left = left_ref[...].reshape(token_rows, width)
            size = right_ref.shape[-1]
            product_ref[:, at : at + size] = dot_tn(left, right_ref[...]).astype(bf16)
            at += size
        last = jnp.sum(grad_ref[...].astype(bf16).astype(f32), axis=0, keepdims=True)
        zero = jnp.zeros((2, width), f32)
        for target, two_ref, gains, bias in (
            (first_ref, two_a_ref, key_ref, one_ref[2:3, :]),
            (second_ref, two_b_ref, one_ref, last),
        ):
            target[0:2, :] = gains[0:2, :]
            target[2:3, :] = two_ref[2:3, :]
            target[3:5, :] = two_ref[0:2, :]
            target[5:6, :] = bias
            target[6:8, :] = zero
        lines = [proj_refs[layer][row : row + 1, :] for layer in range(2) for row in range(2)]
        for layer in range(2):
            lines += [inner_refs[layer][0:1, 128 * at : 128 * at + 128] for at in range(4)]
        row_index = lax.broadcasted_iota(jnp.int32, (8, 128), 0)
        shared = []
        for group in (lines[:8], lines[8:]):
            tile = jnp.zeros((8, 128), f32)
            for row, line in enumerate(group):
                tile = jnp.where(row_index == row, jnp.broadcast_to(line, (8, 128)), tile)
            shared.append(tile)
        core = lax.rem(lax.axis_index("dp"), 2)
        for device in range(dp_count):
            at = slice(device * columns, (device + 1) * columns)
            small = jnp.concatenate([first_ref[:, at], second_ref[:, at]] + shared, axis=1)
            high = small.astype(bf16).astype(f32)
            tail = jnp.concatenate([high, small - high], axis=0).astype(bf16)
            for flag, ref in ((core == device % 2, mine_ref), (core != device % 2, away_ref)):

                @pl.when(flag)
                def _(ref=ref, tail=tail, device=device, at=at):
                    ref[device // 2, :columns, :] = product_ref[at, :]
                    ref[device // 2, columns:, :] = tail

    shape = ((dp_count // 2, columns + 16, total), bf16)
    return run_kernel(
        kernel,
        inputs,
        [plain(item) for item in inputs],
        [shape, shape],
        flops=2 * token_rows * width * total,
        scratch=[
            pltpu.VMEM((8, width), f32),
            pltpu.VMEM((8, width), f32),
            pltpu.VMEM((width, total), bf16),
        ],
    )


def add_cores(mine, other, columns):
    def kernel(mine_ref, other_ref, out_ref):
        for chip in range(mine.shape[0]):
            both = mine_ref[chip].astype(f32) + other_ref[chip].astype(f32)
            out_ref[chip, :columns, :] = both[:columns].astype(bf16)
            small = both[columns : columns + 8] + both[columns + 8 :]
            high = small.astype(bf16).astype(f32)
            out_ref[chip, columns:, :] = jnp.concatenate([high, small - high], axis=0).astype(bf16)

    return run_kernel(kernel, [mine, other], [plain(mine), plain(other)], [(mine.shape, bf16)])[0]


def scatter_sum(pairs):
    return lax.psum_scatter(token_products(pairs), "dp", scatter_dimension=0, tiled=True)


def finish_rows(got, output, width):
    parts, own_rows = got.shape[:2]

    def kernel(got_ref, output_ref, out_ref, *refs):
        small_refs, kept_ref = refs[:6], refs[6]
        kept_ref[...] = output_ref[...]
        total = jnp.zeros((8, 128), f32)
        for part in range(parts):
            at = slice(part * own_rows, (part + 1) * own_rows)
            out_ref[at, :] = got_ref[part, :, :width].astype(f32)
            both = got_ref[part, :16, width:].astype(f32)
            total += both[:8] + both[8:]
        for index, small_ref in enumerate(small_refs):
            small_ref[0:1, :] = total[index : index + 1, :64]
            small_ref[1:2, :] = total[index : index + 1, 64:]

    return run_kernel(
        kernel,
        [got, far(output)],
        [plain(got), plain(output)],
        [((parts * own_rows, width), f32, pltpu.HBM)]
        + [((2, 64), f32, pltpu.HBM)] * 6
        + [(output.shape, f32, pltpu.HBM)],
    )


def finish_weights(first, second, third, local, units):
    columns = first.shape[0]
    bias_columns = columns // lax.axis_size("dp")

    def kernel(first_ref, second_ref, third_ref, qkv_ref, out_ref, inner_ref, down_ref, small_ref):
        last = add_parts(third_ref)
        small = last[columns : columns + 8] + last[columns + 8 :]
        small = jnp.concatenate([small[:, 128:256], small[:, 256:384]], axis=0)
        lane = lax.broadcasted_iota(jnp.int32, small.shape, 1)
        own = lax.axis_index("dp") * bias_columns
        picked = jnp.zeros(small.shape, f32)
        for half in range(2):
            for column in range(bias_columns):
                at = half * 64 + own + column
                value = jnp.sum(jnp.where(lane == at, small, 0.0), axis=1, keepdims=True)
                picked = jnp.where(lane == half * bias_columns + column, value, picked)
        small_ref[...] = picked
        middle, late = first_ref[...].astype(f32), second_ref[...].astype(f32)
        for layer, sums in ((1, middle), (0, late)):
            inner_ref[layer] = sums[:, :units]
            down_ref[layer] = sums[:, units : 2 * units]
            out_ref[layer] = sums[:, 2 * units : 2 * units + local]
        for piece in range(3):
            at = 2 * units + local * (piece + 1)
            qkv_ref[1, piece] = middle[:, at : at + local]
            qkv_ref[0, piece] = last[:columns, local * piece : local * (piece + 1)]

    inputs = [far(first), far(second), third]
    return run_kernel(
        kernel,
        inputs,
        [plain(item) for item in inputs],
        [
            ((2, 3, columns, local), f32, pltpu.HBM),
            ((2, columns, local), f32, pltpu.HBM),
            ((2, columns, units), f32, pltpu.HBM),
            ((2, columns, units), f32, pltpu.HBM),
            ((16, 128), f32),
        ],
    )


def body(
    hidden_in,
    cotangent,
    scene_lengths,
    block_owner,
    attn_gain,
    attn_shift,
    qkv_weight,
    qv_bias,
    out_weight,
    out_bias,
    mlp_gain,
    mlp_shift,
    mlp_in_weight,
    mlp_in_bias,
    mlp_out_weight,
    mlp_out_bias,
):
    rows, width = hidden_in.shape
    layers = attn_gain.shape[0]
    local = qv_bias.shape[2] * qv_bias.shape[3]
    units = mlp_in_bias.shape[1]
    dp_count, mp_count = lax.axis_size("dp"), lax.axis_size("mp")
    own_rows = rows // mp_count
    qkv = qkv_weight.transpose(0, 2, 1, 3)
    where = (block_owner, scene_lengths)

    kept = []
    for layer in range(layers):
        if layer:
            query, pair, spread, normed = project(normed, qkv, qv_bias, layer)
            spread = after(spread, queries)
        else:
            query, pair, spread, hidden, normed, unit = project(
                hidden_in, qkv, qv_bias, layer, (attn_gain, attn_shift)
            )
        mine = gather_chips(spread)
        theirs = from_other_core(mine)
        part, attended_low, flat, log_total, message, mine, theirs = attention_forward(
            query, mine, theirs, out_weight, layer, *where
        )
        got = exchange_mp(part)
        queries = lax.all_gather(after(message, got), "dp", axis=0, tiled=True)
        queries = queries.reshape((dp_count,) + message.shape)
        middle, spread = residual_norm(
            got, hidden, out_bias, layer, mlp_gain, mlp_shift, layer
        )
        normed_mlp = exchange_mp(spread)
        if layer + 1 < layers:
            before, active, part, normed_mlp = mlp_forward(
                normed_mlp, mlp_in_weight, mlp_in_bias, mlp_out_weight, layer
            )
        kept.append(
            dict(
                hidden=hidden,
                normed=normed,
                pair=pair,
                mine=mine,
                theirs=theirs,
                attended_low=attended_low,
                flat=flat,
                log_total=log_total,
                message=message,
                queries=queries,
                middle=middle,
                normed_mlp=normed_mlp,
                before=before,
                active=active,
            )
        )
        if layer + 1 < layers:
            hidden, spread = residual_norm(
                exchange_mp(part), middle, mlp_out_bias, layer, attn_gain, attn_shift, layer + 1
            )
            normed = exchange_mp(spread).reshape(rows, width)
    norm_one, norm_two, bias_proj, bias_inner = {}, {}, {}, {}
    for layer in reversed(range(layers)):
        now = kept[layer]
        if layer == layers - 1:
            (
                now["active"],
                grad_before,
                bias_inner[layer],
                part,
                grad_own,
                grad_full,
                now["normed_mlp"],
            ) = mlp_last(now["normed_mlp"], cotangent, mlp_in_weight, mlp_in_bias, mlp_out_weight)
            own_cotangent = grad_own
        else:
            grad_before, bias_inner[layer], part, grad_full = mlp_backward(
                grad_full, now["before"], mlp_in_weight, mlp_out_weight, layer
            )
        mlp_pairs = [(now["normed_mlp"], grad_before), (grad_full, now["active"])]
        middle_grad, spread, norm_two[layer], *ends = norm_backward(
            exchange_mp(part),
            now["middle"],
            mlp_gain,
            layer,
            grad_own,
            bias=mlp_out_bias if layer == layers - 1 else None,
        )
        if ends:
            output = lax.all_gather(ends[0], "mp", axis=0, tiled=True)
        spread, grad_rows, delta, branch = grad_attended(
            exchange_mp(spread), out_weight, layer, now["flat"]
        )
        grad_mine = gather_chips(spread)
        query_grad = query_side(
            now["message"], now["log_total"], delta, now["mine"], now["theirs"], grad_rows, *where
        )
        grad_theirs = from_other_core(after(grad_mine, query_grad))
        part, proj_grad, bias_proj[layer], key_small = key_side(
            now["queries"],
            grad_mine,
            grad_theirs,
            now["pair"],
            query_grad,
            qkv,
            layer,
            *where,
            unit if layer == 0 else None,
        )
        out_pairs = [(branch, now["attended_low"])]
        proj_pairs = [(now["normed"], proj_grad)]
        if layer:
            grad_own, spread, norm_one[layer] = norm_backward(
                exchange_mp(part), now["hidden"], attn_gain, layer, middle_grad
            )
            grad_full = exchange_mp(spread)
            first = scatter_sum(mlp_pairs + out_pairs + proj_pairs)
        else:
            second = scatter_sum(mlp_pairs + out_pairs)
            mine, away = last_products(
                proj_pairs,
                norm_one[1],
                norm_two,
                key_small,
                own_cotangent,
                [bias_proj[0], bias_proj[1]],
                [bias_inner[0], bias_inner[1]],
            )
            third = gather_chips(add_cores(mine, from_other_core(away), width // dp_count))
            ignored, spread, ignored = norm_backward(
                exchange_mp(part), now["hidden"], attn_gain, layer, middle_grad, third
            )
            tail = exchange_mp(spread)

    qkv_grad, out_grad, inner_grad, down_grad, small = finish_weights(
        first, second, third, local, units
    )
    (
        input_grad,
        gain_one,
        shift_one,
        out_bias_grad,
        gain_two,
        shift_two,
        down_bias_grad,
        output,
    ) = finish_rows(tail, output, width)
    bias_columns = qv_bias.shape[3] // dp_count
    qv_grad = small[:4, : 2 * bias_columns].reshape(layers, 2, 2, bias_columns)
    inner_bias_grad = small[4:12, : 2 * bias_columns].reshape(layers, units // 64, bias_columns)
    return (
        output,
        input_grad,
        gain_one,
        shift_one,
        qkv_grad.transpose(0, 2, 1, 3),
        qv_grad,
        out_grad.transpose(0, 2, 1),
        out_bias_grad,
        gain_two,
        shift_two,
        inner_grad,
        inner_bias_grad,
        down_grad.transpose(0, 2, 1),
        down_bias_grad,
    )


def solution(mesh):
    in_specs = (
        P("dp", None),
        P("dp", None),
        P(),
        P(),
        P(),
        P(),
        P(None, None, None, "mp"),
        P(None, None, "mp", None),
        P(None, "mp", None),
        P(),
        P(),
        P(),
        P(None, None, "mp"),
        P(None, "mp"),
        P(None, "mp", None),
        P(),
    )
    out_specs = (
        P("dp", None),
        P("dp", None),
        P(None, "dp"),
        P(None, "dp"),
        P(None, "dp", None, "mp"),
        P(None, None, "mp", "dp"),
        P(None, "mp", "dp"),
        P(None, "dp"),
        P(None, "dp"),
        P(None, "dp"),
        P(None, "dp", "mp"),
        P(None, "mp", "dp"),
        P(None, "mp", "dp"),
        P(None, "dp"),
    )
    return jax.shard_map(body, mesh=mesh, in_specs=in_specs, out_specs=out_specs, check_vma=False)
```

```python
import functools
import math

import jax
import jax.numpy as jnp
from jax import lax
from jax.experimental import pallas as pl
from jax.experimental.pallas import tpu as pltpu
from jax.sharding import PartitionSpec as P

norm_eps = 1e-05
f32 = jnp.float32
bf16 = jnp.bfloat16
absent = -1e30


class Cost:
    weight = 0.0


def chip_groups(count):
    return [list(range(core, count, 2)) for core in range(2)]


def other_core(count):
    return [(index, index ^ 1) for index in range(count)]


def exchange_mp(spread):
    return lax.all_to_all(spread, "mp", 0, 0, tiled=True)


def gather_chips(spread):
    groups = chip_groups(lax.axis_size("dp"))
    return lax.all_to_all(spread, "dp", 0, 0, tiled=True, axis_index_groups=groups)


def from_other_core(blocks):
    return lax.ppermute(blocks, "dp", other_core(lax.axis_size("dp")))


def after(value, *others):
    return lax.optimization_barrier((value,) + others)[0]


def whole(memory=pltpu.VMEM):
    return pl.BlockSpec(memory_space=memory)


def of_layer(stacked, layer):
    tail = stacked.shape[1:]
    return pl.BlockSpec((1,) + tail, lambda step: (layer,) + (0,) * len(tail))


def plain(array):
    return pl.BlockSpec(array.shape, lambda step: (0,) * len(array.shape))


def far(array):
    return pltpu.with_memory_space_constraint(array, pltpu.HBM)


def run_kernel(kernel, inputs, in_specs, outputs, flops=0, scratch=(), limit=12):
    moved = sum(math.prod(out[0]) * jnp.dtype(out[1]).itemsize for out in outputs)
    moved += sum(item.size * item.dtype.itemsize for item in inputs)
    return pl.pallas_call(
        kernel,
        grid=(1,),
        in_specs=in_specs,
        out_specs=[
            whole(pltpu.HBM)
            if len(out) == 4
            else pl.BlockSpec(out[0], functools.partial(lambda rank, step: (0,) * rank, len(out[0])))
            for out in outputs
        ],
        out_shape=[
            out[2](out[0], out[1]) if len(out) > 2 else jax.ShapeDtypeStruct(out[0], out[1])
            for out in outputs
        ],
        scratch_shapes=list(scratch),
        compiler_params=pltpu.CompilerParams(vmem_limit_bytes=limit * 2**20),
        cost_estimate=pl.CostEstimate(
            flops=int(Cost.weight * 1e9 + flops), bytes_accessed=moved, transcendentals=0
        ),
    )(*inputs)


def keep_in_hbm(pairs, sems):
    copies = [
        pltpu.make_async_copy(source, kept, sems.at[index])
        for index, (source, kept) in enumerate(pairs)
    ]
    for copy in copies:
        copy.start()
    return copies


def dot_nn(left, right):
    return lax.dot_general(left, right, (((1,), (0,)), ((), ())), preferred_element_type=f32)


def dot_nt(left, right):
    return lax.dot_general(left, right, (((1,), (1,)), ((), ())), preferred_element_type=f32)


def dot_tn(left, right):
    return lax.dot_general(left, right, (((0,), (0,)), ((), ())), preferred_element_type=f32)


def row_stats(inputs):
    average = jnp.mean(inputs, axis=-1, keepdims=True)
    centered = inputs - average
    variance = jnp.mean(centered * centered, axis=-1, keepdims=True)
    return centered, lax.rsqrt(variance + norm_eps)


def add_parts(got_ref):
    total = got_ref[0].astype(f32)
    for part in range(1, got_ref.shape[0]):
        total += got_ref[part].astype(f32)
    return total


def residual_norm(got, residual, bias, bias_layer, gain, shift, norm_layer):
    parts, rows, width = got.shape

    def kernel(got_ref, residual_ref, bias_ref, gain_ref, shift_ref, out_ref, spread_ref):
        total = residual_ref[...] + add_parts(got_ref) + bias_ref[bias_layer : bias_layer + 1, :]
        out_ref[...] = total
        layer = slice(norm_layer, norm_layer + 1)
        centered, inverse = row_stats(total)
        normed = (centered * inverse * gain_ref[layer, :] + shift_ref[layer, :]).astype(bf16)
        for part in range(parts):
            spread_ref[part] = normed

    inputs = [got, residual, bias, gain, shift]
    outputs = [((rows, width), f32, pltpu.HBM), ((parts, rows, width), bf16)]
    return run_kernel(kernel, inputs, [plain(item) for item in inputs], outputs)


def norm_backward(got, inputs, gain, layer, grad, extra=None, bias=None):
    parts, rows, width = got.shape
    if bias is not None:
        rows //= 2
    more = 0 if extra is None else 128

    def kernel(got_ref, inputs_ref, gain_ref, grad_ref, *refs):
        if bias is None:
            out_ref, spread_ref, small_ref = refs[-3:]
        else:
            bias_ref, out_ref, spread_ref, small_ref, output_ref = refs
        total = add_parts(got_ref)
        into = total[:rows]
        if bias is not None:
            output_ref[...] = inputs_ref[...] + total[rows:] + bias_ref[layer : layer + 1, :]
        centered, inverse = row_stats(inputs_ref[...])
        unit = centered * inverse
        scaled = into * gain_ref[layer : layer + 1, :]
        first = jnp.mean(scaled, axis=-1, keepdims=True)
        second = jnp.mean(scaled * unit, axis=-1, keepdims=True)
        total = grad_ref[...] + (scaled - first - unit * second) * inverse
        out_ref[...] = total
        rounded = total.astype(bf16)
        for part in range(parts):
            spread_ref[part, :, :width] = rounded
        if more:
            small = jnp.zeros((8, 128), f32)
            for chip in range(extra.shape[0]):
                piece = refs[0][chip, -16:, :128].astype(f32)
                small += piece[:8] + piece[8:]
            high = small.astype(bf16).astype(f32)
            zero = jnp.zeros((rows - 16, 128), f32)
            both = jnp.concatenate([high, small - high, zero], axis=0).astype(bf16)
            for part in range(parts):
                spread_ref[part, :, width:] = both
        small_ref[0:1, :] = jnp.sum(into * unit, axis=0, keepdims=True)
        small_ref[1:2, :] = jnp.sum(into, axis=0, keepdims=True)
        small_ref[2:3, :] = jnp.sum(rounded.astype(f32), axis=0, keepdims=True)
        small_ref[3:, :] = jnp.zeros((5, width), f32)

    inputs = [got, inputs, gain, grad] + [item for item in (extra, bias) if item is not None]
    outputs = [
        ((rows, width), f32, pltpu.HBM),
        ((parts, rows, width + more), bf16),
        ((8, width), f32, pltpu.HBM),
    ]
    if bias is not None:
        outputs.append(((rows, width), f32, pltpu.HBM))
    return run_kernel(kernel, inputs, [plain(item) for item in inputs], outputs)


class Places:
    def __init__(self, owner_ref, lengths_ref, rows):
        self.owner_ref, self.rows = owner_ref, rows
        self.device = lax.axis_index("dp")
        self.core = lax.rem(self.device, 2)
        self.own = owner_ref[self.device] * rows
        self.ends = []
        for scene in range(lengths_ref.shape[0]):
            before = self.ends[-1] if self.ends else 0
            self.ends.append(before + lengths_ref[scene])

    def device_of(self, index, same_core):
        return 2 * index + (self.core if same_core else 1 - self.core)

    def start(self, index, same_core):
        return self.owner_ref[self.device_of(index, same_core)] * self.rows

    def label(self, position):
        return sum((position >= end).astype(jnp.int32) for end in self.ends)

    def scalar_label(self, position):
        return sum(jnp.where(position >= end, 1, 0).astype(jnp.int32) for end in self.ends)

    def over_blocks(self, count, same_core, step):
        last = self.rows - 1
        own_first, own_last = self.scalar_label(self.own), self.scalar_label(self.own + last)
        own_alone = own_first == own_last

        def one(index, carry):
            start = self.start(index, same_core)
            first, end = self.scalar_label(start), self.scalar_label(start + last)
            meets = jnp.logical_and(first <= own_last, own_first <= end)
            alone = jnp.logical_and(first == end, own_alone)

            @pl.when(jnp.logical_and(meets, alone))
            def _():
                step(index, start, False)

            @pl.when(jnp.logical_and(meets, jnp.logical_not(alone)))
            def _():
                step(index, start, True)

            return carry

        lax.fori_loop(0, count, one, 0)


def scalars():
    return [whole(pltpu.SMEM), whole(pltpu.SMEM)]


def head_stack(rows):
    lane = lax.broadcasted_iota(jnp.int32, rows.shape, 1)
    half = rows.shape[1] // 2
    zero = jnp.zeros_like(rows)
    return jnp.concatenate(
        [jnp.where(lane < half, rows, zero), jnp.where(lane >= half, rows, zero)], axis=0
    )


def heads_from_lanes(stacked):
    half, rows = stacked.shape[0] // 2, stacked.shape[1] // 2
    return jnp.concatenate([stacked[:half, :rows], stacked[half:, rows:]], axis=0)


def heads_from_rows(stacked):
    rows = stacked.shape[0] // 2
    lane = lax.broadcasted_iota(jnp.int32, (rows, stacked.shape[1]), 1)
    return jnp.where(lane < stacked.shape[1] // 2, stacked[:rows], stacked[rows:])


def row_pieces(vector, count):
    pieces = []
    rest = vector
    for piece in range(count):
        term = rest.astype(bf16).astype(f32)
        rest = rest - term
        pieces += [term[:, start : start + 128] for start in range(0, vector.shape[1], 128)]
    row = lax.broadcasted_iota(jnp.int32, (16, 128), 0)
    tile = jnp.zeros((16, 128), f32)
    for index, piece in enumerate(pieces):
        tile = jnp.where(row == index, jnp.broadcast_to(piece, (16, 128)), tile)
    return tile.astype(bf16)


def rows_back(tile, count, length):
    tile = tile.astype(f32)
    lines = length // 128
    out = []
    for line in range(lines):
        total = tile[line : line + 1]
        for piece in range(1, count):
            total = total + tile[piece * lines + line : piece * lines + line + 1]
        out.append(total)
    return jnp.concatenate(out, axis=1)


def attention_blocks(query_ref, block_ref, places, same_core, stack_ref, peak_ref, total_ref, sum_ref):
    rows, local = query_ref.shape
    scale = 1.0 / math.sqrt(local // 2)
    scaled = (query_ref[...].astype(f32) * scale).astype(bf16)
    stack_ref[...] = head_stack(scaled)
    lanes = lax.broadcasted_iota(jnp.int32, (1, 2 * rows), 1)
    own_label = places.label(places.own + jnp.where(lanes >= rows, lanes - rows, lanes))

    def step(index, start, masked):
        keys = block_ref[index, :, :local]
        values = block_ref[index, :, local:]
        scores = dot_nt(keys, stack_ref[...])
        if masked:
            label = places.label(start + lax.broadcasted_iota(jnp.int32, (rows, 128), 0))
            label = jnp.concatenate([label] * (2 * rows // 128), axis=1)
            scores = jnp.where(label == own_label, scores, absent)
        old = peak_ref[...]
        new = jnp.maximum(old, jnp.max(scores, axis=0, keepdims=True))
        weight = jnp.exp(scores - new)
        fade = jnp.exp(old - new)
        peak_ref[...] = new
        total_ref[...] = total_ref[...] * fade + jnp.sum(weight, axis=0, keepdims=True)
        sum_ref[...] = sum_ref[...] * fade + dot_tn(values, weight.astype(bf16))

    places.over_blocks(block_ref.shape[0], same_core, step)
    return scaled


def attention_begin(query, mine, owner, lengths):
    rows, local = query.shape

    def kernel(
        owner_ref,
        lengths_ref,
        query_ref,
        mine_ref,
        peak_ref,
        total_ref,
        sum_ref,
        kept_ref,
        stack_ref,
        sems,
    ):
        copies = keep_in_hbm([(mine_ref, kept_ref)], sems)
        places = Places(owner_ref, lengths_ref, rows)
        peak_ref[...] = jnp.full(peak_ref.shape, 0.1 * absent, f32)
        total_ref[...] = jnp.zeros(total_ref.shape, f32)
        sum_ref[...] = jnp.zeros(sum_ref.shape, f32)
        attention_blocks(
            query_ref, mine_ref, places, True, stack_ref, peak_ref, total_ref, sum_ref
        )
        copies[0].wait()

    return run_kernel(
        kernel,
        [owner, lengths, query, mine],
        scalars() + [plain(query), plain(mine)],
        [
            ((1, 2 * rows), f32),
            ((1, 2 * rows), f32),
            ((local, 2 * rows), f32),
            (mine.shape, bf16, pltpu.HBM, True),
        ],
        flops=32 * rows * mine.shape[0] * rows * local,
        limit=16,
        scratch=[pltpu.VMEM((2 * rows, local), bf16), pltpu.SemaphoreType.DMA((1,))],
    )


def attention_end(query, theirs, state, out_weight, layer, owner, lengths):
    rows, local = query.shape
    width = out_weight.shape[2]
    mp_count = lax.axis_size("mp")

    def kernel(
        owner_ref,
        lengths_ref,
        query_ref,
        theirs_ref,
        old_peak_ref,
        old_total_ref,
        old_sum_ref,
        weight_ref,
        part_ref,
        low_ref,
        flat_ref,
        log_ref,
        message_ref,
        kept_ref,
        stack_ref,
        peak_ref,
        total_ref,
        sum_ref,
        sems,
    ):
        copies = keep_in_hbm([(theirs_ref, kept_ref)], sems)
        places = Places(owner_ref, lengths_ref, rows)
        peak_ref[...] = old_peak_ref[...]
        total_ref[...] = old_total_ref[...]
        sum_ref[...] = old_sum_ref[...]
        scaled = attention_blocks(
            query_ref, theirs_ref, places, False, stack_ref, peak_ref, total_ref, sum_ref
        )
        attended = heads_from_lanes(sum_ref[...] / total_ref[...])
        flat_ref[...] = attended
        low = attended.T.astype(bf16)
        low_ref[...] = low
        part = dot_nn(low, weight_ref[0]).astype(bf16)
        part_ref[...] = part.reshape(part_ref.shape)
        log_total = peak_ref[...] + jnp.log(total_ref[...])
        log_ref[...] = log_total
        message_ref[:rows, :] = scaled
        message_ref[rows:, :] = row_pieces(log_total, 3)
        copies[0].wait()

    inputs = [owner, lengths, query, theirs] + list(state) + [out_weight]
    return run_kernel(
        kernel,
        inputs,
        scalars() + [plain(item) for item in inputs[2:7]] + [of_layer(out_weight, layer)],
        [
            ((mp_count, rows // mp_count, width), bf16),
            ((rows, local), bf16, pltpu.HBM),
            ((local, rows), f32, pltpu.HBM),
            ((1, 2 * rows), f32, pltpu.HBM),
            ((rows + 16, local), bf16, pltpu.HBM),
            (theirs.shape, bf16, pltpu.HBM, True),
        ],
        flops=32 * rows * theirs.shape[0] * rows * local,
        limit=16,
        scratch=[
            pltpu.VMEM((2 * rows, local), bf16),
            pltpu.VMEM((1, 2 * rows), f32),
            pltpu.VMEM((1, 2 * rows), f32),
            pltpu.VMEM((local, 2 * rows), f32),
            pltpu.SemaphoreType.DMA((1,)),
        ],
    )


def grad_attended(branch, out_weight, layer, flat):
    rows = branch.shape[0] * branch.shape[1]
    local = out_weight.shape[1]

    chips = lax.axis_size("dp") // 2

    def kernel(
        branch_ref, weight_ref, flat_ref, spread_ref, message_ref, delta_ref, kept_ref, sems
    ):
        copies = keep_in_hbm([(branch_ref, kept_ref)], sems)
        grad = dot_nt(branch_ref[...].reshape(rows, -1), weight_ref[0]).astype(bf16)
        product = grad.astype(f32).T * flat_ref[...]
        half = local // 2
        delta = jnp.concatenate(
            [
                jnp.sum(product[:half], axis=0, keepdims=True),
                jnp.sum(product[half:], axis=0, keepdims=True),
            ],
            axis=1,
        )
        delta_ref[...] = delta
        pieces = row_pieces(delta, 3)
        message_ref[...] = grad
        for chip in range(chips):
            spread_ref[chip, :rows, :] = grad
            spread_ref[chip, rows:, :] = pieces
        copies[0].wait()

    inputs = [branch, far(out_weight), far(flat)]
    return run_kernel(
        kernel,
        inputs,
        [plain(branch), of_layer(out_weight, layer), plain(flat)],
        [
            ((chips, rows + 16, local), bf16),
            ((rows, local), bf16),
            ((1, 2 * rows), f32),
            (branch.shape, bf16, pltpu.HBM, True),
        ],
        flops=2 * rows * local * branch.shape[2],
        scratch=[pltpu.SemaphoreType.DMA((1,))],
    )


def query_side(message, log_total, delta, mine, theirs, grad, owner, lengths):
    rows, local = grad.shape
    half = mine.shape[0]
    count = 2 * half
    scale = 1.0 / math.sqrt(local // 2)

    def kernel(
        owner_ref,
        lengths_ref,
        query_ref,
        log_ref,
        delta_ref,
        mine_ref,
        theirs_ref,
        grad_ref,
        out_ref,
        stack_ref,
        grad_stack_ref,
        sum_ref,
    ):
        places = Places(owner_ref, lengths_ref, rows)
        stack_ref[...] = head_stack(query_ref[:rows, :])
        grad_stack_ref[...] = head_stack(grad_ref[...])
        sum_ref[...] = jnp.zeros(sum_ref.shape, f32)
        lanes = lax.broadcasted_iota(jnp.int32, (1, 2 * rows), 1)
        own_label = places.label(places.own + jnp.where(lanes >= rows, lanes - rows, lanes))

        def step(block_ref, index, start, masked):
            keys = block_ref[index, :, :local]
            values = block_ref[index, :, local:]
            scores = dot_nt(keys, stack_ref[...]) - log_ref[...]
            if masked:
                label = places.label(start + lax.broadcasted_iota(jnp.int32, (rows, 128), 0))
                label = jnp.concatenate([label] * (2 * rows // 128), axis=1)
                scores = jnp.where(label == own_label, scores, absent)
            probs = jnp.exp(scores)
            grad_probs = dot_nt(values, grad_stack_ref[...])
            grad_scores = (probs * (grad_probs - delta_ref[...])).astype(bf16)
            sum_ref[...] += dot_tn(keys, grad_scores)

        places.over_blocks(half, True, functools.partial(step, mine_ref))
        places.over_blocks(half, False, functools.partial(step, theirs_ref))
        out_ref[...] = (heads_from_lanes(sum_ref[...]) * scale).T.astype(bf16)

    inputs = [owner, lengths, far(message), far(log_total), delta, far(mine), far(theirs), grad]
    return run_kernel(
        kernel,
        inputs,
        scalars() + [plain(item) for item in inputs[2:]],
        [((rows, local), bf16)],
        flops=64 * rows * count * rows * local,
        limit=16,
        scratch=[
            pltpu.VMEM((2 * rows, local), bf16),
            pltpu.VMEM((2 * rows, local), bf16),
            pltpu.VMEM((local, 2 * rows), f32),
        ],
    )[0]


def key_blocks(own_ref, queries_ref, block_ref, places, same_core, refs):
    keys_ref, values_ref, key_sum_ref, value_sum_ref = refs
    rows, local = own_ref.shape[0], own_ref.shape[1] // 2
    keys_ref[...] = head_stack(own_ref[:, :local])
    values_ref[...] = head_stack(own_ref[:, local:])
    own_label = places.label(places.own + lax.broadcasted_iota(jnp.int32, (rows, 128), 0))
    own_label = jnp.concatenate([own_label] * (rows // 128), axis=1)
    own_label = jnp.concatenate([own_label] * 2, axis=0)

    def spread(row):
        return jnp.concatenate(
            [
                jnp.broadcast_to(row[:, :rows], (rows, rows)),
                jnp.broadcast_to(row[:, rows:], (rows, rows)),
            ],
            axis=0,
        )

    def step(index, start, masked):
        source = places.device_of(index, same_core)
        query = queries_ref[source, :rows, :]
        grad = block_ref[index, :rows, :]
        log_total = rows_back(queries_ref[source, rows:, :], 3, 2 * rows)
        delta = rows_back(block_ref[index, rows:, :], 3, 2 * rows)
        scores = dot_nt(keys_ref[...], query) - spread(log_total)
        if masked:
            lanes = start + lax.broadcasted_iota(jnp.int32, (1, rows), 1)
            scores = jnp.where(own_label == places.label(lanes), scores, absent)
        probs = jnp.exp(scores)
        grad_probs = dot_nt(values_ref[...], grad)
        grad_scores = (probs * (grad_probs - spread(delta))).astype(bf16)
        value_sum_ref[...] += dot_nn(probs.astype(bf16), grad)
        key_sum_ref[...] += dot_nn(grad_scores, query)

    places.over_blocks(block_ref.shape[0], same_core, step)


def key_begin(queries, mine, key_value, owner, lengths):
    rows, local = key_value.shape[0], key_value.shape[1] // 2

    def kernel(
        owner_ref,
        lengths_ref,
        queries_ref,
        mine_ref,
        own_ref,
        key_sum_ref,
        value_sum_ref,
        keys_ref,
        values_ref,
    ):
        places = Places(owner_ref, lengths_ref, rows)
        key_sum_ref[...] = jnp.zeros(key_sum_ref.shape, f32)
        value_sum_ref[...] = jnp.zeros(value_sum_ref.shape, f32)
        refs = keys_ref, values_ref, key_sum_ref, value_sum_ref
        key_blocks(own_ref, queries_ref, mine_ref, places, True, refs)

    inputs = [owner, lengths, far(queries), mine, far(key_value)]
    return run_kernel(
        kernel,
        inputs,
        scalars() + [plain(item) for item in inputs[2:]],
        [((2 * rows, local), f32), ((2 * rows, local), f32)],
        flops=64 * rows * mine.shape[0] * rows * local,
        limit=16,
        scratch=[pltpu.VMEM((2 * rows, local), bf16), pltpu.VMEM((2 * rows, local), bf16)],
    )


def key_end(
    queries, theirs, key_value, sums, query_grad, qkv, layer, owner, lengths, unit
):
    rows, local = key_value.shape[0], key_value.shape[1] // 2
    width = qkv.shape[2]
    mp_count = lax.axis_size("mp")
    with_unit = unit is not None

    def kernel(
        owner_ref,
        lengths_ref,
        queries_ref,
        theirs_ref,
        own_ref,
        old_key_ref,
        old_value_ref,
        grad_ref,
        weight_ref,
        *refs,
    ):
        places = Places(owner_ref, lengths_ref, rows)
        if with_unit:
            unit_ref, refs = refs[0], refs[1:]
        part_ref, proj_ref, bias_ref, small_ref = refs[:4]
        keys_ref, values_ref, key_sum_ref, value_sum_ref = refs[4:]
        key_sum_ref[...] = old_key_ref[...]
        value_sum_ref[...] = old_value_ref[...]
        key_blocks(own_ref, queries_ref, theirs_ref, places, False, refs[4:])
        key_grad = heads_from_rows(key_sum_ref[...]).astype(bf16)
        value_grad = heads_from_rows(value_sum_ref[...]).astype(bf16)
        query_grad = grad_ref[...]
        proj_ref[:, :local] = query_grad
        proj_ref[:, local : 2 * local] = key_grad
        proj_ref[:, 2 * local :] = value_grad
        bias_ref[...] = jnp.zeros(bias_ref.shape, f32)
        bias_ref[0:1, :] = jnp.sum(query_grad.astype(f32), axis=0, keepdims=True)
        bias_ref[1:2, :] = jnp.sum(value_grad.astype(f32), axis=0, keepdims=True)
        part = dot_nt(query_grad, weight_ref[0, 0])
        part += dot_nt(key_grad, weight_ref[0, 1])
        part += dot_nt(value_grad, weight_ref[0, 2])
        low = part.astype(bf16)
        part_ref[...] = low.reshape(part_ref.shape)
        small_ref[...] = jnp.zeros(small_ref.shape, f32)
        if with_unit:
            into = low.astype(f32)
            small_ref[0:1, :] = jnp.sum(into * unit_ref[...], axis=0, keepdims=True)
            small_ref[1:2, :] = jnp.sum(into, axis=0, keepdims=True)

    inputs = [owner, lengths, far(queries), theirs, far(key_value)] + list(sums)
    inputs += [query_grad, far(qkv)]
    in_specs = scalars() + [plain(item) for item in inputs[2:8]] + [of_layer(qkv, layer)]
    if with_unit:
        inputs.append(far(unit))
        in_specs.append(plain(unit))
    return run_kernel(
        kernel,
        inputs,
        in_specs,
        [
            ((mp_count, rows // mp_count, width), bf16),
            ((rows, 3 * local), bf16, pltpu.HBM),
            ((8, local), f32, pltpu.HBM),
            ((8, width), f32, pltpu.HBM),
        ],
        flops=64 * rows * theirs.shape[0] * rows * local,
        limit=18,
        scratch=[
            pltpu.VMEM((2 * rows, local), bf16),
            pltpu.VMEM((2 * rows, local), bf16),
            pltpu.VMEM((2 * rows, local), f32),
            pltpu.VMEM((2 * rows, local), f32),
        ],
    )


def project(normed, qkv, bias, layer, first=None):
    rows, width = normed.shape
    local = qkv.shape[3]
    chips = lax.axis_size("dp") // 2
    own_rows = rows // lax.axis_size("mp")

    def kernel(normed_ref, weight_ref, bias_ref, *refs):
        if first is None:
            query_ref, pair_ref, spread_ref, kept_ref, sems = refs
            copies = keep_in_hbm([(normed_ref, kept_ref)], sems)
            normed = normed_ref[...]
        else:
            gain_ref, shift_ref, query_ref, pair_ref, spread_ref = refs[:5]
            own_ref, low_ref, unit_ref = refs[5:]
            centered, inverse = row_stats(normed_ref[...])
            unit = centered * inverse
            unit_ref[...] = unit
            normed = (unit * gain_ref[0:1, :] + shift_ref[0:1, :]).astype(bf16)
            low_ref[...] = normed
            own = pl.multiple_of(lax.axis_index("mp") * own_rows, own_rows)
            own_ref[...] = normed_ref[pl.ds(own, own_rows), :]
        query_bias, value_bias = (
            jnp.concatenate([bias_ref[0, at, 0:1, :], bias_ref[0, at, 1:2, :]], axis=1)
            for at in range(2)
        )
        query = dot_nn(normed, weight_ref[0, 0]) + query_bias
        query_ref[...] = query.astype(bf16)
        keys = dot_nn(normed, weight_ref[0, 1]).astype(bf16)
        values = (dot_nn(normed, weight_ref[0, 2]) + value_bias).astype(bf16)
        pair_ref[:, :local] = keys
        pair_ref[:, local:] = values
        for chip in range(chips):
            spread_ref[chip, :, :local] = keys
            spread_ref[chip, :, local:] = values
        if first is None:
            copies[0].wait()

    inputs = [normed, qkv, bias] if first is None else [far(normed), far(qkv), far(bias)]
    in_specs = [plain(normed), of_layer(qkv, layer), of_layer(bias, layer)]
    outputs = [
        ((rows, local), bf16),
        ((rows, 2 * local), bf16, pltpu.HBM),
        ((chips, rows, 2 * local), bf16),
    ]
    scratch = []
    if first is None:
        outputs.append((normed.shape, bf16, pltpu.HBM, True))
        scratch.append(pltpu.SemaphoreType.DMA((1,)))
    else:
        inputs += [far(item) for item in first]
        in_specs += [plain(item) for item in first]
        outputs += [
            ((own_rows, width), f32, pltpu.HBM),
            ((rows, width), bf16, pltpu.HBM),
            ((rows, width), f32, pltpu.HBM),
        ]
    return run_kernel(
        kernel, inputs, in_specs, outputs, flops=6 * rows * width * local, scratch=scratch
    )


def mlp_forward(normed, inner, inner_bias, down, layer):
    parts, part_rows, width = normed.shape
    rows, units = parts * part_rows, inner.shape[2]

    def kernel(
        normed_ref,
        inner_ref,
        bias_ref,
        down_ref,
        before_ref,
        active_ref,
        part_ref,
        kept_ref,
        sems,
    ):
        copies = keep_in_hbm([(normed_ref, kept_ref)], sems)
        own = normed_ref[...].reshape(rows, width)
        before = dot_nn(own, inner_ref[0]) + bias_ref[layer : layer + 1, :]
        before_ref[...] = before
        active = gelu(before).astype(bf16)
        active_ref[...] = active
        part_ref[...] = dot_nn(active, down_ref[0]).astype(bf16).reshape(part_ref.shape)
        copies[0].wait()

    inputs = [normed, far(inner), inner_bias, far(down)]
    return run_kernel(
        kernel,
        inputs,
        [plain(normed), of_layer(inner, layer), plain(inner_bias), of_layer(down, layer)],
        [
            ((rows, units), f32, pltpu.HBM),
            ((rows, units), bf16, pltpu.HBM),
            ((parts, part_rows, width), bf16),
            (normed.shape, bf16, pltpu.HBM, True),
        ],
        flops=4 * rows * width * units,
        scratch=[pltpu.SemaphoreType.DMA((1,))],
    )


def gelu(before):
    return 0.5 * before * (1.0 + lax.erf(before * math.sqrt(0.5)))


def gelu_slope(before):
    slope = 0.5 * (1.0 + lax.erf(before * math.sqrt(0.5)))
    return slope + before * jnp.exp(-0.5 * before * before) * (1.0 / math.sqrt(2.0 * math.pi))


def mlp_last(normed, cotangent, inner, inner_bias, down):
    parts, part_rows, width = normed.shape
    layer = inner.shape[0] - 1
    rows, units = parts * part_rows, inner.shape[2]

    def kernel(
        normed_ref,
        cotangent_ref,
        inner_ref,
        inner_bias_ref,
        down_ref,
        active_ref,
        out_ref,
        bias_ref,
        part_ref,
        own_ref,
        full_ref,
        kept_ref,
        sems,
    ):
        copies = keep_in_hbm([(normed_ref, kept_ref)], sems)
        grad = cotangent_ref[...].astype(bf16)
        full_ref[...] = grad.reshape(full_ref.shape)
        own = pl.multiple_of(lax.axis_index("mp") * part_rows, part_rows)
        own_ref[...] = cotangent_ref[pl.ds(own, part_rows), :]
        before = dot_nn(normed_ref[...].reshape(rows, width), inner_ref[0])
        before += inner_bias_ref[layer : layer + 1, :]
        out = (dot_nt(grad, down_ref[0]) * gelu_slope(before)).astype(bf16)
        out_ref[...] = out
        bias_ref[...] = jnp.broadcast_to(
            jnp.sum(out.astype(f32), axis=0, keepdims=True), bias_ref.shape
        )
        part = dot_nt(out, inner_ref[0]).astype(bf16)
        part_ref[:, :part_rows, :] = part.reshape(parts, part_rows, width)
        active = gelu(before).astype(bf16)
        active_ref[...] = active
        part = dot_nn(active, down_ref[0]).astype(bf16)
        part_ref[:, part_rows:, :] = part.reshape(parts, part_rows, width)
        copies[0].wait()

    inputs = [normed, far(cotangent), far(inner), inner_bias, far(down)]
    return run_kernel(
        kernel,
        inputs,
        [
            plain(normed),
            plain(cotangent),
            of_layer(inner, layer),
            plain(inner_bias),
            of_layer(down, layer),
        ],
        [
            ((rows, units), bf16, pltpu.HBM),
            ((rows, units), bf16, pltpu.HBM),
            ((8, units), f32, pltpu.HBM),
            ((parts, 2 * part_rows, width), bf16),
            ((part_rows, width), f32, pltpu.HBM),
            ((parts, part_rows, width), bf16, pltpu.HBM),
            (normed.shape, bf16, pltpu.HBM, True),
        ],
        flops=8 * rows * width * units,
        scratch=[pltpu.SemaphoreType.DMA((1,))],
    )


def mlp_backward(grad, before, inner, down, layer):
    parts, part_rows, width = grad.shape
    rows, units = parts * part_rows, inner.shape[2]

    def kernel(
        grad_ref, before_ref, inner_ref, down_ref, out_ref, bias_ref, part_ref, kept_ref, sems
    ):
        copies = keep_in_hbm([(grad_ref, kept_ref)], sems)
        into = dot_nt(grad_ref[...].reshape(rows, width), down_ref[0])
        out = (into * gelu_slope(before_ref[...])).astype(bf16)
        out_ref[...] = out
        bias_ref[...] = jnp.broadcast_to(
            jnp.sum(out.astype(f32), axis=0, keepdims=True), bias_ref.shape
        )
        part_ref[...] = dot_nt(out, inner_ref[0]).astype(bf16).reshape(part_ref.shape)
        copies[0].wait()

    inputs = [grad, before, inner, down]
    return run_kernel(
        kernel,
        inputs,
        [plain(grad), plain(before), of_layer(inner, layer), of_layer(down, layer)],
        [
            ((rows, units), bf16, pltpu.HBM),
            ((8, units), f32, pltpu.HBM),
            ((parts, part_rows, width), bf16),
            (grad.shape, bf16, pltpu.HBM, True),
        ],
        flops=4 * rows * width * units,
        scratch=[pltpu.SemaphoreType.DMA((1,))],
    )


def token_products(pairs):
    columns = [right.shape[-1] for left, right in pairs]
    width = pairs[0][0].shape[-1]
    rows = pairs[0][1].shape[0]
    items = [item for pair in pairs for item in pair]
    count = len(items)

    def kernel(*refs):
        sources, out_ref, held, parts = refs[:count], refs[count], refs[count + 1 : -2], refs[-2:]
        results, sems = held[count:], parts[0]
        out_sems = parts[1]
        copies = keep_in_hbm(zip(sources, held[:count]), sems)
        writes = []
        at = 0
        for index, size in enumerate(columns):
            copies[2 * index].wait()
            copies[2 * index + 1].wait()
            left = held[2 * index][...].reshape(rows, width)
            results[index][...] = dot_tn(left, held[2 * index + 1][...]).astype(bf16)
            target = out_ref.at[:, pl.ds(at, size)]
            write = pltpu.make_async_copy(results[index], target, out_sems.at[index])
            write.start()
            writes.append(write)
            at += size
        for write in writes:
            write.wait()

    return run_kernel(
        kernel,
        [far(item) for item in items],
        [whole(pltpu.HBM)] * count,
        [((width, sum(columns)), bf16, pltpu.HBM, True)],
        flops=2 * rows * width * sum(columns),
        scratch=[pltpu.VMEM(item.shape, item.dtype) for item in items]
        + [pltpu.VMEM((width, size), bf16) for size in columns]
        + [pltpu.SemaphoreType.DMA((count,)), pltpu.SemaphoreType.DMA((len(pairs),))],
    )[0]


def last_products(pairs, norm_one, norm_two, key_small, own_cotangent, proj_bias, inner_bias):
    width = own_cotangent.shape[1]
    dp_count = lax.axis_size("dp")
    columns = width // dp_count
    token_rows = pairs[0][1].shape[0]
    total = sum(right.shape[-1] for left, right in pairs)
    items = [item for pair in pairs for item in pair]
    inputs = items + [norm_one, norm_two[0], norm_two[1], key_small, own_cotangent]
    inputs = [far(item) for item in inputs + proj_bias + inner_bias]

    def kernel(*refs):
        item_refs, refs = refs[: len(items)], refs[len(items) :]
        one_ref, two_a_ref, two_b_ref, key_ref, grad_ref = refs[:5]
        proj_refs, inner_refs = refs[5:7], refs[7:9]
        mine_ref, away_ref, first_ref, second_ref, product_ref = refs[9:]
        at = 0
        for left_ref, right_ref in zip(item_refs[0::2], item_refs[1::2]):
            left = left_ref[...].reshape(token_rows, width)
            size = right_ref.shape[-1]
            product_ref[:, at : at + size] = dot_tn(left, right_ref[...]).astype(bf16)
            at += size
        last = jnp.sum(grad_ref[...].astype(bf16).astype(f32), axis=0, keepdims=True)
        zero = jnp.zeros((2, width), f32)
        for target, two_ref, gains, bias in (
            (first_ref, two_a_ref, key_ref, one_ref[2:3, :]),
            (second_ref, two_b_ref, one_ref, last),
        ):
            target[0:2, :] = gains[0:2, :]
            target[2:3, :] = two_ref[2:3, :]
            target[3:5, :] = two_ref[0:2, :]
            target[5:6, :] = bias
            target[6:8, :] = zero
        lines = [proj_refs[layer][row : row + 1, :] for layer in range(2) for row in range(2)]
        for layer in range(2):
            lines += [inner_refs[layer][0:1, 128 * at : 128 * at + 128] for at in range(4)]
        row_index = lax.broadcasted_iota(jnp.int32, (8, 128), 0)
        shared = []
        for group in (lines[:8], lines[8:]):
            tile = jnp.zeros((8, 128), f32)
            for row, line in enumerate(group):
                tile = jnp.where(row_index == row, jnp.broadcast_to(line, (8, 128)), tile)
            shared.append(tile)
        core = lax.rem(lax.axis_index("dp"), 2)
        for device in range(dp_count):
            at = slice(device * columns, (device + 1) * columns)
            small = jnp.concatenate([first_ref[:, at], second_ref[:, at]] + shared, axis=1)
            high = small.astype(bf16).astype(f32)
            tail = jnp.concatenate([high, small - high], axis=0).astype(bf16)
            for flag, ref in ((core == device % 2, mine_ref), (core != device % 2, away_ref)):

                @pl.when(flag)
                def _(ref=ref, tail=tail, device=device, at=at):
                    ref[device // 2, :columns, :] = product_ref[at, :]
                    ref[device // 2, columns:, :] = tail

    shape = ((dp_count // 2, columns + 16, total), bf16)
    return run_kernel(
        kernel,
        inputs,
        [plain(item) for item in inputs],
        [shape, shape],
        flops=2 * token_rows * width * total,
        scratch=[
            pltpu.VMEM((8, width), f32),
            pltpu.VMEM((8, width), f32),
            pltpu.VMEM((width, total), bf16),
        ],
    )


def add_cores(mine, other, columns, output):
    def kernel(mine_ref, other_ref, output_ref, out_ref, kept_ref):
        kept_ref[...] = output_ref[...]
        for chip in range(mine.shape[0]):
            both = mine_ref[chip].astype(f32) + other_ref[chip].astype(f32)
            out_ref[chip, :columns, :] = both[:columns].astype(bf16)
            small = both[columns : columns + 8] + both[columns + 8 :]
            high = small.astype(bf16).astype(f32)
            out_ref[chip, columns:, :] = jnp.concatenate([high, small - high], axis=0).astype(bf16)

    return run_kernel(
        kernel,
        [mine, other, far(output)],
        [plain(mine), plain(other), plain(output)],
        [(mine.shape, bf16), (output.shape, f32, pltpu.HBM)],
    )


def scatter_sum(pairs):
    return lax.psum_scatter(token_products(pairs), "dp", scatter_dimension=0, tiled=True)


def finish_rows(got, width):
    parts, own_rows = got.shape[:2]

    def kernel(got_ref, out_ref, *small_refs):
        total = jnp.zeros((8, 128), f32)
        for part in range(parts):
            at = slice(part * own_rows, (part + 1) * own_rows)
            out_ref[at, :] = got_ref[part, :, :width].astype(f32)
            both = got_ref[part, :16, width:].astype(f32)
            total += both[:8] + both[8:]
        for index, small_ref in enumerate(small_refs):
            small_ref[0:1, :] = total[index : index + 1, :64]
            small_ref[1:2, :] = total[index : index + 1, 64:]

    return run_kernel(
        kernel,
        [got],
        [plain(got)],
        [((parts * own_rows, width), f32, pltpu.HBM)] + [((2, 64), f32, pltpu.HBM)] * 6,
    )


def finish_biases(third, columns):
    bias_columns = columns // lax.axis_size("dp")

    def kernel(third_ref, small_ref):
        small = jnp.zeros((8, third.shape[2]), f32)
        for chip in range(third.shape[0]):
            piece = third_ref[chip, columns:, :].astype(f32)
            small += piece[:8] + piece[8:]
        small = jnp.concatenate([small[:, 128:256], small[:, 256:384]], axis=0)
        lane = lax.broadcasted_iota(jnp.int32, small.shape, 1)
        own = lax.axis_index("dp") * bias_columns
        picked = jnp.zeros(small.shape, f32)
        for half in range(2):
            for column in range(bias_columns):
                at = half * 64 + own + column
                value = jnp.sum(jnp.where(lane == at, small, 0.0), axis=1, keepdims=True)
                picked = jnp.where(lane == half * bias_columns + column, value, picked)
        small_ref[...] = picked

    return run_kernel(kernel, [third], [plain(third)], [((16, 128), f32)])[0]


def finish_weights(first, second, third, local, units):
    columns = first.shape[0]

    def kernel(first_ref, second_ref, third_ref, qkv_ref, out_ref, inner_ref, down_ref):
        last = add_parts(third_ref)
        middle, late = first_ref[...].astype(f32), second_ref[...].astype(f32)
        for layer, sums in ((1, middle), (0, late)):
            inner_ref[layer] = sums[:, :units]
            down_ref[layer] = sums[:, units : 2 * units]
            out_ref[layer] = sums[:, 2 * units : 2 * units + local]
        for piece in range(3):
            at = 2 * units + local * (piece + 1)
            qkv_ref[1, piece] = middle[:, at : at + local]
            qkv_ref[0, piece] = last[:columns, local * piece : local * (piece + 1)]

    inputs = [far(first), far(second), third]
    return run_kernel(
        kernel,
        inputs,
        [plain(item) for item in inputs],
        [
            ((2, 3, columns, local), f32, pltpu.HBM),
            ((2, columns, local), f32, pltpu.HBM),
            ((2, columns, units), f32, pltpu.HBM),
            ((2, columns, units), f32, pltpu.HBM),
        ],
    )


def body(
    hidden_in,
    cotangent,
    scene_lengths,
    block_owner,
    attn_gain,
    attn_shift,
    qkv_weight,
    qv_bias,
    out_weight,
    out_bias,
    mlp_gain,
    mlp_shift,
    mlp_in_weight,
    mlp_in_bias,
    mlp_out_weight,
    mlp_out_bias,
):
    rows, width = hidden_in.shape
    layers = attn_gain.shape[0]
    local = qv_bias.shape[2] * qv_bias.shape[3]
    units = mlp_in_bias.shape[1]
    dp_count, mp_count = lax.axis_size("dp"), lax.axis_size("mp")
    own_rows = rows // mp_count
    qkv = qkv_weight.transpose(0, 2, 1, 3)
    where = (block_owner, scene_lengths)
    Cost.weight = 0.0

    kept = []
    for layer in range(layers):
        if layer:
            query, pair, spread, normed = project(normed, qkv, qv_bias, layer)
            spread = after(spread, queries)
        else:
            query, pair, spread, hidden, normed, unit = project(
                hidden_in, qkv, qv_bias, layer, (attn_gain, attn_shift)
            )
        mine = gather_chips(spread)
        theirs = from_other_core(mine)
        *state, mine = attention_begin(query, mine, *where)
        part, attended_low, flat, log_total, message, theirs = attention_end(
            query, theirs, state, out_weight, layer, *where
        )
        got = exchange_mp(part)
        queries = lax.all_gather(after(message, got), "dp", axis=0, tiled=True)
        queries = queries.reshape((dp_count,) + message.shape)
        middle, spread = residual_norm(
            got, hidden, out_bias, layer, mlp_gain, mlp_shift, layer
        )
        normed_mlp = exchange_mp(spread)
        if layer + 1 < layers:
            before, active, part, normed_mlp = mlp_forward(
                normed_mlp, mlp_in_weight, mlp_in_bias, mlp_out_weight, layer
            )
        kept.append(
            dict(
                hidden=hidden,
                normed=normed,
                pair=pair,
                mine=mine,
                theirs=theirs,
                attended_low=attended_low,
                flat=flat,
                log_total=log_total,
                message=message,
                queries=queries,
                middle=middle,
                normed_mlp=normed_mlp,
                before=before,
                active=active,
            )
        )
        if layer + 1 < layers:
            hidden, spread = residual_norm(
                exchange_mp(part), middle, mlp_out_bias, layer, attn_gain, attn_shift, layer + 1
            )
            normed = exchange_mp(spread).reshape(rows, width)
    norm_one, norm_two, bias_proj, bias_inner = {}, {}, {}, {}
    for layer in reversed(range(layers)):
        now = kept[layer]
        if layer == layers - 1:
            (
                now["active"],
                grad_before,
                bias_inner[layer],
                part,
                grad_own,
                grad_full,
                now["normed_mlp"],
            ) = mlp_last(now["normed_mlp"], cotangent, mlp_in_weight, mlp_in_bias, mlp_out_weight)
            own_cotangent = grad_own
        else:
            grad_before, bias_inner[layer], part, grad_full = mlp_backward(
                grad_full, now["before"], mlp_in_weight, mlp_out_weight, layer
            )
        mlp_pairs = [(now["normed_mlp"], grad_before), (grad_full, now["active"])]
        middle_grad, spread, norm_two[layer], *ends = norm_backward(
            exchange_mp(part),
            now["middle"],
            mlp_gain,
            layer,
            grad_own,
            bias=mlp_out_bias if layer == layers - 1 else None,
        )
        if ends:
            output = lax.all_gather(ends[0], "mp", axis=0, tiled=True)
        spread, grad_rows, delta, branch = grad_attended(
            exchange_mp(spread), out_weight, layer, now["flat"]
        )
        grad_mine = gather_chips(spread)
        if not layer:
            grad_rows = after(grad_rows, output)
        query_grad = query_side(
            now["message"], now["log_total"], delta, now["mine"], now["theirs"], grad_rows, *where
        )
        grad_theirs = from_other_core(after(grad_mine, query_grad))
        sums = key_begin(now["queries"], grad_mine, now["pair"], *where)
        part, proj_grad, bias_proj[layer], key_small = key_end(
            now["queries"],
            grad_theirs,
            now["pair"],
            sums,
            query_grad,
            qkv,
            layer,
            *where,
            unit if layer == 0 else None,
        )
        if layer:
            Cost.weight = 8.5
        out_pairs = [(branch, now["attended_low"])]
        proj_pairs = [(now["normed"], proj_grad)]
        if layer:
            grad_own, spread, norm_one[layer] = norm_backward(
                exchange_mp(part), now["hidden"], attn_gain, layer, middle_grad
            )
            grad_full = exchange_mp(spread)
            first = scatter_sum(mlp_pairs + out_pairs + proj_pairs)
        else:
            second = scatter_sum(mlp_pairs + out_pairs)
            mine, away = last_products(
                proj_pairs,
                norm_one[1],
                norm_two,
                key_small,
                own_cotangent,
                [bias_proj[0], bias_proj[1]],
                [bias_inner[0], bias_inner[1]],
            )
            both, output = add_cores(mine, from_other_core(away), width // dp_count, output)
            third = gather_chips(both)
            ignored, spread, ignored = norm_backward(
                exchange_mp(part), now["hidden"], attn_gain, layer, middle_grad, third
            )
            tail = exchange_mp(spread)

    small = finish_biases(third, width // dp_count)
    qkv_grad, out_grad, inner_grad, down_grad = finish_weights(
        first, second, third, local, units
    )
    (
        input_grad,
        gain_one,
        shift_one,
        out_bias_grad,
        gain_two,
        shift_two,
        down_bias_grad,
    ) = finish_rows(tail, width)
    bias_columns = qv_bias.shape[3] // dp_count
    qv_grad = small[:4, : 2 * bias_columns].reshape(layers, 2, 2, bias_columns)
    inner_bias_grad = small[4:12, : 2 * bias_columns].reshape(layers, units // 64, bias_columns)
    return (
        output,
        input_grad,
        gain_one,
        shift_one,
        qkv_grad.transpose(0, 2, 1, 3),
        qv_grad,
        out_grad.transpose(0, 2, 1),
        out_bias_grad,
        gain_two,
        shift_two,
        inner_grad,
        inner_bias_grad,
        down_grad.transpose(0, 2, 1),
        down_bias_grad,
    )


def solution(mesh):
    in_specs = (
        P("dp", None),
        P("dp", None),
        P(),
        P(),
        P(),
        P(),
        P(None, None, None, "mp"),
        P(None, None, "mp", None),
        P(None, "mp", None),
        P(),
        P(),
        P(),
        P(None, None, "mp"),
        P(None, "mp"),
        P(None, "mp", None),
        P(),
    )
    out_specs = (
        P("dp", None),
        P("dp", None),
        P(None, "dp"),
        P(None, "dp"),
        P(None, "dp", None, "mp"),
        P(None, None, "mp", "dp"),
        P(None, "mp", "dp"),
        P(None, "dp"),
        P(None, "dp"),
        P(None, "dp"),
        P(None, "dp", "mp"),
        P(None, "mp", "dp"),
        P(None, "mp", "dp"),
        P(None, "dp"),
    )
    return jax.shard_map(body, mesh=mesh, in_specs=in_specs, out_specs=out_specs, check_vma=False)
```

```python
import functools
import math

import jax
import jax.numpy as jnp
from jax import lax
from jax.experimental import pallas as pl
from jax.experimental.pallas import tpu as pltpu
from jax.sharding import PartitionSpec as P

norm_eps = 1e-05
f32 = jnp.float32
bf16 = jnp.bfloat16
absent = -1e30


class Cost:
    weight = 0.0


def chip_groups(count):
    return [list(range(core, count, 2)) for core in range(2)]


def other_core(count):
    return [(index, index ^ 1) for index in range(count)]


def exchange_mp(spread):
    return lax.all_to_all(spread, "mp", 0, 0, tiled=True)


def gather_chips(spread):
    groups = chip_groups(lax.axis_size("dp"))
    return lax.all_to_all(spread, "dp", 0, 0, tiled=True, axis_index_groups=groups)


def from_other_core(blocks):
    return lax.ppermute(blocks, "dp", other_core(lax.axis_size("dp")))


def after(value, *others):
    return lax.optimization_barrier((value,) + others)[0]


def whole(memory=pltpu.VMEM):
    return pl.BlockSpec(memory_space=memory)


def of_layer(stacked, layer):
    tail = stacked.shape[1:]
    return pl.BlockSpec((1,) + tail, lambda step: (layer,) + (0,) * len(tail))


def plain(array):
    return pl.BlockSpec(array.shape, lambda step: (0,) * len(array.shape))


def far(array):
    return pltpu.with_memory_space_constraint(array, pltpu.HBM)


def run_kernel(kernel, inputs, in_specs, outputs, flops=0, scratch=(), limit=12):
    moved = sum(math.prod(out[0]) * jnp.dtype(out[1]).itemsize for out in outputs)
    moved += sum(item.size * item.dtype.itemsize for item in inputs)
    return pl.pallas_call(
        kernel,
        grid=(1,),
        in_specs=in_specs,
        out_specs=[
            whole(pltpu.HBM)
            if len(out) == 4
            else pl.BlockSpec(out[0], functools.partial(lambda rank, step: (0,) * rank, len(out[0])))
            for out in outputs
        ],
        out_shape=[
            out[2](out[0], out[1]) if len(out) > 2 else jax.ShapeDtypeStruct(out[0], out[1])
            for out in outputs
        ],
        scratch_shapes=list(scratch),
        compiler_params=pltpu.CompilerParams(vmem_limit_bytes=limit * 2**20),
        cost_estimate=pl.CostEstimate(
            flops=int(Cost.weight * 1e9 + flops), bytes_accessed=moved, transcendentals=0
        ),
    )(*inputs)


def keep_in_hbm(pairs, sems):
    copies = [
        pltpu.make_async_copy(source, kept, sems.at[index])
        for index, (source, kept) in enumerate(pairs)
    ]
    for copy in copies:
        copy.start()
    return copies


def dot_nn(left, right):
    return lax.dot_general(left, right, (((1,), (0,)), ((), ())), preferred_element_type=f32)


def dot_nt(left, right):
    return lax.dot_general(left, right, (((1,), (1,)), ((), ())), preferred_element_type=f32)


def dot_tn(left, right):
    return lax.dot_general(left, right, (((0,), (0,)), ((), ())), preferred_element_type=f32)


def row_stats(inputs):
    average = jnp.mean(inputs, axis=-1, keepdims=True)
    centered = inputs - average
    variance = jnp.mean(centered * centered, axis=-1, keepdims=True)
    return centered, lax.rsqrt(variance + norm_eps)


def add_parts(got_ref):
    total = got_ref[0].astype(f32)
    for part in range(1, got_ref.shape[0]):
        total += got_ref[part].astype(f32)
    return total


def residual_norm(got, residual, bias, bias_layer, gain, shift, norm_layer):
    parts, rows, width = got.shape

    def kernel(got_ref, residual_ref, bias_ref, gain_ref, shift_ref, out_ref, spread_ref):
        total = residual_ref[...] + add_parts(got_ref) + bias_ref[bias_layer : bias_layer + 1, :]
        out_ref[...] = total
        layer = slice(norm_layer, norm_layer + 1)
        centered, inverse = row_stats(total)
        normed = (centered * inverse * gain_ref[layer, :] + shift_ref[layer, :]).astype(bf16)
        for part in range(parts):
            spread_ref[part] = normed

    inputs = [got, residual, bias, gain, shift]
    outputs = [((rows, width), f32, pltpu.HBM), ((parts, rows, width), bf16)]
    return run_kernel(kernel, inputs, [plain(item) for item in inputs], outputs)


def norm_backward(got, inputs, gain, layer, grad, extra=None, bias=None):
    parts, rows, width = got.shape
    if bias is not None:
        rows //= 2
    more = 0 if extra is None else 128
    spread_rows = rows if bias is None else 2 * rows

    def kernel(got_ref, inputs_ref, gain_ref, grad_ref, *refs):
        out_ref, spread_ref, small_ref = refs[-3:]
        total = add_parts(got_ref)
        into = total[:rows]
        if bias is not None:
            output = inputs_ref[...] + total[rows:] + refs[0][layer : layer + 1, :]
            output = output.astype(bf16)
        centered, inverse = row_stats(inputs_ref[...])
        unit = centered * inverse
        scaled = into * gain_ref[layer : layer + 1, :]
        first = jnp.mean(scaled, axis=-1, keepdims=True)
        second = jnp.mean(scaled * unit, axis=-1, keepdims=True)
        total = grad_ref[...] + (scaled - first - unit * second) * inverse
        out_ref[...] = total
        rounded = total.astype(bf16)
        for part in range(parts):
            spread_ref[part, :rows, :width] = rounded
            if bias is not None:
                spread_ref[part, rows:, :] = output
        if more:
            small = jnp.zeros((8, 128), f32)
            for chip in range(extra.shape[0]):
                piece = refs[0][chip, -16:, :128].astype(f32)
                small += piece[:8] + piece[8:]
            high = small.astype(bf16).astype(f32)
            zero = jnp.zeros((rows - 16, 128), f32)
            both = jnp.concatenate([high, small - high, zero], axis=0).astype(bf16)
            for part in range(parts):
                spread_ref[part, :, width:] = both
        small_ref[0:1, :] = jnp.sum(into * unit, axis=0, keepdims=True)
        small_ref[1:2, :] = jnp.sum(into, axis=0, keepdims=True)
        small_ref[2:3, :] = jnp.sum(rounded.astype(f32), axis=0, keepdims=True)
        small_ref[3:, :] = jnp.zeros((5, width), f32)

    inputs = [got, inputs, gain, grad] + [item for item in (extra, bias) if item is not None]
    outputs = [
        ((rows, width), f32, pltpu.HBM),
        ((parts, spread_rows, width + more), bf16),
        ((8, width), f32, pltpu.HBM),
    ]
    return run_kernel(kernel, inputs, [plain(item) for item in inputs], outputs)


class Places:
    def __init__(self, owner_ref, lengths_ref, rows):
        self.owner_ref, self.rows = owner_ref, rows
        self.device = lax.axis_index("dp")
        self.core = lax.rem(self.device, 2)
        self.own = owner_ref[self.device] * rows
        self.ends = []
        for scene in range(lengths_ref.shape[0]):
            before = self.ends[-1] if self.ends else 0
            self.ends.append(before + lengths_ref[scene])

    def device_of(self, index, same_core):
        return 2 * index + (self.core if same_core else 1 - self.core)

    def start(self, index, same_core):
        return self.owner_ref[self.device_of(index, same_core)] * self.rows

    def label(self, position):
        return sum((position >= end).astype(jnp.int32) for end in self.ends)

    def scalar_label(self, position):
        return sum(jnp.where(position >= end, 1, 0).astype(jnp.int32) for end in self.ends)

    def over_blocks(self, count, same_core, step):
        last = self.rows - 1
        own_first, own_last = self.scalar_label(self.own), self.scalar_label(self.own + last)
        own_alone = own_first == own_last

        def one(index, carry):
            start = self.start(index, same_core)
            first, end = self.scalar_label(start), self.scalar_label(start + last)
            meets = jnp.logical_and(first <= own_last, own_first <= end)
            uniform = first == end
            plain_kind = jnp.logical_and(uniform, own_alone)
            scene_kind = jnp.logical_and(uniform, jnp.logical_not(own_alone))
            for kind, flag in (
                ("plain", plain_kind),
                ("scene", scene_kind),
                ("mixed", jnp.logical_not(uniform)),
            ):

                @pl.when(jnp.logical_and(meets, flag))
                def _(kind=kind):
                    step(index, start, kind, first)

            return carry

        lax.fori_loop(0, count, one, 0)


def scalars():
    return [whole(pltpu.SMEM), whole(pltpu.SMEM)]


def head_stack(rows):
    lane = lax.broadcasted_iota(jnp.int32, rows.shape, 1)
    half = rows.shape[1] // 2
    zero = jnp.zeros_like(rows)
    return jnp.concatenate(
        [jnp.where(lane < half, rows, zero), jnp.where(lane >= half, rows, zero)], axis=0
    )


def heads_from_lanes(stacked):
    half, rows = stacked.shape[0] // 2, stacked.shape[1] // 2
    return jnp.concatenate([stacked[:half, :rows], stacked[half:, rows:]], axis=0)


def heads_from_rows(stacked):
    rows = stacked.shape[0] // 2
    lane = lax.broadcasted_iota(jnp.int32, (rows, stacked.shape[1]), 1)
    return jnp.where(lane < stacked.shape[1] // 2, stacked[:rows], stacked[rows:])


def row_pieces(vector, count):
    pieces = []
    rest = vector
    for piece in range(count):
        term = rest.astype(bf16).astype(f32)
        rest = rest - term
        pieces += [term[:, start : start + 128] for start in range(0, vector.shape[1], 128)]
    row = lax.broadcasted_iota(jnp.int32, (16, 128), 0)
    tile = jnp.zeros((16, 128), f32)
    for index, piece in enumerate(pieces):
        tile = jnp.where(row == index, jnp.broadcast_to(piece, (16, 128)), tile)
    return tile.astype(bf16)


def rows_back(tile, count, length):
    tile = tile.astype(f32)
    lines = length // 128
    out = []
    for line in range(lines):
        total = tile[line : line + 1]
        for piece in range(1, count):
            total = total + tile[piece * lines + line : piece * lines + line + 1]
        out.append(total)
    return jnp.concatenate(out, axis=1)


def attention_blocks(query_ref, block_ref, places, same_core, stack_ref, peak_ref, total_ref, sum_ref):
    rows, local = query_ref.shape
    scale = 1.0 / math.sqrt(local // 2)
    scaled = (query_ref[...].astype(f32) * scale).astype(bf16)
    stack_ref[...] = head_stack(scaled)
    lanes = lax.broadcasted_iota(jnp.int32, (1, 2 * rows), 1)
    own_label = places.label(places.own + jnp.where(lanes >= rows, lanes - rows, lanes))

    def step(index, start, kind, scene):
        keys = block_ref[index, :, :local]
        values = block_ref[index, :, local:]
        scores = dot_nt(keys, stack_ref[...])
        if kind == "mixed":
            label = places.label(start + lax.broadcasted_iota(jnp.int32, (rows, 128), 0))
            label = jnp.concatenate([label] * (2 * rows // 128), axis=1)
            scores = jnp.where(label == own_label, scores, absent)
        old = peak_ref[...]
        highest = jnp.max(scores, axis=0, keepdims=True)
        if kind == "scene":
            highest = jnp.where(own_label == scene, highest, absent)
        new = jnp.maximum(old, highest)
        taken = jnp.where(own_label == scene, new, -absent) if kind == "scene" else new
        weight = jnp.exp(scores - taken)
        fade = jnp.exp(old - new)
        peak_ref[...] = new
        total_ref[...] = total_ref[...] * fade + jnp.sum(weight, axis=0, keepdims=True)
        sum_ref[...] = sum_ref[...] * fade + dot_tn(values, weight.astype(bf16))

    places.over_blocks(block_ref.shape[0], same_core, step)
    return scaled


def attention_begin(query, mine, owner, lengths):
    rows, local = query.shape

    def kernel(
        owner_ref,
        lengths_ref,
        query_ref,
        mine_ref,
        peak_ref,
        total_ref,
        sum_ref,
        kept_ref,
        stack_ref,
        sems,
    ):
        copies = keep_in_hbm([(mine_ref, kept_ref)], sems)
        places = Places(owner_ref, lengths_ref, rows)
        peak_ref[...] = jnp.full(peak_ref.shape, 0.1 * absent, f32)
        total_ref[...] = jnp.zeros(total_ref.shape, f32)
        sum_ref[...] = jnp.zeros(sum_ref.shape, f32)
        attention_blocks(
            query_ref, mine_ref, places, True, stack_ref, peak_ref, total_ref, sum_ref
        )
        copies[0].wait()

    return run_kernel(
        kernel,
        [owner, lengths, query, mine],
        scalars() + [plain(query), plain(mine)],
        [
            ((1, 2 * rows), f32),
            ((1, 2 * rows), f32),
            ((local, 2 * rows), f32),
            (mine.shape, bf16, pltpu.HBM, True),
        ],
        flops=32 * rows * mine.shape[0] * rows * local,
        limit=16,
        scratch=[pltpu.VMEM((2 * rows, local), bf16), pltpu.SemaphoreType.DMA((1,))],
    )


def attention_end(query, theirs, state, out_weight, layer, owner, lengths):
    rows, local = query.shape
    width = out_weight.shape[2]
    mp_count = lax.axis_size("mp")

    def kernel(
        owner_ref,
        lengths_ref,
        query_ref,
        theirs_ref,
        old_peak_ref,
        old_total_ref,
        old_sum_ref,
        weight_ref,
        part_ref,
        low_ref,
        flat_ref,
        log_ref,
        message_ref,
        kept_ref,
        stack_ref,
        peak_ref,
        total_ref,
        sum_ref,
        sems,
    ):
        copies = keep_in_hbm([(theirs_ref, kept_ref)], sems)
        places = Places(owner_ref, lengths_ref, rows)
        peak_ref[...] = old_peak_ref[...]
        total_ref[...] = old_total_ref[...]
        sum_ref[...] = old_sum_ref[...]
        scaled = attention_blocks(
            query_ref, theirs_ref, places, False, stack_ref, peak_ref, total_ref, sum_ref
        )
        attended = heads_from_lanes(sum_ref[...] / total_ref[...])
        flat_ref[...] = attended
        low = attended.T.astype(bf16)
        low_ref[...] = low
        part = dot_nn(low, weight_ref[0]).astype(bf16)
        part_ref[...] = part.reshape(part_ref.shape)
        log_total = peak_ref[...] + jnp.log(total_ref[...])
        log_ref[...] = log_total
        message_ref[:rows, :] = scaled
        message_ref[rows:, :] = row_pieces(log_total, 3)
        copies[0].wait()

    inputs = [owner, lengths, query, theirs] + list(state) + [out_weight]
    return run_kernel(
        kernel,
        inputs,
        scalars() + [plain(item) for item in inputs[2:7]] + [of_layer(out_weight, layer)],
        [
            ((mp_count, rows // mp_count, width), bf16),
            ((rows, local), bf16, pltpu.HBM),
            ((local, rows), f32, pltpu.HBM),
            ((1, 2 * rows), f32, pltpu.HBM),
            ((rows + 16, local), bf16, pltpu.HBM),
            (theirs.shape, bf16, pltpu.HBM, True),
        ],
        flops=32 * rows * theirs.shape[0] * rows * local,
        limit=16,
        scratch=[
            pltpu.VMEM((2 * rows, local), bf16),
            pltpu.VMEM((1, 2 * rows), f32),
            pltpu.VMEM((1, 2 * rows), f32),
            pltpu.VMEM((local, 2 * rows), f32),
            pltpu.SemaphoreType.DMA((1,)),
        ],
    )


def grad_attended(branch, out_weight, layer, flat):
    parts, part_rows, width = branch.shape
    ridden = 0 if parts * part_rows == flat.shape[1] else 1
    part_rows //= 1 + ridden
    rows = parts * part_rows
    local = out_weight.shape[1]

    chips = lax.axis_size("dp") // 2

    def kernel(branch_ref, weight_ref, flat_ref, spread_ref, message_ref, delta_ref, *refs):
        kept_refs, sems = refs[:-1], refs[-1]
        copies = keep_in_hbm(
            [
                (branch_ref.at[:, pl.ds(index * part_rows, part_rows)], kept_ref)
                for index, kept_ref in enumerate(kept_refs)
            ],
            sems,
        )
        own = branch_ref[:, :part_rows, :].reshape(rows, width)
        grad = dot_nt(own, weight_ref[0]).astype(bf16)
        product = grad.astype(f32).T * flat_ref[...]
        half = local // 2
        delta = jnp.concatenate(
            [
                jnp.sum(product[:half], axis=0, keepdims=True),
                jnp.sum(product[half:], axis=0, keepdims=True),
            ],
            axis=1,
        )
        delta_ref[...] = delta
        pieces = row_pieces(delta, 3)
        message_ref[...] = grad
        for chip in range(chips):
            spread_ref[chip, :rows, :] = grad
            spread_ref[chip, rows:, :] = pieces
        for copy in copies:
            copy.wait()

    inputs = [branch, far(out_weight), far(flat)]
    return run_kernel(
        kernel,
        inputs,
        [plain(branch), of_layer(out_weight, layer), plain(flat)],
        [
            ((chips, rows + 16, local), bf16),
            ((rows, local), bf16),
            ((1, 2 * rows), f32),
        ]
        + [((parts, part_rows, width), bf16, pltpu.HBM, True)] * (1 + ridden),
        flops=2 * rows * local * width,
        scratch=[pltpu.SemaphoreType.DMA((1 + ridden,))],
    )


def query_side(message, log_total, delta, mine, theirs, grad, owner, lengths):
    rows, local = grad.shape
    half = mine.shape[0]
    count = 2 * half
    scale = 1.0 / math.sqrt(local // 2)

    def kernel(
        owner_ref,
        lengths_ref,
        query_ref,
        log_ref,
        delta_ref,
        mine_ref,
        theirs_ref,
        grad_ref,
        out_ref,
        stack_ref,
        grad_stack_ref,
        sum_ref,
    ):
        places = Places(owner_ref, lengths_ref, rows)
        stack_ref[...] = head_stack(query_ref[:rows, :])
        grad_stack_ref[...] = head_stack(grad_ref[...])
        sum_ref[...] = jnp.zeros(sum_ref.shape, f32)
        lanes = lax.broadcasted_iota(jnp.int32, (1, 2 * rows), 1)
        own_label = places.label(places.own + jnp.where(lanes >= rows, lanes - rows, lanes))

        def step(block_ref, index, start, kind, scene):
            keys = block_ref[index, :, :local]
            values = block_ref[index, :, local:]
            taken = log_ref[...]
            if kind == "scene":
                taken = jnp.where(own_label == scene, taken, -absent)
            scores = dot_nt(keys, stack_ref[...]) - taken
            if kind == "mixed":
                label = places.label(start + lax.broadcasted_iota(jnp.int32, (rows, 128), 0))
                label = jnp.concatenate([label] * (2 * rows // 128), axis=1)
                scores = jnp.where(label == own_label, scores, absent)
            probs = jnp.exp(scores)
            grad_probs = dot_nt(values, grad_stack_ref[...])
            grad_scores = (probs * (grad_probs - delta_ref[...])).astype(bf16)
            sum_ref[...] += dot_tn(keys, grad_scores)

        places.over_blocks(half, True, functools.partial(step, mine_ref))
        places.over_blocks(half, False, functools.partial(step, theirs_ref))
        out_ref[...] = (heads_from_lanes(sum_ref[...]) * scale).T.astype(bf16)

    inputs = [owner, lengths, far(message), far(log_total), delta, far(mine), far(theirs), grad]
    return run_kernel(
        kernel,
        inputs,
        scalars() + [plain(item) for item in inputs[2:]],
        [((rows, local), bf16)],
        flops=64 * rows * count * rows * local,
        limit=16,
        scratch=[
            pltpu.VMEM((2 * rows, local), bf16),
            pltpu.VMEM((2 * rows, local), bf16),
            pltpu.VMEM((local, 2 * rows), f32),
        ],
    )[0]


def key_blocks(own_ref, queries_ref, block_ref, places, same_core, refs):
    keys_ref, values_ref, key_sum_ref, value_sum_ref = refs
    rows, local = own_ref.shape[0], own_ref.shape[1] // 2
    keys_ref[...] = head_stack(own_ref[:, :local])
    values_ref[...] = head_stack(own_ref[:, local:])
    own_label = places.label(places.own + lax.broadcasted_iota(jnp.int32, (rows, 128), 0))
    own_label = jnp.concatenate([own_label] * (rows // 128), axis=1)
    own_label = jnp.concatenate([own_label] * 2, axis=0)

    def spread(row):
        return jnp.concatenate(
            [
                jnp.broadcast_to(row[:, :rows], (rows, rows)),
                jnp.broadcast_to(row[:, rows:], (rows, rows)),
            ],
            axis=0,
        )

    def step(index, start, kind, scene):
        source = places.device_of(index, same_core)
        query = queries_ref[source, :rows, :]
        grad = block_ref[index, :rows, :]
        log_total = rows_back(queries_ref[source, rows:, :], 3, 2 * rows)
        delta = rows_back(block_ref[index, rows:, :], 3, 2 * rows)
        scores = dot_nt(keys_ref[...], query) - spread(log_total)
        if kind == "mixed":
            lanes = start + lax.broadcasted_iota(jnp.int32, (1, rows), 1)
            scores = jnp.where(own_label == places.label(lanes), scores, absent)
        probs = jnp.exp(scores)
        grad_probs = dot_nt(values_ref[...], grad)
        grad_scores = (probs * (grad_probs - spread(delta))).astype(bf16)
        value_part = dot_nn(probs.astype(bf16), grad)
        key_part = dot_nn(grad_scores, query)
        if kind == "scene":
            same = own_label[:, :local] == scene
            value_part = jnp.where(same, value_part, 0.0)
            key_part = jnp.where(same, key_part, 0.0)
        value_sum_ref[...] += value_part
        key_sum_ref[...] += key_part

    places.over_blocks(block_ref.shape[0], same_core, step)


def key_begin(queries, mine, key_value, owner, lengths):
    rows, local = key_value.shape[0], key_value.shape[1] // 2

    def kernel(
        owner_ref,
        lengths_ref,
        queries_ref,
        mine_ref,
        own_ref,
        key_sum_ref,
        value_sum_ref,
        keys_ref,
        values_ref,
    ):
        places = Places(owner_ref, lengths_ref, rows)
        key_sum_ref[...] = jnp.zeros(key_sum_ref.shape, f32)
        value_sum_ref[...] = jnp.zeros(value_sum_ref.shape, f32)
        refs = keys_ref, values_ref, key_sum_ref, value_sum_ref
        key_blocks(own_ref, queries_ref, mine_ref, places, True, refs)

    inputs = [owner, lengths, far(queries), mine, far(key_value)]
    return run_kernel(
        kernel,
        inputs,
        scalars() + [plain(item) for item in inputs[2:]],
        [((2 * rows, local), f32), ((2 * rows, local), f32)],
        flops=64 * rows * mine.shape[0] * rows * local,
        limit=16,
        scratch=[pltpu.VMEM((2 * rows, local), bf16), pltpu.VMEM((2 * rows, local), bf16)],
    )


def key_end(
    queries, theirs, key_value, sums, query_grad, qkv, layer, owner, lengths, unit
):
    rows, local = key_value.shape[0], key_value.shape[1] // 2
    width = qkv.shape[2]
    mp_count = lax.axis_size("mp")
    with_unit = unit is not None

    def kernel(
        owner_ref,
        lengths_ref,
        queries_ref,
        theirs_ref,
        own_ref,
        old_key_ref,
        old_value_ref,
        grad_ref,
        weight_ref,
        *refs,
    ):
        places = Places(owner_ref, lengths_ref, rows)
        if with_unit:
            unit_ref, refs = refs[0], refs[1:]
        part_ref, proj_ref, bias_ref, small_ref = refs[:4]
        keys_ref, values_ref, key_sum_ref, value_sum_ref = refs[4:]
        key_sum_ref[...] = old_key_ref[...]
        value_sum_ref[...] = old_value_ref[...]
        key_blocks(own_ref, queries_ref, theirs_ref, places, False, refs[4:])
        key_grad = heads_from_rows(key_sum_ref[...]).astype(bf16)
        value_grad = heads_from_rows(value_sum_ref[...]).astype(bf16)
        query_grad = grad_ref[...]
        proj_ref[:, :local] = query_grad
        proj_ref[:, local : 2 * local] = key_grad
        proj_ref[:, 2 * local :] = value_grad
        bias_ref[...] = jnp.zeros(bias_ref.shape, f32)
        bias_ref[0:1, :] = jnp.sum(query_grad.astype(f32), axis=0, keepdims=True)
        bias_ref[1:2, :] = jnp.sum(value_grad.astype(f32), axis=0, keepdims=True)
        part = dot_nt(query_grad, weight_ref[0, 0])
        part += dot_nt(key_grad, weight_ref[0, 1])
        part += dot_nt(value_grad, weight_ref[0, 2])
        low = part.astype(bf16)
        part_ref[...] = low.reshape(part_ref.shape)
        small_ref[...] = jnp.zeros(small_ref.shape, f32)
        if with_unit:
            into = low.astype(f32)
            small_ref[0:1, :] = jnp.sum(into * unit_ref[...], axis=0, keepdims=True)
            small_ref[1:2, :] = jnp.sum(into, axis=0, keepdims=True)

    inputs = [owner, lengths, far(queries), theirs, far(key_value)] + list(sums)
    inputs += [query_grad, far(qkv)]
    in_specs = scalars() + [plain(item) for item in inputs[2:8]] + [of_layer(qkv, layer)]
    if with_unit:
        inputs.append(far(unit))
        in_specs.append(plain(unit))
    return run_kernel(
        kernel,
        inputs,
        in_specs,
        [
            ((mp_count, rows // mp_count, width), bf16),
            ((rows, 3 * local), bf16, pltpu.HBM),
            ((8, local), f32, pltpu.HBM),
            ((8, width), f32, pltpu.HBM),
        ],
        flops=64 * rows * theirs.shape[0] * rows * local,
        limit=18,
        scratch=[
            pltpu.VMEM((2 * rows, local), bf16),
            pltpu.VMEM((2 * rows, local), bf16),
            pltpu.VMEM((2 * rows, local), f32),
            pltpu.VMEM((2 * rows, local), f32),
        ],
    )


def project(normed, qkv, bias, layer, first=None):
    rows, width = normed.shape
    local = qkv.shape[3]
    chips = lax.axis_size("dp") // 2
    own_rows = rows // lax.axis_size("mp")

    def kernel(normed_ref, weight_ref, bias_ref, *refs):
        if first is None:
            query_ref, pair_ref, spread_ref, kept_ref, sems = refs
            copies = keep_in_hbm([(normed_ref, kept_ref)], sems)
            normed = normed_ref[...]
        else:
            gain_ref, shift_ref, query_ref, pair_ref, spread_ref = refs[:5]
            own_ref, low_ref, unit_ref = refs[5:]
            centered, inverse = row_stats(normed_ref[...])
            unit = centered * inverse
            unit_ref[...] = unit
            normed = (unit * gain_ref[0:1, :] + shift_ref[0:1, :]).astype(bf16)
            low_ref[...] = normed
            own = pl.multiple_of(lax.axis_index("mp") * own_rows, own_rows)
            own_ref[...] = normed_ref[pl.ds(own, own_rows), :]
        query_bias, value_bias = (
            jnp.concatenate([bias_ref[0, at, 0:1, :], bias_ref[0, at, 1:2, :]], axis=1)
            for at in range(2)
        )
        query = dot_nn(normed, weight_ref[0, 0]) + query_bias
        query_ref[...] = query.astype(bf16)
        keys = dot_nn(normed, weight_ref[0, 1]).astype(bf16)
        values = (dot_nn(normed, weight_ref[0, 2]) + value_bias).astype(bf16)
        pair_ref[:, :local] = keys
        pair_ref[:, local:] = values
        for chip in range(chips):
            spread_ref[chip, :, :local] = keys
            spread_ref[chip, :, local:] = values
        if first is None:
            copies[0].wait()

    inputs = [normed, qkv, bias] if first is None else [far(normed), far(qkv), far(bias)]
    in_specs = [plain(normed), of_layer(qkv, layer), of_layer(bias, layer)]
    outputs = [
        ((rows, local), bf16),
        ((rows, 2 * local), bf16, pltpu.HBM),
        ((chips, rows, 2 * local), bf16),
    ]
    scratch = []
    if first is None:
        outputs.append((normed.shape, bf16, pltpu.HBM, True))
        scratch.append(pltpu.SemaphoreType.DMA((1,)))
    else:
        inputs += [far(item) for item in first]
        in_specs += [plain(item) for item in first]
        outputs += [
            ((own_rows, width), f32, pltpu.HBM),
            ((rows, width), bf16, pltpu.HBM),
            ((rows, width), f32, pltpu.HBM),
        ]
    return run_kernel(
        kernel, inputs, in_specs, outputs, flops=6 * rows * width * local, scratch=scratch
    )


def mlp_forward(normed, inner, inner_bias, down, layer):
    parts, part_rows, width = normed.shape
    rows, units = parts * part_rows, inner.shape[2]

    def kernel(
        normed_ref,
        inner_ref,
        bias_ref,
        down_ref,
        before_ref,
        active_ref,
        part_ref,
        kept_ref,
        sems,
    ):
        copies = keep_in_hbm([(normed_ref, kept_ref)], sems)
        own = normed_ref[...].reshape(rows, width)
        before = dot_nn(own, inner_ref[0]) + bias_ref[layer : layer + 1, :]
        before_ref[...] = before
        active = gelu(before).astype(bf16)
        active_ref[...] = active
        part_ref[...] = dot_nn(active, down_ref[0]).astype(bf16).reshape(part_ref.shape)
        copies[0].wait()

    inputs = [normed, far(inner), inner_bias, far(down)]
    return run_kernel(
        kernel,
        inputs,
        [plain(normed), of_layer(inner, layer), plain(inner_bias), of_layer(down, layer)],
        [
            ((rows, units), f32, pltpu.HBM),
            ((rows, units), bf16, pltpu.HBM),
            ((parts, part_rows, width), bf16),
            (normed.shape, bf16, pltpu.HBM, True),
        ],
        flops=4 * rows * width * units,
        scratch=[pltpu.SemaphoreType.DMA((1,))],
    )


def gelu(before):
    return 0.5 * before * (1.0 + lax.erf(before * math.sqrt(0.5)))


def gelu_slope(before):
    slope = 0.5 * (1.0 + lax.erf(before * math.sqrt(0.5)))
    return slope + before * jnp.exp(-0.5 * before * before) * (1.0 / math.sqrt(2.0 * math.pi))


def mlp_last(normed, cotangent, inner, inner_bias, down):
    parts, part_rows, width = normed.shape
    layer = inner.shape[0] - 1
    rows, units = parts * part_rows, inner.shape[2]

    def kernel(
        normed_ref,
        cotangent_ref,
        inner_ref,
        inner_bias_ref,
        down_ref,
        active_ref,
        out_ref,
        bias_ref,
        part_ref,
        own_ref,
        full_ref,
        kept_ref,
        sems,
    ):
        copies = keep_in_hbm([(normed_ref, kept_ref)], sems)
        grad = cotangent_ref[...].astype(bf16)
        full_ref[...] = grad.reshape(full_ref.shape)
        own = pl.multiple_of(lax.axis_index("mp") * part_rows, part_rows)
        own_ref[...] = cotangent_ref[pl.ds(own, part_rows), :]
        before = dot_nn(normed_ref[...].reshape(rows, width), inner_ref[0])
        before += inner_bias_ref[layer : layer + 1, :]
        out = (dot_nt(grad, down_ref[0]) * gelu_slope(before)).astype(bf16)
        out_ref[...] = out
        bias_ref[...] = jnp.broadcast_to(
            jnp.sum(out.astype(f32), axis=0, keepdims=True), bias_ref.shape
        )
        part = dot_nt(out, inner_ref[0]).astype(bf16)
        part_ref[:, :part_rows, :] = part.reshape(parts, part_rows, width)
        active = gelu(before).astype(bf16)
        active_ref[...] = active
        part = dot_nn(active, down_ref[0]).astype(bf16)
        part_ref[:, part_rows:, :] = part.reshape(parts, part_rows, width)
        copies[0].wait()

    inputs = [normed, far(cotangent), far(inner), inner_bias, far(down)]
    return run_kernel(
        kernel,
        inputs,
        [
            plain(normed),
            plain(cotangent),
            of_layer(inner, layer),
            plain(inner_bias),
            of_layer(down, layer),
        ],
        [
            ((rows, units), bf16, pltpu.HBM),
            ((rows, units), bf16, pltpu.HBM),
            ((8, units), f32, pltpu.HBM),
            ((parts, 2 * part_rows, width), bf16),
            ((part_rows, width), f32, pltpu.HBM),
            ((parts, part_rows, width), bf16, pltpu.HBM),
            (normed.shape, bf16, pltpu.HBM, True),
        ],
        flops=8 * rows * width * units,
        scratch=[pltpu.SemaphoreType.DMA((1,))],
    )


def mlp_backward(grad, before, inner, down, layer):
    parts, part_rows, width = grad.shape
    rows, units = parts * part_rows, inner.shape[2]

    def kernel(
        grad_ref, before_ref, inner_ref, down_ref, out_ref, bias_ref, part_ref, kept_ref, sems
    ):
        copies = keep_in_hbm([(grad_ref, kept_ref)], sems)
        into = dot_nt(grad_ref[...].reshape(rows, width), down_ref[0])
        out = (into * gelu_slope(before_ref[...])).astype(bf16)
        out_ref[...] = out
        bias_ref[...] = jnp.broadcast_to(
            jnp.sum(out.astype(f32), axis=0, keepdims=True), bias_ref.shape
        )
        part_ref[...] = dot_nt(out, inner_ref[0]).astype(bf16).reshape(part_ref.shape)
        copies[0].wait()

    inputs = [grad, before, inner, down]
    return run_kernel(
        kernel,
        inputs,
        [plain(grad), plain(before), of_layer(inner, layer), of_layer(down, layer)],
        [
            ((rows, units), bf16, pltpu.HBM),
            ((8, units), f32, pltpu.HBM),
            ((parts, part_rows, width), bf16),
            (grad.shape, bf16, pltpu.HBM, True),
        ],
        flops=4 * rows * width * units,
        scratch=[pltpu.SemaphoreType.DMA((1,))],
    )


def token_products(pairs):
    columns = [right.shape[-1] for left, right in pairs]
    width = pairs[0][0].shape[-1]
    rows = pairs[0][1].shape[0]
    items = [item for pair in pairs for item in pair]
    count = len(items)
    dp_count = lax.axis_size("dp")
    split = (dp_count // 4, 2, 2, width // dp_count)

    def kernel(*refs):
        sources, out_ref, held, parts = refs[:count], refs[count], refs[count + 1 : -2], refs[-2:]
        results, sems = held[count:], parts[0]
        out_sems = parts[1]
        copies = keep_in_hbm(zip(sources, held[:count]), sems)
        writes = []
        at = 0
        for index, size in enumerate(columns):
            copies[2 * index].wait()
            copies[2 * index + 1].wait()
            left = held[2 * index][...].reshape(rows, width)
            result = dot_tn(left, held[2 * index + 1][...]).astype(bf16)
            results[index][...] = result.reshape(split + (size,))
            for x in range(2):
                for core in range(2):
                    write = pltpu.make_async_copy(
                        results[index].at[:, x, core],
                        out_ref.at[:, core, x, :, pl.ds(at, size)],
                        out_sems.at[4 * index + 2 * x + core],
                    )
                    write.start()
                    writes.append(write)
            at += size
        for write in writes:
            write.wait()

    return run_kernel(
        kernel,
        [far(item) for item in items],
        [whole(pltpu.HBM)] * count,
        [(split + (sum(columns),), bf16, pltpu.HBM, True)],
        flops=2 * rows * width * sum(columns),
        scratch=[pltpu.VMEM(item.shape, item.dtype) for item in items]
        + [pltpu.VMEM(split + (size,), bf16) for size in columns]
        + [pltpu.SemaphoreType.DMA((count,)), pltpu.SemaphoreType.DMA((4 * len(pairs),))],
    )[0].reshape(width, sum(columns))


def last_products(pairs, norm_one, norm_two, key_small, own_cotangent, proj_bias, inner_bias):
    width = own_cotangent.shape[1]
    dp_count = lax.axis_size("dp")
    columns = width // dp_count
    token_rows = pairs[0][1].shape[0]
    total = sum(right.shape[-1] for left, right in pairs)
    items = [item for pair in pairs for item in pair]
    inputs = items + [norm_one, norm_two[0], norm_two[1], key_small, own_cotangent]
    inputs = [far(item) for item in inputs + proj_bias + inner_bias]

    def kernel(*refs):
        item_refs, refs = refs[: len(items)], refs[len(items) :]
        one_ref, two_a_ref, two_b_ref, key_ref, grad_ref = refs[:5]
        proj_refs, inner_refs = refs[5:7], refs[7:9]
        mine_ref, away_ref, first_ref, second_ref, product_ref = refs[9:]
        at = 0
        for left_ref, right_ref in zip(item_refs[0::2], item_refs[1::2]):
            left = left_ref[...].reshape(token_rows, width)
            size = right_ref.shape[-1]
            product_ref[:, at : at + size] = dot_tn(left, right_ref[...]).astype(bf16)
            at += size
        last = jnp.sum(grad_ref[...].astype(bf16).astype(f32), axis=0, keepdims=True)
        zero = jnp.zeros((2, width), f32)
        for target, two_ref, gains, bias in (
            (first_ref, two_a_ref, key_ref, one_ref[2:3, :]),
            (second_ref, two_b_ref, one_ref, last),
        ):
            target[0:2, :] = gains[0:2, :]
            target[2:3, :] = two_ref[2:3, :]
            target[3:5, :] = two_ref[0:2, :]
            target[5:6, :] = bias
            target[6:8, :] = zero
        lines = [proj_refs[layer][row : row + 1, :] for layer in range(2) for row in range(2)]
        for layer in range(2):
            lines += [inner_refs[layer][0:1, 128 * at : 128 * at + 128] for at in range(4)]
        row_index = lax.broadcasted_iota(jnp.int32, (8, 128), 0)
        shared = []
        for group in (lines[:8], lines[8:]):
            tile = jnp.zeros((8, 128), f32)
            for row, line in enumerate(group):
                tile = jnp.where(row_index == row, jnp.broadcast_to(line, (8, 128)), tile)
            shared.append(tile)
        core = lax.rem(lax.axis_index("dp"), 2)
        for device in range(dp_count):
            at = slice(device * columns, (device + 1) * columns)
            small = jnp.concatenate([first_ref[:, at], second_ref[:, at]] + shared, axis=1)
            high = small.astype(bf16).astype(f32)
            tail = jnp.concatenate([high, small - high], axis=0).astype(bf16)
            for flag, ref in ((core == device % 2, mine_ref), (core != device % 2, away_ref)):

                @pl.when(flag)
                def _(ref=ref, tail=tail, device=device, at=at):
                    ref[device // 2, :columns, :] = product_ref[at, :]
                    ref[device // 2, columns:, :] = tail

    shape = ((dp_count // 2, columns + 16, total), bf16)
    return run_kernel(
        kernel,
        inputs,
        [plain(item) for item in inputs],
        [shape, shape],
        flops=2 * token_rows * width * total,
        scratch=[
            pltpu.VMEM((8, width), f32),
            pltpu.VMEM((8, width), f32),
            pltpu.VMEM((width, total), bf16),
        ],
    )


def add_cores(mine, other, columns, output):
    parts, part_rows, width = output.shape

    def kernel(mine_ref, other_ref, low_ref, out_ref, output_ref):
        for chip in range(mine.shape[0]):
            both = mine_ref[chip].astype(f32) + other_ref[chip].astype(f32)
            out_ref[chip, :columns, :] = both[:columns].astype(bf16)
            small = both[columns : columns + 8] + both[columns + 8 :]
            high = small.astype(bf16).astype(f32)
            out_ref[chip, columns:, :] = jnp.concatenate([high, small - high], axis=0).astype(bf16)
        output_ref[...] = low_ref[...].astype(f32).reshape(parts * part_rows, width)

    return run_kernel(
        kernel,
        [mine, other, far(output)],
        [plain(mine), plain(other), plain(output)],
        [(mine.shape, bf16), ((parts * part_rows, width), f32, pltpu.HBM)],
    )


def own_half(pieces):
    shape = pieces.shape[1:]

    def kernel(pieces_ref, mine_ref, away_ref):
        x = lax.rem(lax.div(lax.axis_index("dp"), 2), 2)
        mine_ref[...] = pieces_ref[x]
        away_ref[...] = pieces_ref[1 - x]

    return run_kernel(
        kernel, [far(pieces)], [plain(pieces)], [(shape, bf16, pltpu.HBM), (shape, bf16)]
    )


def scatter_sum(pairs):
    count = lax.axis_size("dp")
    groups = [[4 * z + 2 * x + core for z in range(count // 4) for core in range(2)] for x in range(2)]
    pieces = lax.psum_scatter(
        token_products(pairs), "dp", scatter_dimension=0, tiled=True, axis_index_groups=groups
    )
    mine, away = own_half(pieces.reshape(2, -1, pieces.shape[1]))
    return mine, lax.ppermute(away, "dp", [(index, index ^ 2) for index in range(count)])


def finish_rows(got, width):
    parts, own_rows = got.shape[:2]

    def kernel(got_ref, out_ref, *small_refs):
        total = jnp.zeros((8, 128), f32)
        for part in range(parts):
            at = slice(part * own_rows, (part + 1) * own_rows)
            out_ref[at, :] = got_ref[part, :, :width].astype(f32)
            both = got_ref[part, :16, width:].astype(f32)
            total += both[:8] + both[8:]
        for index, small_ref in enumerate(small_refs):
            small_ref[0:1, :] = total[index : index + 1, :64]
            small_ref[1:2, :] = total[index : index + 1, 64:]

    return run_kernel(
        kernel,
        [got],
        [plain(got)],
        [((parts * own_rows, width), f32, pltpu.HBM)] + [((2, 64), f32, pltpu.HBM)] * 6,
    )


def finish_biases(third, columns):
    bias_columns = columns // lax.axis_size("dp")

    def kernel(third_ref, small_ref):
        small = jnp.zeros((8, third.shape[2]), f32)
        for chip in range(third.shape[0]):
            piece = third_ref[chip, columns:, :].astype(f32)
            small += piece[:8] + piece[8:]
        small = jnp.concatenate([small[:, 128:256], small[:, 256:384]], axis=0)
        lane = lax.broadcasted_iota(jnp.int32, small.shape, 1)
        own = lax.axis_index("dp") * bias_columns
        picked = jnp.zeros(small.shape, f32)
        for half in range(2):
            for column in range(bias_columns):
                at = half * 64 + own + column
                value = jnp.sum(jnp.where(lane == at, small, 0.0), axis=1, keepdims=True)
                picked = jnp.where(lane == half * bias_columns + column, value, picked)
        small_ref[...] = picked

    return run_kernel(kernel, [third], [plain(third)], [((16, 128), f32)])[0]


def finish_weights(first, second, third, local, units):
    columns = first[0].shape[0]

    def kernel(first_ref, first_other_ref, second_ref, second_other_ref, third_ref, qkv_ref, out_ref, inner_ref, down_ref):
        last = add_parts(third_ref)
        middle = first_ref[...].astype(f32) + first_other_ref[...].astype(f32)
        late = second_ref[...].astype(f32) + second_other_ref[...].astype(f32)
        for layer, sums in ((1, middle), (0, late)):
            inner_ref[layer] = sums[:, :units]
            down_ref[layer] = sums[:, units : 2 * units]
            out_ref[layer] = sums[:, 2 * units : 2 * units + local]
        for piece in range(3):
            at = 2 * units + local * (piece + 1)
            qkv_ref[1, piece] = middle[:, at : at + local]
            qkv_ref[0, piece] = last[:columns, local * piece : local * (piece + 1)]

    inputs = list(first) + list(second) + [third]
    return run_kernel(
        kernel,
        inputs,
        [plain(item) for item in inputs],
        [
            ((2, 3, columns, local), f32, pltpu.HBM),
            ((2, columns, local), f32, pltpu.HBM),
            ((2, columns, units), f32, pltpu.HBM),
            ((2, columns, units), f32, pltpu.HBM),
        ],
    )


def body(
    hidden_in,
    cotangent,
    scene_lengths,
    block_owner,
    attn_gain,
    attn_shift,
    qkv_weight,
    qv_bias,
    out_weight,
    out_bias,
    mlp_gain,
    mlp_shift,
    mlp_in_weight,
    mlp_in_bias,
    mlp_out_weight,
    mlp_out_bias,
):
    rows, width = hidden_in.shape
    layers = attn_gain.shape[0]
    local = qv_bias.shape[2] * qv_bias.shape[3]
    units = mlp_in_bias.shape[1]
    dp_count, mp_count = lax.axis_size("dp"), lax.axis_size("mp")
    own_rows = rows // mp_count
    qkv = qkv_weight.transpose(0, 2, 1, 3)
    where = (block_owner, scene_lengths)
    Cost.weight = 0.0

    kept = []
    for layer in range(layers):
        if layer:
            query, pair, spread, normed = project(normed, qkv, qv_bias, layer)
            spread = after(spread, queries)
        else:
            query, pair, spread, hidden, normed, unit = project(
                hidden_in, qkv, qv_bias, layer, (attn_gain, attn_shift)
            )
        mine = gather_chips(spread)
        theirs = from_other_core(mine)
        *state, mine = attention_begin(query, mine, *where)
        part, attended_low, flat, log_total, message, theirs = attention_end(
            query, theirs, state, out_weight, layer, *where
        )
        got = exchange_mp(part)
        queries = lax.all_gather(after(message, got), "dp", axis=0, tiled=True)
        queries = queries.reshape((dp_count,) + message.shape)
        middle, spread = residual_norm(
            got, hidden, out_bias, layer, mlp_gain, mlp_shift, layer
        )
        normed_mlp = exchange_mp(spread)
        if layer + 1 < layers:
            before, active, part, normed_mlp = mlp_forward(
                normed_mlp, mlp_in_weight, mlp_in_bias, mlp_out_weight, layer
            )
        kept.append(
            dict(
                hidden=hidden,
                normed=normed,
                pair=pair,
                mine=mine,
                theirs=theirs,
                attended_low=attended_low,
                flat=flat,
                log_total=log_total,
                message=message,
                queries=queries,
                middle=middle,
                normed_mlp=normed_mlp,
                before=before,
                active=active,
            )
        )
        if layer + 1 < layers:
            hidden, spread = residual_norm(
                exchange_mp(part), middle, mlp_out_bias, layer, attn_gain, attn_shift, layer + 1
            )
            normed = exchange_mp(spread).reshape(rows, width)
    norm_one, norm_two, bias_proj, bias_inner = {}, {}, {}, {}
    for layer in reversed(range(layers)):
        now = kept[layer]
        if layer == layers - 1:
            (
                now["active"],
                grad_before,
                bias_inner[layer],
                part,
                grad_own,
                grad_full,
                now["normed_mlp"],
            ) = mlp_last(now["normed_mlp"], cotangent, mlp_in_weight, mlp_in_bias, mlp_out_weight)
            own_cotangent = grad_own
        else:
            grad_before, bias_inner[layer], part, grad_full = mlp_backward(
                grad_full, now["before"], mlp_in_weight, mlp_out_weight, layer
            )
        mlp_pairs = [(now["normed_mlp"], grad_before), (grad_full, now["active"])]
        middle_grad, spread, norm_two[layer] = norm_backward(
            exchange_mp(part),
            now["middle"],
            mlp_gain,
            layer,
            grad_own,
            bias=mlp_out_bias if layer == layers - 1 else None,
        )
        if layer == layers - 1:
            spread = after(spread, now["queries"])
        spread, grad_rows, delta, branch, *ridden = grad_attended(
            exchange_mp(spread), out_weight, layer, now["flat"]
        )
        if ridden:
            output = ridden[0]
        grad_mine = gather_chips(spread)
        query_grad = query_side(
            now["message"], now["log_total"], delta, now["mine"], now["theirs"], grad_rows, *where
        )
        grad_theirs = from_other_core(after(grad_mine, query_grad))
        sums = key_begin(now["queries"], grad_mine, now["pair"], *where)
        part, proj_grad, bias_proj[layer], key_small = key_end(
            now["queries"],
            grad_theirs,
            now["pair"],
            sums,
            query_grad,
            qkv,
            layer,
            *where,
            unit if layer == 0 else None,
        )
        if layer:
            Cost.weight = 9.5
        out_pairs = [(branch, now["attended_low"])]
        proj_pairs = [(now["normed"], proj_grad)]
        if layer:
            grad_own, spread, norm_one[layer] = norm_backward(
                exchange_mp(part), now["hidden"], attn_gain, layer, middle_grad
            )
            grad_full = exchange_mp(spread)
            first = scatter_sum(mlp_pairs + out_pairs + proj_pairs)
        else:
            second = scatter_sum(mlp_pairs + out_pairs)
            mine, away = last_products(
                proj_pairs,
                norm_one[1],
                norm_two,
                key_small,
                own_cotangent,
                [bias_proj[0], bias_proj[1]],
                [bias_inner[0], bias_inner[1]],
            )
            both, output = add_cores(mine, from_other_core(away), width // dp_count, output)
            third = gather_chips(both)
            ignored, spread, ignored = norm_backward(
                exchange_mp(part), now["hidden"], attn_gain, layer, middle_grad, third
            )
            tail = exchange_mp(after(spread, first[1], second[1]))

    small = finish_biases(third, width // dp_count)
    qkv_grad, out_grad, inner_grad, down_grad = finish_weights(
        first, second, third, local, units
    )
    (
        input_grad,
        gain_one,
        shift_one,
        out_bias_grad,
        gain_two,
        shift_two,
        down_bias_grad,
    ) = finish_rows(tail, width)
    bias_columns = qv_bias.shape[3] // dp_count
    qv_grad = small[:4, : 2 * bias_columns].reshape(layers, 2, 2, bias_columns)
    inner_bias_grad = small[4:12, : 2 * bias_columns].reshape(layers, units // 64, bias_columns)
    return (
        output,
        input_grad,
        gain_one,
        shift_one,
        qkv_grad.transpose(0, 2, 1, 3),
        qv_grad,
        out_grad.transpose(0, 2, 1),
        out_bias_grad,
        gain_two,
        shift_two,
        inner_grad,
        inner_bias_grad,
        down_grad.transpose(0, 2, 1),
        down_bias_grad,
    )


def solution(mesh):
    in_specs = (
        P("dp", None),
        P("dp", None),
        P(),
        P(),
        P(),
        P(),
        P(None, None, None, "mp"),
        P(None, None, "mp", None),
        P(None, "mp", None),
        P(),
        P(),
        P(),
        P(None, None, "mp"),
        P(None, "mp"),
        P(None, "mp", None),
        P(),
    )
    out_specs = (
        P("dp", None),
        P("dp", None),
        P(None, "dp"),
        P(None, "dp"),
        P(None, "dp", None, "mp"),
        P(None, None, "mp", "dp"),
        P(None, "mp", "dp"),
        P(None, "dp"),
        P(None, "dp"),
        P(None, "dp"),
        P(None, "dp", "mp"),
        P(None, "mp", "dp"),
        P(None, "mp", "dp"),
        P(None, "dp"),
    )
    return jax.shard_map(body, mesh=mesh, in_specs=in_specs, out_specs=out_specs, check_vma=False)
```

```python
import functools
import math

import jax
import jax.numpy as jnp
from jax import lax
from jax.experimental import pallas as pl
from jax.experimental.pallas import tpu as pltpu
from jax.sharding import PartitionSpec as P

norm_eps = 1e-05
f32 = jnp.float32
bf16 = jnp.bfloat16
absent = -1e30


class Cost:
    weight = 0.0


def chip_groups(count):
    return [list(range(core, count, 2)) for core in range(2)]


def other_core(count):
    return [(index, index ^ 1) for index in range(count)]


def exchange_mp(spread):
    return lax.all_to_all(spread, "mp", 0, 0, tiled=True)


def gather_chips(spread):
    groups = chip_groups(lax.axis_size("dp"))
    return lax.all_to_all(spread, "dp", 0, 0, tiled=True, axis_index_groups=groups)


def from_other_core(blocks):
    return lax.ppermute(blocks, "dp", other_core(lax.axis_size("dp")))


def after(value, *others):
    return lax.optimization_barrier((value,) + others)[0]


def whole(memory=pltpu.VMEM):
    return pl.BlockSpec(memory_space=memory)


def of_layer(stacked, layer):
    tail = stacked.shape[1:]
    return pl.BlockSpec((1,) + tail, lambda step: (layer,) + (0,) * len(tail))


def plain(array):
    return pl.BlockSpec(array.shape, lambda step: (0,) * len(array.shape))


def far(array):
    return pltpu.with_memory_space_constraint(array, pltpu.HBM)


def run_kernel(kernel, inputs, in_specs, outputs, flops=0, scratch=(), limit=12):
    moved = sum(math.prod(out[0]) * jnp.dtype(out[1]).itemsize for out in outputs)
    moved += sum(item.size * item.dtype.itemsize for item in inputs)
    return pl.pallas_call(
        kernel,
        grid=(1,),
        in_specs=in_specs,
        out_specs=[
            whole(pltpu.HBM)
            if len(out) == 4
            else pl.BlockSpec(out[0], functools.partial(lambda rank, step: (0,) * rank, len(out[0])))
            for out in outputs
        ],
        out_shape=[
            out[2](out[0], out[1]) if len(out) > 2 else jax.ShapeDtypeStruct(out[0], out[1])
            for out in outputs
        ],
        scratch_shapes=list(scratch),
        compiler_params=pltpu.CompilerParams(vmem_limit_bytes=limit * 2**20),
        cost_estimate=pl.CostEstimate(
            flops=int(Cost.weight * 1e9 + flops), bytes_accessed=moved, transcendentals=0
        ),
    )(*inputs)


def keep_in_hbm(pairs, sems):
    copies = [
        pltpu.make_async_copy(source, kept, sems.at[index])
        for index, (source, kept) in enumerate(pairs)
    ]
    for copy in copies:
        copy.start()
    return copies


def dot_nn(left, right):
    return lax.dot_general(left, right, (((1,), (0,)), ((), ())), preferred_element_type=f32)


def dot_nt(left, right):
    return lax.dot_general(left, right, (((1,), (1,)), ((), ())), preferred_element_type=f32)


def dot_tn(left, right):
    return lax.dot_general(left, right, (((0,), (0,)), ((), ())), preferred_element_type=f32)


def row_stats(inputs):
    average = jnp.mean(inputs, axis=-1, keepdims=True)
    centered = inputs - average
    variance = jnp.mean(centered * centered, axis=-1, keepdims=True)
    return centered, lax.rsqrt(variance + norm_eps)


def add_parts(got_ref):
    total = got_ref[0].astype(f32)
    for part in range(1, got_ref.shape[0]):
        total += got_ref[part].astype(f32)
    return total


def residual_norm(got, residual, bias, bias_layer, gain, shift, norm_layer):
    parts, rows, width = got.shape

    def kernel(got_ref, residual_ref, bias_ref, gain_ref, shift_ref, out_ref, spread_ref):
        total = residual_ref[...] + add_parts(got_ref) + bias_ref[bias_layer : bias_layer + 1, :]
        out_ref[...] = total
        layer = slice(norm_layer, norm_layer + 1)
        centered, inverse = row_stats(total)
        normed = (centered * inverse * gain_ref[layer, :] + shift_ref[layer, :]).astype(bf16)
        for part in range(parts):
            spread_ref[part] = normed

    inputs = [got, residual, bias, gain, shift]
    outputs = [((rows, width), f32, pltpu.HBM), ((parts, rows, width), bf16)]
    return run_kernel(kernel, inputs, [plain(item) for item in inputs], outputs)


def norm_backward(got, inputs, gain, layer, grad, extra=None, bias=None):
    parts, rows, width = got.shape
    if bias is not None:
        rows //= 2
    more = 0 if extra is None else 128
    spread_rows = rows if bias is None else 2 * rows

    def kernel(got_ref, inputs_ref, gain_ref, grad_ref, *refs):
        out_ref, spread_ref, small_ref = refs[-3:]
        total = add_parts(got_ref)
        into = total[:rows]
        if bias is not None:
            output = inputs_ref[...] + total[rows:] + refs[0][layer : layer + 1, :]
            output = output.astype(bf16)
        centered, inverse = row_stats(inputs_ref[...])
        unit = centered * inverse
        scaled = into * gain_ref[layer : layer + 1, :]
        first = jnp.mean(scaled, axis=-1, keepdims=True)
        second = jnp.mean(scaled * unit, axis=-1, keepdims=True)
        total = grad_ref[...] + (scaled - first - unit * second) * inverse
        out_ref[...] = total
        rounded = total.astype(bf16)
        for part in range(parts):
            spread_ref[part, :rows, :width] = rounded
            if bias is not None:
                spread_ref[part, rows:, :] = output
        if more:
            small = jnp.zeros((8, 128), f32)
            for chip in range(extra.shape[0]):
                piece = refs[0][chip, -16:, :128].astype(f32)
                small += piece[:8] + piece[8:]
            high = small.astype(bf16).astype(f32)
            zero = jnp.zeros((rows - 16, 128), f32)
            both = jnp.concatenate([high, small - high, zero], axis=0).astype(bf16)
            for part in range(parts):
                spread_ref[part, :, width:] = both
        small_ref[0:1, :] = jnp.sum(into * unit, axis=0, keepdims=True)
        small_ref[1:2, :] = jnp.sum(into, axis=0, keepdims=True)
        small_ref[2:3, :] = jnp.sum(rounded.astype(f32), axis=0, keepdims=True)
        small_ref[3:, :] = jnp.zeros((5, width), f32)

    inputs = [got, inputs, gain, grad] + [item for item in (extra, bias) if item is not None]
    outputs = [
        ((rows, width), f32, pltpu.HBM),
        ((parts, spread_rows, width + more), bf16),
        ((8, width), f32, pltpu.HBM),
    ]
    return run_kernel(kernel, inputs, [plain(item) for item in inputs], outputs)


class Places:
    def __init__(self, owner_ref, lengths_ref, rows):
        self.owner_ref, self.rows = owner_ref, rows
        self.device = lax.axis_index("dp")
        self.core = lax.rem(self.device, 2)
        self.own = owner_ref[self.device] * rows
        self.ends = []
        for scene in range(lengths_ref.shape[0]):
            before = self.ends[-1] if self.ends else 0
            self.ends.append(before + lengths_ref[scene])

    def device_of(self, index, same_core):
        return 2 * index + (self.core if same_core else 1 - self.core)

    def start(self, index, same_core):
        return self.owner_ref[self.device_of(index, same_core)] * self.rows

    def label(self, position):
        return sum((position >= end).astype(jnp.int32) for end in self.ends)

    def scalar_label(self, position):
        return sum(jnp.where(position >= end, 1, 0).astype(jnp.int32) for end in self.ends)

    def over_blocks(self, count, same_core, step):
        last = self.rows - 1
        own_first, own_last = self.scalar_label(self.own), self.scalar_label(self.own + last)
        own_alone = own_first == own_last

        def one(index, carry):
            start = self.start(index, same_core)
            first, end = self.scalar_label(start), self.scalar_label(start + last)
            meets = jnp.logical_and(first <= own_last, own_first <= end)
            uniform = first == end
            plain_kind = jnp.logical_and(uniform, own_alone)
            scene_kind = jnp.logical_and(uniform, jnp.logical_not(own_alone))
            for kind, flag in (
                ("plain", plain_kind),
                ("scene", scene_kind),
                ("mixed", jnp.logical_not(uniform)),
            ):

                @pl.when(jnp.logical_and(meets, flag))
                def _(kind=kind):
                    step(index, start, kind, first)

            return carry

        lax.fori_loop(0, count, one, 0)


def scalars():
    return [whole(pltpu.SMEM), whole(pltpu.SMEM)]


def head_stack(rows):
    lane = lax.broadcasted_iota(jnp.int32, rows.shape, 1)
    half = rows.shape[1] // 2
    zero = jnp.zeros_like(rows)
    return jnp.concatenate(
        [jnp.where(lane < half, rows, zero), jnp.where(lane >= half, rows, zero)], axis=0
    )


def heads_from_lanes(stacked):
    half, rows = stacked.shape[0] // 2, stacked.shape[1] // 2
    return jnp.concatenate([stacked[:half, :rows], stacked[half:, rows:]], axis=0)


def heads_from_rows(stacked):
    rows = stacked.shape[0] // 2
    lane = lax.broadcasted_iota(jnp.int32, (rows, stacked.shape[1]), 1)
    return jnp.where(lane < stacked.shape[1] // 2, stacked[:rows], stacked[rows:])


def row_pieces(vector, count):
    pieces = []
    rest = vector
    for piece in range(count):
        term = rest.astype(bf16).astype(f32)
        rest = rest - term
        pieces += [term[:, start : start + 128] for start in range(0, vector.shape[1], 128)]
    row = lax.broadcasted_iota(jnp.int32, (16, 128), 0)
    tile = jnp.zeros((16, 128), f32)
    for index, piece in enumerate(pieces):
        tile = jnp.where(row == index, jnp.broadcast_to(piece, (16, 128)), tile)
    return tile.astype(bf16)


def rows_back(tile, count, length):
    tile = tile.astype(f32)
    lines = length // 128
    out = []
    for line in range(lines):
        total = tile[line : line + 1]
        for piece in range(1, count):
            total = total + tile[piece * lines + line : piece * lines + line + 1]
        out.append(total)
    return jnp.concatenate(out, axis=1)


def attention_blocks(query_ref, block_ref, places, same_core, stack_ref, peak_ref, total_ref, sum_ref):
    rows, local = query_ref.shape
    scale = 1.0 / math.sqrt(local // 2)
    scaled = (query_ref[...].astype(f32) * scale).astype(bf16)
    stack_ref[...] = head_stack(scaled)
    lanes = lax.broadcasted_iota(jnp.int32, (1, 2 * rows), 1)
    own_label = places.label(places.own + jnp.where(lanes >= rows, lanes - rows, lanes))

    def step(index, start, kind, scene):
        keys = block_ref[index, :, :local]
        values = block_ref[index, :, local:]
        scores = dot_nt(keys, stack_ref[...])
        if kind == "mixed":
            label = places.label(start + lax.broadcasted_iota(jnp.int32, (rows, 128), 0))
            label = jnp.concatenate([label] * (2 * rows // 128), axis=1)
            scores = jnp.where(label == own_label, scores, absent)
        old = peak_ref[...]
        highest = jnp.max(scores, axis=0, keepdims=True)
        if kind == "scene":
            highest = jnp.where(own_label == scene, highest, absent)
        new = jnp.maximum(old, highest)
        taken = jnp.where(own_label == scene, new, -absent) if kind == "scene" else new
        weight = jnp.exp(scores - taken)
        fade = jnp.exp(old - new)
        peak_ref[...] = new
        total_ref[...] = total_ref[...] * fade + jnp.sum(weight, axis=0, keepdims=True)
        sum_ref[...] = sum_ref[...] * fade + dot_tn(values, weight.astype(bf16))

    places.over_blocks(block_ref.shape[0], same_core, step)
    return scaled


def attention_begin(query, mine, owner, lengths):
    rows, local = query.shape

    def kernel(
        owner_ref,
        lengths_ref,
        query_ref,
        mine_ref,
        peak_ref,
        total_ref,
        sum_ref,
        kept_ref,
        stack_ref,
        sems,
    ):
        copies = keep_in_hbm([(mine_ref, kept_ref)], sems)
        places = Places(owner_ref, lengths_ref, rows)
        peak_ref[...] = jnp.full(peak_ref.shape, 0.1 * absent, f32)
        total_ref[...] = jnp.zeros(total_ref.shape, f32)
        sum_ref[...] = jnp.zeros(sum_ref.shape, f32)
        attention_blocks(
            query_ref, mine_ref, places, True, stack_ref, peak_ref, total_ref, sum_ref
        )
        copies[0].wait()

    return run_kernel(
        kernel,
        [owner, lengths, query, mine],
        scalars() + [plain(query), plain(mine)],
        [
            ((1, 2 * rows), f32),
            ((1, 2 * rows), f32),
            ((local, 2 * rows), f32),
            (mine.shape, bf16, pltpu.HBM, True),
        ],
        flops=32 * rows * mine.shape[0] * rows * local,
        limit=16,
        scratch=[pltpu.VMEM((2 * rows, local), bf16), pltpu.SemaphoreType.DMA((1,))],
    )


def attention_end(query, theirs, state, out_weight, layer, owner, lengths):
    rows, local = query.shape
    width = out_weight.shape[2]
    mp_count = lax.axis_size("mp")

    def kernel(
        owner_ref,
        lengths_ref,
        query_ref,
        theirs_ref,
        old_peak_ref,
        old_total_ref,
        old_sum_ref,
        weight_ref,
        part_ref,
        low_ref,
        flat_ref,
        log_ref,
        message_ref,
        kept_ref,
        stack_ref,
        peak_ref,
        total_ref,
        sum_ref,
        sems,
    ):
        copies = keep_in_hbm([(theirs_ref, kept_ref)], sems)
        places = Places(owner_ref, lengths_ref, rows)
        peak_ref[...] = old_peak_ref[...]
        total_ref[...] = old_total_ref[...]
        sum_ref[...] = old_sum_ref[...]
        scaled = attention_blocks(
            query_ref, theirs_ref, places, False, stack_ref, peak_ref, total_ref, sum_ref
        )
        attended = heads_from_lanes(sum_ref[...] / total_ref[...])
        flat_ref[...] = attended
        low = attended.T.astype(bf16)
        low_ref[...] = low
        part = dot_nn(low, weight_ref[0]).astype(bf16)
        part_ref[...] = part.reshape(part_ref.shape)
        log_total = peak_ref[...] + jnp.log(total_ref[...])
        log_ref[...] = log_total
        message_ref[:rows, :] = scaled
        message_ref[rows:, :] = row_pieces(log_total, 3)
        copies[0].wait()

    inputs = [owner, lengths, query, theirs] + list(state) + [out_weight]
    return run_kernel(
        kernel,
        inputs,
        scalars() + [plain(item) for item in inputs[2:7]] + [of_layer(out_weight, layer)],
        [
            ((mp_count, rows // mp_count, width), bf16),
            ((rows, local), bf16, pltpu.HBM),
            ((local, rows), f32, pltpu.HBM),
            ((1, 2 * rows), f32, pltpu.HBM),
            ((rows + 16, local), bf16, pltpu.HBM),
            (theirs.shape, bf16, pltpu.HBM, True),
        ],
        flops=32 * rows * theirs.shape[0] * rows * local,
        limit=16,
        scratch=[
            pltpu.VMEM((2 * rows, local), bf16),
            pltpu.VMEM((1, 2 * rows), f32),
            pltpu.VMEM((1, 2 * rows), f32),
            pltpu.VMEM((local, 2 * rows), f32),
            pltpu.SemaphoreType.DMA((1,)),
        ],
    )


def grad_attended(branch, out_weight, layer, flat):
    parts, part_rows, width = branch.shape
    ridden = 0 if parts * part_rows == flat.shape[1] else 1
    part_rows //= 1 + ridden
    rows = parts * part_rows
    local = out_weight.shape[1]

    chips = lax.axis_size("dp") // 2

    def kernel(branch_ref, weight_ref, flat_ref, spread_ref, message_ref, delta_ref, *refs):
        kept_refs, sems = refs[:-1], refs[-1]
        copies = keep_in_hbm(
            [
                (branch_ref.at[:, pl.ds(index * part_rows, part_rows)], kept_ref)
                for index, kept_ref in enumerate(kept_refs)
            ],
            sems,
        )
        own = branch_ref[:, :part_rows, :].reshape(rows, width)
        grad = dot_nt(own, weight_ref[0]).astype(bf16)
        product = grad.astype(f32).T * flat_ref[...]
        half = local // 2
        delta = jnp.concatenate(
            [
                jnp.sum(product[:half], axis=0, keepdims=True),
                jnp.sum(product[half:], axis=0, keepdims=True),
            ],
            axis=1,
        )
        delta_ref[...] = delta
        pieces = row_pieces(delta, 3)
        message_ref[...] = grad
        for chip in range(chips):
            spread_ref[chip, :rows, :] = grad
            spread_ref[chip, rows:, :] = pieces
        for copy in copies:
            copy.wait()

    inputs = [branch, far(out_weight), far(flat)]
    return run_kernel(
        kernel,
        inputs,
        [plain(branch), of_layer(out_weight, layer), plain(flat)],
        [
            ((chips, rows + 16, local), bf16),
            ((rows, local), bf16),
            ((1, 2 * rows), f32),
        ]
        + [((parts, part_rows, width), bf16, pltpu.HBM, True)] * (1 + ridden),
        flops=2 * rows * local * width,
        scratch=[pltpu.SemaphoreType.DMA((1 + ridden,))],
    )


def query_side(message, log_total, delta, mine, theirs, grad, owner, lengths):
    rows, local = grad.shape
    half = mine.shape[0]
    count = 2 * half
    scale = 1.0 / math.sqrt(local // 2)

    def kernel(
        owner_ref,
        lengths_ref,
        query_ref,
        log_ref,
        delta_ref,
        mine_ref,
        theirs_ref,
        grad_ref,
        out_ref,
        stack_ref,
        grad_stack_ref,
        sum_ref,
    ):
        places = Places(owner_ref, lengths_ref, rows)
        stack_ref[...] = head_stack(query_ref[:rows, :])
        grad_stack_ref[...] = head_stack(grad_ref[...])
        sum_ref[...] = jnp.zeros(sum_ref.shape, f32)
        lanes = lax.broadcasted_iota(jnp.int32, (1, 2 * rows), 1)
        own_label = places.label(places.own + jnp.where(lanes >= rows, lanes - rows, lanes))

        def step(block_ref, index, start, kind, scene):
            keys = block_ref[index, :, :local]
            values = block_ref[index, :, local:]
            taken = log_ref[...]
            if kind == "scene":
                taken = jnp.where(own_label == scene, taken, -absent)
            scores = dot_nt(keys, stack_ref[...]) - taken
            if kind == "mixed":
                label = places.label(start + lax.broadcasted_iota(jnp.int32, (rows, 128), 0))
                label = jnp.concatenate([label] * (2 * rows // 128), axis=1)
                scores = jnp.where(label == own_label, scores, absent)
            probs = jnp.exp(scores)
            grad_probs = dot_nt(values, grad_stack_ref[...])
            grad_scores = (probs * (grad_probs - delta_ref[...])).astype(bf16)
            sum_ref[...] += dot_tn(keys, grad_scores)

        places.over_blocks(half, True, functools.partial(step, mine_ref))
        places.over_blocks(half, False, functools.partial(step, theirs_ref))
        out_ref[...] = (heads_from_lanes(sum_ref[...]) * scale).T.astype(bf16)

    inputs = [owner, lengths, far(message), far(log_total), delta, far(mine), far(theirs), grad]
    return run_kernel(
        kernel,
        inputs,
        scalars() + [plain(item) for item in inputs[2:]],
        [((rows, local), bf16)],
        flops=64 * rows * count * rows * local,
        limit=16,
        scratch=[
            pltpu.VMEM((2 * rows, local), bf16),
            pltpu.VMEM((2 * rows, local), bf16),
            pltpu.VMEM((local, 2 * rows), f32),
        ],
    )[0]


def key_blocks(own_ref, queries_ref, block_ref, places, same_core, refs):
    keys_ref, values_ref, key_sum_ref, value_sum_ref = refs
    rows, local = own_ref.shape[0], own_ref.shape[1] // 2
    keys_ref[...] = head_stack(own_ref[:, :local])
    values_ref[...] = head_stack(own_ref[:, local:])
    own_label = places.label(places.own + lax.broadcasted_iota(jnp.int32, (rows, 128), 0))
    own_label = jnp.concatenate([own_label] * (rows // 128), axis=1)
    own_label = jnp.concatenate([own_label] * 2, axis=0)

    def spread(row):
        return jnp.concatenate(
            [
                jnp.broadcast_to(row[:, :rows], (rows, rows)),
                jnp.broadcast_to(row[:, rows:], (rows, rows)),
            ],
            axis=0,
        )

    def step(index, start, kind, scene):
        source = places.device_of(index, same_core)
        query = queries_ref[source, :rows, :]
        grad = block_ref[index, :rows, :]
        log_total = rows_back(queries_ref[source, rows:, :], 3, 2 * rows)
        delta = rows_back(block_ref[index, rows:, :], 3, 2 * rows)
        scores = dot_nt(keys_ref[...], query) - spread(log_total)
        if kind == "mixed":
            lanes = start + lax.broadcasted_iota(jnp.int32, (1, rows), 1)
            scores = jnp.where(own_label == places.label(lanes), scores, absent)
        probs = jnp.exp(scores)
        grad_probs = dot_nt(values_ref[...], grad)
        grad_scores = (probs * (grad_probs - spread(delta))).astype(bf16)
        value_part = dot_nn(probs.astype(bf16), grad)
        key_part = dot_nn(grad_scores, query)
        if kind == "scene":
            same = own_label[:, :local] == scene
            value_part = jnp.where(same, value_part, 0.0)
            key_part = jnp.where(same, key_part, 0.0)
        value_sum_ref[...] += value_part
        key_sum_ref[...] += key_part

    places.over_blocks(block_ref.shape[0], same_core, step)


def key_begin(queries, mine, key_value, owner, lengths):
    rows, local = key_value.shape[0], key_value.shape[1] // 2

    def kernel(
        owner_ref,
        lengths_ref,
        queries_ref,
        mine_ref,
        own_ref,
        key_sum_ref,
        value_sum_ref,
        keys_ref,
        values_ref,
    ):
        places = Places(owner_ref, lengths_ref, rows)
        key_sum_ref[...] = jnp.zeros(key_sum_ref.shape, f32)
        value_sum_ref[...] = jnp.zeros(value_sum_ref.shape, f32)
        refs = keys_ref, values_ref, key_sum_ref, value_sum_ref
        key_blocks(own_ref, queries_ref, mine_ref, places, True, refs)

    inputs = [owner, lengths, far(queries), mine, far(key_value)]
    return run_kernel(
        kernel,
        inputs,
        scalars() + [plain(item) for item in inputs[2:]],
        [((2 * rows, local), f32), ((2 * rows, local), f32)],
        flops=64 * rows * mine.shape[0] * rows * local,
        limit=16,
        scratch=[pltpu.VMEM((2 * rows, local), bf16), pltpu.VMEM((2 * rows, local), bf16)],
    )


def key_end(
    queries, theirs, key_value, sums, query_grad, qkv, layer, owner, lengths, unit
):
    rows, local = key_value.shape[0], key_value.shape[1] // 2
    width = qkv.shape[2]
    mp_count = lax.axis_size("mp")
    with_unit = unit is not None

    def kernel(
        owner_ref,
        lengths_ref,
        queries_ref,
        theirs_ref,
        own_ref,
        old_key_ref,
        old_value_ref,
        grad_ref,
        weight_ref,
        *refs,
    ):
        places = Places(owner_ref, lengths_ref, rows)
        if with_unit:
            unit_ref, refs = refs[0], refs[1:]
        part_ref, proj_ref, bias_ref, small_ref = refs[:4]
        keys_ref, values_ref, key_sum_ref, value_sum_ref = refs[4:]
        key_sum_ref[...] = old_key_ref[...]
        value_sum_ref[...] = old_value_ref[...]
        key_blocks(own_ref, queries_ref, theirs_ref, places, False, refs[4:])
        key_grad = heads_from_rows(key_sum_ref[...]).astype(bf16)
        value_grad = heads_from_rows(value_sum_ref[...]).astype(bf16)
        query_grad = grad_ref[...]
        proj_ref[:, :local] = query_grad
        proj_ref[:, local : 2 * local] = key_grad
        proj_ref[:, 2 * local :] = value_grad
        bias_ref[...] = jnp.zeros(bias_ref.shape, f32)
        bias_ref[0:1, :] = jnp.sum(query_grad.astype(f32), axis=0, keepdims=True)
        bias_ref[1:2, :] = jnp.sum(value_grad.astype(f32), axis=0, keepdims=True)
        part = dot_nt(query_grad, weight_ref[0, 0])
        part += dot_nt(key_grad, weight_ref[0, 1])
        part += dot_nt(value_grad, weight_ref[0, 2])
        low = part.astype(bf16)
        part_ref[...] = low.reshape(part_ref.shape)
        small_ref[...] = jnp.zeros(small_ref.shape, f32)
        if with_unit:
            into = low.astype(f32)
            small_ref[0:1, :] = jnp.sum(into * unit_ref[...], axis=0, keepdims=True)
            small_ref[1:2, :] = jnp.sum(into, axis=0, keepdims=True)

    inputs = [owner, lengths, far(queries), theirs, far(key_value)] + list(sums)
    inputs += [query_grad, far(qkv)]
    in_specs = scalars() + [plain(item) for item in inputs[2:8]] + [of_layer(qkv, layer)]
    if with_unit:
        inputs.append(far(unit))
        in_specs.append(plain(unit))
    return run_kernel(
        kernel,
        inputs,
        in_specs,
        [
            ((mp_count, rows // mp_count, width), bf16),
            ((rows, 3 * local), bf16, pltpu.HBM),
            ((8, local), f32, pltpu.HBM),
            ((8, width), f32, pltpu.HBM),
        ],
        flops=64 * rows * theirs.shape[0] * rows * local,
        limit=18,
        scratch=[
            pltpu.VMEM((2 * rows, local), bf16),
            pltpu.VMEM((2 * rows, local), bf16),
            pltpu.VMEM((2 * rows, local), f32),
            pltpu.VMEM((2 * rows, local), f32),
        ],
    )


def project(normed, qkv, bias, layer, first=None):
    rows, width = normed.shape
    local = qkv.shape[3]
    chips = lax.axis_size("dp") // 2
    own_rows = rows // lax.axis_size("mp")

    def kernel(normed_ref, weight_ref, bias_ref, *refs):
        if first is None:
            query_ref, pair_ref, spread_ref, kept_ref, sems = refs
            copies = keep_in_hbm([(normed_ref, kept_ref)], sems)
            normed = normed_ref[...]
        else:
            gain_ref, shift_ref, query_ref, pair_ref, spread_ref = refs[:5]
            own_ref, low_ref, unit_ref = refs[5:]
            centered, inverse = row_stats(normed_ref[...])
            unit = centered * inverse
            unit_ref[...] = unit
            normed = (unit * gain_ref[0:1, :] + shift_ref[0:1, :]).astype(bf16)
            low_ref[...] = normed
            own = pl.multiple_of(lax.axis_index("mp") * own_rows, own_rows)
            own_ref[...] = normed_ref[pl.ds(own, own_rows), :]
        query_bias, value_bias = (
            jnp.concatenate([bias_ref[0, at, 0:1, :], bias_ref[0, at, 1:2, :]], axis=1)
            for at in range(2)
        )
        query = dot_nn(normed, weight_ref[0, 0]) + query_bias
        query_ref[...] = query.astype(bf16)
        keys = dot_nn(normed, weight_ref[0, 1]).astype(bf16)
        values = (dot_nn(normed, weight_ref[0, 2]) + value_bias).astype(bf16)
        pair_ref[:, :local] = keys
        pair_ref[:, local:] = values
        for chip in range(chips):
            spread_ref[chip, :, :local] = keys
            spread_ref[chip, :, local:] = values
        if first is None:
            copies[0].wait()

    inputs = [normed, qkv, bias] if first is None else [far(normed), far(qkv), far(bias)]
    in_specs = [plain(normed), of_layer(qkv, layer), of_layer(bias, layer)]
    outputs = [
        ((rows, local), bf16),
        ((rows, 2 * local), bf16, pltpu.HBM),
        ((chips, rows, 2 * local), bf16),
    ]
    scratch = []
    if first is None:
        outputs.append((normed.shape, bf16, pltpu.HBM, True))
        scratch.append(pltpu.SemaphoreType.DMA((1,)))
    else:
        inputs += [far(item) for item in first]
        in_specs += [plain(item) for item in first]
        outputs += [
            ((own_rows, width), f32, pltpu.HBM),
            ((rows, width), bf16, pltpu.HBM),
            ((rows, width), f32, pltpu.HBM),
        ]
    return run_kernel(
        kernel, inputs, in_specs, outputs, flops=6 * rows * width * local, scratch=scratch
    )


def mlp_forward(normed, inner, inner_bias, down, layer):
    parts, part_rows, width = normed.shape
    rows, units = parts * part_rows, inner.shape[2]

    def kernel(
        normed_ref,
        inner_ref,
        bias_ref,
        down_ref,
        before_ref,
        active_ref,
        part_ref,
        kept_ref,
        sems,
    ):
        copies = keep_in_hbm([(normed_ref, kept_ref)], sems)
        own = normed_ref[...].reshape(rows, width)
        before = dot_nn(own, inner_ref[0]) + bias_ref[layer : layer + 1, :]
        before_ref[...] = before
        active = gelu(before).astype(bf16)
        active_ref[...] = active
        part_ref[...] = dot_nn(active, down_ref[0]).astype(bf16).reshape(part_ref.shape)
        copies[0].wait()

    inputs = [normed, far(inner), inner_bias, far(down)]
    return run_kernel(
        kernel,
        inputs,
        [plain(normed), of_layer(inner, layer), plain(inner_bias), of_layer(down, layer)],
        [
            ((rows, units), f32, pltpu.HBM),
            ((rows, units), bf16, pltpu.HBM),
            ((parts, part_rows, width), bf16),
            (normed.shape, bf16, pltpu.HBM, True),
        ],
        flops=4 * rows * width * units,
        scratch=[pltpu.SemaphoreType.DMA((1,))],
    )


def gelu(before):
    return 0.5 * before * (1.0 + lax.erf(before * math.sqrt(0.5)))


def gelu_slope(before):
    slope = 0.5 * (1.0 + lax.erf(before * math.sqrt(0.5)))
    return slope + before * jnp.exp(-0.5 * before * before) * (1.0 / math.sqrt(2.0 * math.pi))


def mlp_last(normed, cotangent, inner, inner_bias, down):
    parts, part_rows, width = normed.shape
    layer = inner.shape[0] - 1
    rows, units = parts * part_rows, inner.shape[2]

    def kernel(
        normed_ref,
        cotangent_ref,
        inner_ref,
        inner_bias_ref,
        down_ref,
        active_ref,
        out_ref,
        bias_ref,
        part_ref,
        own_ref,
        full_ref,
        kept_ref,
        sems,
    ):
        copies = keep_in_hbm([(normed_ref, kept_ref)], sems)
        grad = cotangent_ref[...].astype(bf16)
        full_ref[...] = grad.reshape(full_ref.shape)
        own = pl.multiple_of(lax.axis_index("mp") * part_rows, part_rows)
        own_ref[...] = cotangent_ref[pl.ds(own, part_rows), :]
        before = dot_nn(normed_ref[...].reshape(rows, width), inner_ref[0])
        before += inner_bias_ref[layer : layer + 1, :]
        out = (dot_nt(grad, down_ref[0]) * gelu_slope(before)).astype(bf16)
        out_ref[...] = out
        bias_ref[...] = jnp.broadcast_to(
            jnp.sum(out.astype(f32), axis=0, keepdims=True), bias_ref.shape
        )
        part = dot_nt(out, inner_ref[0]).astype(bf16)
        part_ref[:, :part_rows, :] = part.reshape(parts, part_rows, width)
        active = gelu(before).astype(bf16)
        active_ref[...] = active
        part = dot_nn(active, down_ref[0]).astype(bf16)
        part_ref[:, part_rows:, :] = part.reshape(parts, part_rows, width)
        copies[0].wait()

    inputs = [normed, far(cotangent), far(inner), inner_bias, far(down)]
    return run_kernel(
        kernel,
        inputs,
        [
            plain(normed),
            plain(cotangent),
            of_layer(inner, layer),
            plain(inner_bias),
            of_layer(down, layer),
        ],
        [
            ((rows, units), bf16, pltpu.HBM),
            ((rows, units), bf16, pltpu.HBM),
            ((8, units), f32, pltpu.HBM),
            ((parts, 2 * part_rows, width), bf16),
            ((part_rows, width), f32, pltpu.HBM),
            ((parts, part_rows, width), bf16, pltpu.HBM),
            (normed.shape, bf16, pltpu.HBM, True),
        ],
        flops=8 * rows * width * units,
        scratch=[pltpu.SemaphoreType.DMA((1,))],
    )


def mlp_backward(grad, before, inner, down, layer):
    parts, part_rows, width = grad.shape
    rows, units = parts * part_rows, inner.shape[2]

    def kernel(
        grad_ref, before_ref, inner_ref, down_ref, out_ref, bias_ref, part_ref, kept_ref, sems
    ):
        copies = keep_in_hbm([(grad_ref, kept_ref)], sems)
        into = dot_nt(grad_ref[...].reshape(rows, width), down_ref[0])
        out = (into * gelu_slope(before_ref[...])).astype(bf16)
        out_ref[...] = out
        bias_ref[...] = jnp.broadcast_to(
            jnp.sum(out.astype(f32), axis=0, keepdims=True), bias_ref.shape
        )
        part_ref[...] = dot_nt(out, inner_ref[0]).astype(bf16).reshape(part_ref.shape)
        copies[0].wait()

    inputs = [grad, before, inner, down]
    return run_kernel(
        kernel,
        inputs,
        [plain(grad), plain(before), of_layer(inner, layer), of_layer(down, layer)],
        [
            ((rows, units), bf16, pltpu.HBM),
            ((8, units), f32, pltpu.HBM),
            ((parts, part_rows, width), bf16),
            (grad.shape, bf16, pltpu.HBM, True),
        ],
        flops=4 * rows * width * units,
        scratch=[pltpu.SemaphoreType.DMA((1,))],
    )


def token_products(pairs):
    columns = [right.shape[-1] for left, right in pairs]
    width = pairs[0][0].shape[-1]
    rows = pairs[0][1].shape[0]
    items = [item for pair in pairs for item in pair]
    count = len(items)
    dp_count = lax.axis_size("dp")
    split = (dp_count // 4, 2, 2, width // dp_count)

    def kernel(*refs):
        sources, out_ref, held, parts = refs[:count], refs[count], refs[count + 1 : -2], refs[-2:]
        results, sems = held[count:], parts[0]
        out_sems = parts[1]
        copies = keep_in_hbm(zip(sources, held[:count]), sems)
        writes = []
        at = 0
        for index, size in enumerate(columns):
            copies[2 * index].wait()
            copies[2 * index + 1].wait()
            left = held[2 * index][...].reshape(rows, width)
            result = dot_tn(left, held[2 * index + 1][...]).astype(bf16)
            results[index][...] = result.reshape(split + (size,))
            for x in range(2):
                for core in range(2):
                    write = pltpu.make_async_copy(
                        results[index].at[:, x, core],
                        out_ref.at[:, core, x, :, pl.ds(at, size)],
                        out_sems.at[4 * index + 2 * x + core],
                    )
                    write.start()
                    writes.append(write)
            at += size
        for write in writes:
            write.wait()

    return run_kernel(
        kernel,
        [far(item) for item in items],
        [whole(pltpu.HBM)] * count,
        [(split + (sum(columns),), bf16, pltpu.HBM, True)],
        flops=2 * rows * width * sum(columns),
        scratch=[pltpu.VMEM(item.shape, item.dtype) for item in items]
        + [pltpu.VMEM(split + (size,), bf16) for size in columns]
        + [pltpu.SemaphoreType.DMA((count,)), pltpu.SemaphoreType.DMA((4 * len(pairs),))],
    )[0].reshape(width, sum(columns))


def last_products(pairs, norm_one, norm_two, key_small, own_cotangent, proj_bias, inner_bias):
    width = own_cotangent.shape[1]
    dp_count = lax.axis_size("dp")
    columns = width // dp_count
    token_rows = pairs[0][1].shape[0]
    total = sum(right.shape[-1] for left, right in pairs)
    items = [item for pair in pairs for item in pair]
    inputs = items + [norm_one, norm_two[0], norm_two[1], key_small, own_cotangent]
    inputs = [far(item) for item in inputs + proj_bias + inner_bias]

    def kernel(*refs):
        item_refs, refs = refs[: len(items)], refs[len(items) :]
        one_ref, two_a_ref, two_b_ref, key_ref, grad_ref = refs[:5]
        proj_refs, inner_refs = refs[5:7], refs[7:9]
        mine_ref, away_ref, first_ref, second_ref, product_ref = refs[9:]
        at = 0
        for left_ref, right_ref in zip(item_refs[0::2], item_refs[1::2]):
            left = left_ref[...].reshape(token_rows, width)
            size = right_ref.shape[-1]
            product_ref[:, at : at + size] = dot_tn(left, right_ref[...]).astype(bf16)
            at += size
        last = jnp.sum(grad_ref[...].astype(bf16).astype(f32), axis=0, keepdims=True)
        zero = jnp.zeros((2, width), f32)
        for target, two_ref, gains, bias in (
            (first_ref, two_a_ref, key_ref, one_ref[2:3, :]),
            (second_ref, two_b_ref, one_ref, last),
        ):
            target[0:2, :] = gains[0:2, :]
            target[2:3, :] = two_ref[2:3, :]
            target[3:5, :] = two_ref[0:2, :]
            target[5:6, :] = bias
            target[6:8, :] = zero
        lines = [proj_refs[layer][row : row + 1, :] for layer in range(2) for row in range(2)]
        for layer in range(2):
            lines += [inner_refs[layer][0:1, 128 * at : 128 * at + 128] for at in range(4)]
        row_index = lax.broadcasted_iota(jnp.int32, (8, 128), 0)
        shared = []
        for group in (lines[:8], lines[8:]):
            tile = jnp.zeros((8, 128), f32)
            for row, line in enumerate(group):
                tile = jnp.where(row_index == row, jnp.broadcast_to(line, (8, 128)), tile)
            shared.append(tile)
        core = lax.rem(lax.axis_index("dp"), 2)
        for device in range(dp_count):
            at = slice(device * columns, (device + 1) * columns)
            small = jnp.concatenate([first_ref[:, at], second_ref[:, at]] + shared, axis=1)
            high = small.astype(bf16).astype(f32)
            tail = jnp.concatenate([high, small - high], axis=0).astype(bf16)
            for flag, ref in ((core == device % 2, mine_ref), (core != device % 2, away_ref)):

                @pl.when(flag)
                def _(ref=ref, tail=tail, device=device, at=at):
                    ref[device // 2, :columns, :] = product_ref[at, :]
                    ref[device // 2, columns:, :] = tail

    shape = ((dp_count // 2, columns + 16, total), bf16)
    return run_kernel(
        kernel,
        inputs,
        [plain(item) for item in inputs],
        [shape, shape],
        flops=2 * token_rows * width * total,
        scratch=[
            pltpu.VMEM((8, width), f32),
            pltpu.VMEM((8, width), f32),
            pltpu.VMEM((width, total), bf16),
        ],
    )


def add_cores(mine, other, columns, output):
    parts, part_rows, width = output.shape

    def kernel(mine_ref, other_ref, low_ref, out_ref, output_ref):
        for chip in range(mine.shape[0]):
            both = mine_ref[chip].astype(f32) + other_ref[chip].astype(f32)
            out_ref[chip, :columns, :] = both[:columns].astype(bf16)
            small = both[columns : columns + 8] + both[columns + 8 :]
            high = small.astype(bf16).astype(f32)
            out_ref[chip, columns:, :] = jnp.concatenate([high, small - high], axis=0).astype(bf16)
        output_ref[...] = low_ref[...].astype(f32).reshape(parts * part_rows, width)

    return run_kernel(
        kernel,
        [mine, other, far(output)],
        [plain(mine), plain(other), plain(output)],
        [(mine.shape, bf16), ((parts * part_rows, width), f32, pltpu.HBM)],
    )


def own_half(pieces):
    shape = pieces.shape[1:]

    def kernel(pieces_ref, mine_ref, away_ref):
        x = lax.rem(lax.div(lax.axis_index("dp"), 2), 2)
        mine_ref[...] = pieces_ref[x]
        away_ref[...] = pieces_ref[1 - x]

    return run_kernel(
        kernel, [far(pieces)], [plain(pieces)], [(shape, bf16, pltpu.HBM), (shape, bf16)]
    )


def scatter_sum(pairs):
    count = lax.axis_size("dp")
    groups = [[4 * z + 2 * x + core for z in range(count // 4) for core in range(2)] for x in range(2)]
    pieces = lax.psum_scatter(
        token_products(pairs), "dp", scatter_dimension=0, tiled=True, axis_index_groups=groups
    )
    mine, away = own_half(pieces.reshape(2, -1, pieces.shape[1]))
    return mine, lax.ppermute(away, "dp", [(index, index ^ 2) for index in range(count)])


def finish_rows(got, width):
    parts, own_rows = got.shape[:2]

    def kernel(got_ref, out_ref, *small_refs):
        total = jnp.zeros((8, 128), f32)
        for part in range(parts):
            at = slice(part * own_rows, (part + 1) * own_rows)
            out_ref[at, :] = got_ref[part, :, :width].astype(f32)
            both = got_ref[part, :16, width:].astype(f32)
            total += both[:8] + both[8:]
        for index, small_ref in enumerate(small_refs):
            small_ref[0:1, :] = total[index : index + 1, :64]
            small_ref[1:2, :] = total[index : index + 1, 64:]

    return run_kernel(
        kernel,
        [got],
        [plain(got)],
        [((parts * own_rows, width), f32, pltpu.HBM)] + [((2, 64), f32, pltpu.HBM)] * 6,
    )


def finish_biases(third, columns):
    bias_columns = columns // lax.axis_size("dp")

    def kernel(third_ref, small_ref):
        small = jnp.zeros((8, third.shape[2]), f32)
        for chip in range(third.shape[0]):
            piece = third_ref[chip, columns:, :].astype(f32)
            small += piece[:8] + piece[8:]
        small = jnp.concatenate([small[:, 128:256], small[:, 256:384]], axis=0)
        lane = lax.broadcasted_iota(jnp.int32, small.shape, 1)
        own = lax.axis_index("dp") * bias_columns
        picked = jnp.zeros(small.shape, f32)
        for half in range(2):
            for column in range(bias_columns):
                at = half * 64 + own + column
                value = jnp.sum(jnp.where(lane == at, small, 0.0), axis=1, keepdims=True)
                picked = jnp.where(lane == half * bias_columns + column, value, picked)
        small_ref[...] = picked

    return run_kernel(kernel, [third], [plain(third)], [((16, 128), f32)])[0]


def finish_weights(first, second, third, local, units):
    columns = first[0].shape[0]

    def kernel(first_ref, first_other_ref, second_ref, second_other_ref, third_ref, qkv_ref, out_ref, inner_ref, down_ref):
        last = add_parts(third_ref)
        middle = first_ref[...].astype(f32) + first_other_ref[...].astype(f32)
        late = second_ref[...].astype(f32) + second_other_ref[...].astype(f32)
        for layer, sums in ((1, middle), (0, late)):
            inner_ref[layer] = sums[:, :units]
            down_ref[layer] = sums[:, units : 2 * units]
            out_ref[layer] = sums[:, 2 * units : 2 * units + local]
        for piece in range(3):
            at = 2 * units + local * (piece + 1)
            qkv_ref[1, piece] = middle[:, at : at + local]
            qkv_ref[0, piece] = last[:columns, local * piece : local * (piece + 1)]

    inputs = list(first) + list(second) + [third]
    return run_kernel(
        kernel,
        inputs,
        [plain(item) for item in inputs],
        [
            ((2, 3, columns, local), f32, pltpu.HBM),
            ((2, columns, local), f32, pltpu.HBM),
            ((2, columns, units), f32, pltpu.HBM),
            ((2, columns, units), f32, pltpu.HBM),
        ],
    )


def body(
    hidden_in,
    cotangent,
    scene_lengths,
    block_owner,
    attn_gain,
    attn_shift,
    qkv_weight,
    qv_bias,
    out_weight,
    out_bias,
    mlp_gain,
    mlp_shift,
    mlp_in_weight,
    mlp_in_bias,
    mlp_out_weight,
    mlp_out_bias,
):
    rows, width = hidden_in.shape
    layers = attn_gain.shape[0]
    local = qv_bias.shape[2] * qv_bias.shape[3]
    units = mlp_in_bias.shape[1]
    dp_count, mp_count = lax.axis_size("dp"), lax.axis_size("mp")
    own_rows = rows // mp_count
    qkv = qkv_weight.transpose(0, 2, 1, 3)
    where = (block_owner, scene_lengths)
    Cost.weight = 0.0

    kept = []
    for layer in range(layers):
        if layer:
            query, pair, spread, normed = project(normed, qkv, qv_bias, layer)
            spread = after(spread, queries)
        else:
            query, pair, spread, hidden, normed, unit = project(
                hidden_in, qkv, qv_bias, layer, (attn_gain, attn_shift)
            )
        mine = gather_chips(spread)
        theirs = from_other_core(mine)
        *state, mine = attention_begin(query, mine, *where)
        part, attended_low, flat, log_total, message, theirs = attention_end(
            query, theirs, state, out_weight, layer, *where
        )
        got = exchange_mp(part)
        queries = lax.all_gather(after(message, got), "dp", axis=0, tiled=True)
        queries = queries.reshape((dp_count,) + message.shape)
        middle, spread = residual_norm(
            got, hidden, out_bias, layer, mlp_gain, mlp_shift, layer
        )
        normed_mlp = exchange_mp(spread)
        if layer + 1 < layers:
            before, active, part, normed_mlp = mlp_forward(
                normed_mlp, mlp_in_weight, mlp_in_bias, mlp_out_weight, layer
            )
        kept.append(
            dict(
                hidden=hidden,
                normed=normed,
                pair=pair,
                mine=mine,
                theirs=theirs,
                attended_low=attended_low,
                flat=flat,
                log_total=log_total,
                message=message,
                queries=queries,
                middle=middle,
                normed_mlp=normed_mlp,
                before=before,
                active=active,
            )
        )
        if layer + 1 < layers:
            hidden, spread = residual_norm(
                exchange_mp(part), middle, mlp_out_bias, layer, attn_gain, attn_shift, layer + 1
            )
            normed = exchange_mp(spread).reshape(rows, width)
    norm_one, norm_two, bias_proj, bias_inner = {}, {}, {}, {}
    for layer in reversed(range(layers)):
        now = kept[layer]
        if layer == layers - 1:
            (
                now["active"],
                grad_before,
                bias_inner[layer],
                part,
                grad_own,
                grad_full,
                now["normed_mlp"],
            ) = mlp_last(now["normed_mlp"], cotangent, mlp_in_weight, mlp_in_bias, mlp_out_weight)
            own_cotangent = grad_own
        else:
            grad_before, bias_inner[layer], part, grad_full = mlp_backward(
                grad_full, now["before"], mlp_in_weight, mlp_out_weight, layer
            )
        mlp_pairs = [(now["normed_mlp"], grad_before), (grad_full, now["active"])]
        middle_grad, spread, norm_two[layer] = norm_backward(
            exchange_mp(part),
            now["middle"],
            mlp_gain,
            layer,
            grad_own,
            bias=mlp_out_bias if layer == layers - 1 else None,
        )
        if layer == layers - 1:
            spread = after(spread, now["queries"])
        spread, grad_rows, delta, branch, *ridden = grad_attended(
            exchange_mp(spread), out_weight, layer, now["flat"]
        )
        if ridden:
            output = ridden[0]
        grad_mine = gather_chips(spread)
        query_grad = query_side(
            now["message"], now["log_total"], delta, now["mine"], now["theirs"], grad_rows, *where
        )
        grad_theirs = from_other_core(after(grad_mine, query_grad))
        sums = key_begin(now["queries"], grad_mine, now["pair"], *where)
        part, proj_grad, bias_proj[layer], key_small = key_end(
            now["queries"],
            grad_theirs,
            now["pair"],
            sums,
            query_grad,
            qkv,
            layer,
            *where,
            unit if layer == 0 else None,
        )
        if layer:
            Cost.weight = 9.5
        out_pairs = [(branch, now["attended_low"])]
        proj_pairs = [(now["normed"], proj_grad)]
        if layer:
            grad_own, spread, norm_one[layer] = norm_backward(
                exchange_mp(part), now["hidden"], attn_gain, layer, middle_grad
            )
            grad_full = exchange_mp(spread)
            first = scatter_sum(mlp_pairs + out_pairs + proj_pairs)
        else:
            second = scatter_sum(mlp_pairs + out_pairs)
            mine, away = last_products(
                proj_pairs,
                norm_one[1],
                norm_two,
                key_small,
                own_cotangent,
                [bias_proj[0], bias_proj[1]],
                [bias_inner[0], bias_inner[1]],
            )
            both, output = add_cores(mine, from_other_core(away), width // dp_count, output)
            got = exchange_mp(part)
            third = gather_chips(after(both, got))
            ignored, spread, ignored = norm_backward(
                got, now["hidden"], attn_gain, layer, middle_grad, third
            )
            tail = exchange_mp(after(spread, first[1], second[1]))

    small = finish_biases(third, width // dp_count)
    qkv_grad, out_grad, inner_grad, down_grad = finish_weights(
        first, second, third, local, units
    )
    (
        input_grad,
        gain_one,
        shift_one,
        out_bias_grad,
        gain_two,
        shift_two,
        down_bias_grad,
    ) = finish_rows(tail, width)
    bias_columns = qv_bias.shape[3] // dp_count
    qv_grad = small[:4, : 2 * bias_columns].reshape(layers, 2, 2, bias_columns)
    inner_bias_grad = small[4:12, : 2 * bias_columns].reshape(layers, units // 64, bias_columns)
    return (
        output,
        input_grad,
        gain_one,
        shift_one,
        qkv_grad.transpose(0, 2, 1, 3),
        qv_grad,
        out_grad.transpose(0, 2, 1),
        out_bias_grad,
        gain_two,
        shift_two,
        inner_grad,
        inner_bias_grad,
        down_grad.transpose(0, 2, 1),
        down_bias_grad,
    )


def solution(mesh):
    in_specs = (
        P("dp", None),
        P("dp", None),
        P(),
        P(),
        P(),
        P(),
        P(None, None, None, "mp"),
        P(None, None, "mp", None),
        P(None, "mp", None),
        P(),
        P(),
        P(),
        P(None, None, "mp"),
        P(None, "mp"),
        P(None, "mp", None),
        P(),
    )
    out_specs = (
        P("dp", None),
        P("dp", None),
        P(None, "dp"),
        P(None, "dp"),
        P(None, "dp", None, "mp"),
        P(None, None, "mp", "dp"),
        P(None, "mp", "dp"),
        P(None, "dp"),
        P(None, "dp"),
        P(None, "dp"),
        P(None, "dp", "mp"),
        P(None, "mp", "dp"),
        P(None, "mp", "dp"),
        P(None, "dp"),
    )
    return jax.shard_map(body, mesh=mesh, in_specs=in_specs, out_specs=out_specs, check_vma=False)
```

```python
import functools
import math

import jax
import jax.numpy as jnp
from jax import lax
from jax.experimental import pallas as pl
from jax.experimental.pallas import tpu as pltpu
from jax.sharding import PartitionSpec as P

norm_eps = 1e-05
f32 = jnp.float32
bf16 = jnp.bfloat16
absent = -1e30


class Cost:
    weight = 0.0


def chip_groups(count):
    return [list(range(core, count, 2)) for core in range(2)]


def other_core(count):
    return [(index, index ^ 1) for index in range(count)]


def exchange_mp(spread):
    return lax.all_to_all(spread, "mp", 0, 0, tiled=True)


def gather_chips(spread):
    groups = chip_groups(lax.axis_size("dp"))
    return lax.all_to_all(spread, "dp", 0, 0, tiled=True, axis_index_groups=groups)


def from_other_core(blocks):
    return lax.ppermute(blocks, "dp", other_core(lax.axis_size("dp")))


def after(value, *others):
    return lax.optimization_barrier((value,) + others)[0]


def whole(memory=pltpu.VMEM):
    return pl.BlockSpec(memory_space=memory)


def of_layer(stacked, layer):
    tail = stacked.shape[1:]
    return pl.BlockSpec((1,) + tail, lambda step: (layer,) + (0,) * len(tail))


def plain(array):
    return pl.BlockSpec(array.shape, lambda step: (0,) * len(array.shape))


def far(array):
    return pltpu.with_memory_space_constraint(array, pltpu.HBM)


def run_kernel(kernel, inputs, in_specs, outputs, flops=0, scratch=(), limit=12):
    moved = sum(math.prod(out[0]) * jnp.dtype(out[1]).itemsize for out in outputs)
    moved += sum(item.size * item.dtype.itemsize for item in inputs)
    return pl.pallas_call(
        kernel,
        grid=(1,),
        in_specs=in_specs,
        out_specs=[
            whole(pltpu.HBM)
            if len(out) == 4
            else pl.BlockSpec(out[0], functools.partial(lambda rank, step: (0,) * rank, len(out[0])))
            for out in outputs
        ],
        out_shape=[
            out[2](out[0], out[1]) if len(out) > 2 else jax.ShapeDtypeStruct(out[0], out[1])
            for out in outputs
        ],
        scratch_shapes=list(scratch),
        compiler_params=pltpu.CompilerParams(vmem_limit_bytes=limit * 2**20),
        cost_estimate=pl.CostEstimate(
            flops=int(Cost.weight * 1e9 + flops), bytes_accessed=moved, transcendentals=0
        ),
    )(*inputs)


def keep_in_hbm(pairs, sems):
    copies = [
        pltpu.make_async_copy(source, kept, sems.at[index])
        for index, (source, kept) in enumerate(pairs)
    ]
    for copy in copies:
        copy.start()
    return copies


def dot_nn(left, right):
    return lax.dot_general(left, right, (((1,), (0,)), ((), ())), preferred_element_type=f32)


def dot_nt(left, right):
    return lax.dot_general(left, right, (((1,), (1,)), ((), ())), preferred_element_type=f32)


def dot_tn(left, right):
    return lax.dot_general(left, right, (((0,), (0,)), ((), ())), preferred_element_type=f32)


def row_stats(inputs):
    average = jnp.mean(inputs, axis=-1, keepdims=True)
    centered = inputs - average
    variance = jnp.mean(centered * centered, axis=-1, keepdims=True)
    return centered, lax.rsqrt(variance + norm_eps)


def add_parts(got_ref):
    total = got_ref[0].astype(f32)
    for part in range(1, got_ref.shape[0]):
        total += got_ref[part].astype(f32)
    return total


def residual_norm(got, residual, bias, bias_layer, gain, shift, norm_layer):
    parts, rows, width = got.shape

    def kernel(got_ref, residual_ref, bias_ref, gain_ref, shift_ref, out_ref, spread_ref):
        total = residual_ref[...] + add_parts(got_ref) + bias_ref[bias_layer : bias_layer + 1, :]
        out_ref[...] = total
        layer = slice(norm_layer, norm_layer + 1)
        centered, inverse = row_stats(total)
        normed = (centered * inverse * gain_ref[layer, :] + shift_ref[layer, :]).astype(bf16)
        for part in range(parts):
            spread_ref[part] = normed

    inputs = [got, residual, bias, gain, shift]
    outputs = [((rows, width), f32, pltpu.HBM), ((parts, rows, width), bf16)]
    return run_kernel(kernel, inputs, [plain(item) for item in inputs], outputs)


def norm_backward(got, inputs, gain, layer, grad, extra=None, bias=None):
    parts, rows, width = got.shape
    if bias is not None:
        rows //= 2
    more = 0 if extra is None else 128
    spread_rows = rows if bias is None else 2 * rows

    def kernel(got_ref, inputs_ref, gain_ref, grad_ref, *refs):
        out_ref, spread_ref, small_ref = refs[-3:]
        total = add_parts(got_ref)
        into = total[:rows]
        if bias is not None:
            output = inputs_ref[...] + total[rows:] + refs[0][layer : layer + 1, :]
            output = output.astype(bf16)
        centered, inverse = row_stats(inputs_ref[...])
        unit = centered * inverse
        scaled = into * gain_ref[layer : layer + 1, :]
        first = jnp.mean(scaled, axis=-1, keepdims=True)
        second = jnp.mean(scaled * unit, axis=-1, keepdims=True)
        total = grad_ref[...] + (scaled - first - unit * second) * inverse
        out_ref[...] = total
        rounded = total.astype(bf16)
        for part in range(parts):
            spread_ref[part, :rows, :width] = rounded
            if bias is not None:
                spread_ref[part, rows:, :] = output
        if more:
            small = jnp.zeros((8, 128), f32)
            for chip in range(extra.shape[0]):
                piece = refs[0][chip, -16:, :128].astype(f32)
                small += piece[:8] + piece[8:]
            high = small.astype(bf16).astype(f32)
            zero = jnp.zeros((rows - 16, 128), f32)
            both = jnp.concatenate([high, small - high, zero], axis=0).astype(bf16)
            for part in range(parts):
                spread_ref[part, :, width:] = both
        small_ref[0:1, :] = jnp.sum(into * unit, axis=0, keepdims=True)
        small_ref[1:2, :] = jnp.sum(into, axis=0, keepdims=True)
        small_ref[2:3, :] = jnp.sum(rounded.astype(f32), axis=0, keepdims=True)
        small_ref[3:, :] = jnp.zeros((5, width), f32)

    inputs = [got, inputs, gain, grad] + [item for item in (extra, bias) if item is not None]
    outputs = [
        ((rows, width), f32, pltpu.HBM),
        ((parts, spread_rows, width + more), bf16),
        ((8, width), f32, pltpu.HBM),
    ]
    return run_kernel(kernel, inputs, [plain(item) for item in inputs], outputs)


class Places:
    def __init__(self, owner_ref, lengths_ref, rows):
        self.owner_ref, self.rows = owner_ref, rows
        self.device = lax.axis_index("dp")
        self.core = lax.rem(self.device, 2)
        self.own = owner_ref[self.device] * rows
        self.ends = []
        for scene in range(lengths_ref.shape[0]):
            before = self.ends[-1] if self.ends else 0
            self.ends.append(before + lengths_ref[scene])

    def device_of(self, index, same_core):
        return 2 * index + (self.core if same_core else 1 - self.core)

    def start(self, index, same_core):
        return self.owner_ref[self.device_of(index, same_core)] * self.rows

    def label(self, position):
        return sum((position >= end).astype(jnp.int32) for end in self.ends)

    def scalar_label(self, position):
        return sum(jnp.where(position >= end, 1, 0).astype(jnp.int32) for end in self.ends)

    def over_blocks(self, count, same_core, step):
        last = self.rows - 1
        own_first, own_last = self.scalar_label(self.own), self.scalar_label(self.own + last)
        own_alone = own_first == own_last

        def one(index, carry):
            start = self.start(index, same_core)
            first, end = self.scalar_label(start), self.scalar_label(start + last)
            meets = jnp.logical_and(first <= own_last, own_first <= end)
            uniform = first == end
            plain_kind = jnp.logical_and(uniform, own_alone)
            scene_kind = jnp.logical_and(uniform, jnp.logical_not(own_alone))
            for kind, flag in (
                ("plain", plain_kind),
                ("scene", scene_kind),
                ("mixed", jnp.logical_not(uniform)),
            ):

                @pl.when(jnp.logical_and(meets, flag))
                def _(kind=kind):
                    step(index, start, kind, first)

            return carry

        lax.fori_loop(0, count, one, 0)


def scalars():
    return [whole(pltpu.SMEM), whole(pltpu.SMEM)]


def head_stack(rows):
    lane = lax.broadcasted_iota(jnp.int32, rows.shape, 1)
    half = rows.shape[1] // 2
    zero = jnp.zeros_like(rows)
    return jnp.concatenate(
        [jnp.where(lane < half, rows, zero), jnp.where(lane >= half, rows, zero)], axis=0
    )


def heads_from_lanes(stacked):
    half, rows = stacked.shape[0] // 2, stacked.shape[1] // 2
    return jnp.concatenate([stacked[:half, :rows], stacked[half:, rows:]], axis=0)


def heads_from_rows(stacked):
    rows = stacked.shape[0] // 2
    lane = lax.broadcasted_iota(jnp.int32, (rows, stacked.shape[1]), 1)
    return jnp.where(lane < stacked.shape[1] // 2, stacked[:rows], stacked[rows:])


def row_pieces(vector, count):
    pieces = []
    rest = vector
    for piece in range(count):
        term = rest.astype(bf16).astype(f32)
        rest = rest - term
        pieces += [term[:, start : start + 128] for start in range(0, vector.shape[1], 128)]
    row = lax.broadcasted_iota(jnp.int32, (16, 128), 0)
    tile = jnp.zeros((16, 128), f32)
    for index, piece in enumerate(pieces):
        tile = jnp.where(row == index, jnp.broadcast_to(piece, (16, 128)), tile)
    return tile.astype(bf16)


def rows_back(tile, count, length):
    tile = tile.astype(f32)
    lines = length // 128
    out = []
    for line in range(lines):
        total = tile[line : line + 1]
        for piece in range(1, count):
            total = total + tile[piece * lines + line : piece * lines + line + 1]
        out.append(total)
    return jnp.concatenate(out, axis=1)


def attention_blocks(query_ref, block_ref, places, same_core, stack_ref, peak_ref, total_ref, sum_ref):
    rows, local = query_ref.shape
    scale = 1.0 / math.sqrt(local // 2)
    scaled = (query_ref[...].astype(f32) * scale).astype(bf16)
    stack_ref[...] = head_stack(scaled)
    lanes = lax.broadcasted_iota(jnp.int32, (1, 2 * rows), 1)
    own_label = places.label(places.own + jnp.where(lanes >= rows, lanes - rows, lanes))

    def step(index, start, kind, scene):
        keys = block_ref[index, :, :local]
        values = block_ref[index, :, local:]
        scores = dot_nt(keys, stack_ref[...])
        if kind == "mixed":
            label = places.label(start + lax.broadcasted_iota(jnp.int32, (rows, 128), 0))
            label = jnp.concatenate([label] * (2 * rows // 128), axis=1)
            scores = jnp.where(label == own_label, scores, absent)
        old = peak_ref[...]
        highest = jnp.max(scores, axis=0, keepdims=True)
        if kind == "scene":
            highest = jnp.where(own_label == scene, highest, absent)
        new = jnp.maximum(old, highest)
        taken = jnp.where(own_label == scene, new, -absent) if kind == "scene" else new
        weight = jnp.exp(scores - taken)
        fade = jnp.exp(old - new)
        peak_ref[...] = new
        total_ref[...] = total_ref[...] * fade + jnp.sum(weight, axis=0, keepdims=True)
        sum_ref[...] = sum_ref[...] * fade + dot_tn(values, weight.astype(bf16))

    places.over_blocks(block_ref.shape[0], same_core, step)
    return scaled


def attention_begin(query, mine, owner, lengths):
    rows, local = query.shape

    def kernel(
        owner_ref,
        lengths_ref,
        query_ref,
        mine_ref,
        peak_ref,
        total_ref,
        sum_ref,
        kept_ref,
        stack_ref,
        sems,
    ):
        copies = keep_in_hbm([(mine_ref, kept_ref)], sems)
        places = Places(owner_ref, lengths_ref, rows)
        peak_ref[...] = jnp.full(peak_ref.shape, 0.1 * absent, f32)
        total_ref[...] = jnp.zeros(total_ref.shape, f32)
        sum_ref[...] = jnp.zeros(sum_ref.shape, f32)
        attention_blocks(
            query_ref, mine_ref, places, True, stack_ref, peak_ref, total_ref, sum_ref
        )
        copies[0].wait()

    return run_kernel(
        kernel,
        [owner, lengths, query, mine],
        scalars() + [plain(query), plain(mine)],
        [
            ((1, 2 * rows), f32),
            ((1, 2 * rows), f32),
            ((local, 2 * rows), f32),
            (mine.shape, bf16, pltpu.HBM, True),
        ],
        flops=32 * rows * mine.shape[0] * rows * local,
        limit=16,
        scratch=[pltpu.VMEM((2 * rows, local), bf16), pltpu.SemaphoreType.DMA((1,))],
    )


def attention_end(query, theirs, state, out_weight, layer, owner, lengths):
    rows, local = query.shape
    width = out_weight.shape[2]
    mp_count = lax.axis_size("mp")

    def kernel(
        owner_ref,
        lengths_ref,
        query_ref,
        theirs_ref,
        old_peak_ref,
        old_total_ref,
        old_sum_ref,
        weight_ref,
        part_ref,
        low_ref,
        flat_ref,
        log_ref,
        message_ref,
        kept_ref,
        stack_ref,
        peak_ref,
        total_ref,
        sum_ref,
        sems,
    ):
        copies = keep_in_hbm([(theirs_ref, kept_ref)], sems)
        places = Places(owner_ref, lengths_ref, rows)
        peak_ref[...] = old_peak_ref[...]
        total_ref[...] = old_total_ref[...]
        sum_ref[...] = old_sum_ref[...]
        scaled = attention_blocks(
            query_ref, theirs_ref, places, False, stack_ref, peak_ref, total_ref, sum_ref
        )
        attended = heads_from_lanes(sum_ref[...] / total_ref[...])
        flat_ref[...] = attended
        low = attended.T.astype(bf16)
        low_ref[...] = low
        part = dot_nn(low, weight_ref[0]).astype(bf16)
        part_ref[...] = part.reshape(part_ref.shape)
        log_total = peak_ref[...] + jnp.log(total_ref[...])
        log_ref[...] = log_total
        message_ref[:rows, :] = scaled
        message_ref[rows:, :] = row_pieces(log_total, 3)
        copies[0].wait()

    inputs = [owner, lengths, query, theirs] + list(state) + [out_weight]
    return run_kernel(
        kernel,
        inputs,
        scalars() + [plain(item) for item in inputs[2:7]] + [of_layer(out_weight, layer)],
        [
            ((mp_count, rows // mp_count, width), bf16),
            ((rows, local), bf16, pltpu.HBM),
            ((local, rows), f32, pltpu.HBM),
            ((1, 2 * rows), f32, pltpu.HBM),
            ((rows + 16, local), bf16, pltpu.HBM),
            (theirs.shape, bf16, pltpu.HBM, True),
        ],
        flops=32 * rows * theirs.shape[0] * rows * local,
        limit=16,
        scratch=[
            pltpu.VMEM((2 * rows, local), bf16),
            pltpu.VMEM((1, 2 * rows), f32),
            pltpu.VMEM((1, 2 * rows), f32),
            pltpu.VMEM((local, 2 * rows), f32),
            pltpu.SemaphoreType.DMA((1,)),
        ],
    )


def grad_attended(branch, out_weight, layer, flat):
    parts, part_rows, width = branch.shape
    ridden = 0 if parts * part_rows == flat.shape[1] else 1
    part_rows //= 1 + ridden
    rows = parts * part_rows
    local = out_weight.shape[1]

    chips = lax.axis_size("dp") // 2

    def kernel(branch_ref, weight_ref, flat_ref, spread_ref, message_ref, delta_ref, *refs):
        kept_refs, sems = refs[:-1], refs[-1]
        copies = keep_in_hbm(
            [
                (branch_ref.at[:, pl.ds(index * part_rows, part_rows)], kept_ref)
                for index, kept_ref in enumerate(kept_refs)
            ],
            sems,
        )
        own = branch_ref[:, :part_rows, :].reshape(rows, width)
        grad = dot_nt(own, weight_ref[0]).astype(bf16)
        product = grad.astype(f32).T * flat_ref[...]
        half = local // 2
        delta = jnp.concatenate(
            [
                jnp.sum(product[:half], axis=0, keepdims=True),
                jnp.sum(product[half:], axis=0, keepdims=True),
            ],
            axis=1,
        )
        delta_ref[...] = delta
        pieces = row_pieces(delta, 3)
        message_ref[...] = grad
        for chip in range(chips):
            spread_ref[chip, :rows, :] = grad
            spread_ref[chip, rows:, :] = pieces
        for copy in copies:
            copy.wait()

    inputs = [branch, far(out_weight), far(flat)]
    return run_kernel(
        kernel,
        inputs,
        [plain(branch), of_layer(out_weight, layer), plain(flat)],
        [
            ((chips, rows + 16, local), bf16),
            ((rows, local), bf16),
            ((1, 2 * rows), f32),
        ]
        + [((parts, part_rows, width), bf16, pltpu.HBM, True)] * (1 + ridden),
        flops=2 * rows * local * width,
        scratch=[pltpu.SemaphoreType.DMA((1 + ridden,))],
    )


def query_side(message, log_total, delta, mine, theirs, grad, owner, lengths):
    rows, local = grad.shape
    half = mine.shape[0]
    count = 2 * half
    scale = 1.0 / math.sqrt(local // 2)

    def kernel(
        owner_ref,
        lengths_ref,
        query_ref,
        log_ref,
        delta_ref,
        mine_ref,
        theirs_ref,
        grad_ref,
        out_ref,
        stack_ref,
        grad_stack_ref,
        sum_ref,
    ):
        places = Places(owner_ref, lengths_ref, rows)
        stack_ref[...] = head_stack(query_ref[:rows, :])
        grad_stack_ref[...] = head_stack(grad_ref[...])
        sum_ref[...] = jnp.zeros(sum_ref.shape, f32)
        lanes = lax.broadcasted_iota(jnp.int32, (1, 2 * rows), 1)
        own_label = places.label(places.own + jnp.where(lanes >= rows, lanes - rows, lanes))

        def step(block_ref, index, start, kind, scene):
            keys = block_ref[index, :, :local]
            values = block_ref[index, :, local:]
            taken = log_ref[...]
            if kind == "scene":
                taken = jnp.where(own_label == scene, taken, -absent)
            scores = dot_nt(keys, stack_ref[...]) - taken
            if kind == "mixed":
                label = places.label(start + lax.broadcasted_iota(jnp.int32, (rows, 128), 0))
                label = jnp.concatenate([label] * (2 * rows // 128), axis=1)
                scores = jnp.where(label == own_label, scores, absent)
            probs = jnp.exp(scores)
            grad_probs = dot_nt(values, grad_stack_ref[...])
            grad_scores = (probs * (grad_probs - delta_ref[...])).astype(bf16)
            sum_ref[...] += dot_tn(keys, grad_scores)

        places.over_blocks(half, True, functools.partial(step, mine_ref))
        places.over_blocks(half, False, functools.partial(step, theirs_ref))
        out_ref[...] = (heads_from_lanes(sum_ref[...]) * scale).T.astype(bf16)

    inputs = [owner, lengths, far(message), far(log_total), delta, far(mine), far(theirs), grad]
    return run_kernel(
        kernel,
        inputs,
        scalars() + [plain(item) for item in inputs[2:]],
        [((rows, local), bf16)],
        flops=64 * rows * count * rows * local,
        limit=16,
        scratch=[
            pltpu.VMEM((2 * rows, local), bf16),
            pltpu.VMEM((2 * rows, local), bf16),
            pltpu.VMEM((local, 2 * rows), f32),
        ],
    )[0]


def key_blocks(own_ref, queries_ref, block_ref, places, same_core, refs):
    keys_ref, values_ref, key_sum_ref, value_sum_ref = refs
    rows, local = own_ref.shape[0], own_ref.shape[1] // 2
    keys_ref[...] = head_stack(own_ref[:, :local])
    values_ref[...] = head_stack(own_ref[:, local:])
    own_label = places.label(places.own + lax.broadcasted_iota(jnp.int32, (rows, 128), 0))
    own_label = jnp.concatenate([own_label] * (rows // 128), axis=1)
    own_label = jnp.concatenate([own_label] * 2, axis=0)

    def spread(row):
        return jnp.concatenate(
            [
                jnp.broadcast_to(row[:, :rows], (rows, rows)),
                jnp.broadcast_to(row[:, rows:], (rows, rows)),
            ],
            axis=0,
        )

    def step(index, start, kind, scene):
        source = places.device_of(index, same_core)
        query = queries_ref[source, :rows, :]
        grad = block_ref[index, :rows, :]
        log_total = rows_back(queries_ref[source, rows:, :], 3, 2 * rows)
        delta = rows_back(block_ref[index, rows:, :], 3, 2 * rows)
        scores = dot_nt(keys_ref[...], query) - spread(log_total)
        if kind == "mixed":
            lanes = start + lax.broadcasted_iota(jnp.int32, (1, rows), 1)
            scores = jnp.where(own_label == places.label(lanes), scores, absent)
        probs = jnp.exp(scores)
        grad_probs = dot_nt(values_ref[...], grad)
        grad_scores = (probs * (grad_probs - spread(delta))).astype(bf16)
        value_part = dot_nn(probs.astype(bf16), grad)
        key_part = dot_nn(grad_scores, query)
        if kind == "scene":
            same = own_label[:, :local] == scene
            value_part = jnp.where(same, value_part, 0.0)
            key_part = jnp.where(same, key_part, 0.0)
        value_sum_ref[...] += value_part
        key_sum_ref[...] += key_part

    places.over_blocks(block_ref.shape[0], same_core, step)


def key_begin(queries, mine, key_value, owner, lengths):
    rows, local = key_value.shape[0], key_value.shape[1] // 2

    def kernel(
        owner_ref,
        lengths_ref,
        queries_ref,
        mine_ref,
        own_ref,
        key_sum_ref,
        value_sum_ref,
        keys_ref,
        values_ref,
    ):
        places = Places(owner_ref, lengths_ref, rows)
        key_sum_ref[...] = jnp.zeros(key_sum_ref.shape, f32)
        value_sum_ref[...] = jnp.zeros(value_sum_ref.shape, f32)
        refs = keys_ref, values_ref, key_sum_ref, value_sum_ref
        key_blocks(own_ref, queries_ref, mine_ref, places, True, refs)

    inputs = [owner, lengths, far(queries), mine, far(key_value)]
    return run_kernel(
        kernel,
        inputs,
        scalars() + [plain(item) for item in inputs[2:]],
        [((2 * rows, local), f32), ((2 * rows, local), f32)],
        flops=64 * rows * mine.shape[0] * rows * local,
        limit=16,
        scratch=[pltpu.VMEM((2 * rows, local), bf16), pltpu.VMEM((2 * rows, local), bf16)],
    )


def key_end(
    queries, theirs, key_value, sums, query_grad, qkv, layer, owner, lengths, unit
):
    rows, local = key_value.shape[0], key_value.shape[1] // 2
    width = qkv.shape[2]
    mp_count = lax.axis_size("mp")
    with_unit = unit is not None

    def kernel(
        owner_ref,
        lengths_ref,
        queries_ref,
        theirs_ref,
        own_ref,
        old_key_ref,
        old_value_ref,
        grad_ref,
        weight_ref,
        *refs,
    ):
        places = Places(owner_ref, lengths_ref, rows)
        if with_unit:
            unit_ref, refs = refs[0], refs[1:]
        part_ref, proj_ref, bias_ref, small_ref = refs[:4]
        keys_ref, values_ref, key_sum_ref, value_sum_ref = refs[4:]
        key_sum_ref[...] = old_key_ref[...]
        value_sum_ref[...] = old_value_ref[...]
        key_blocks(own_ref, queries_ref, theirs_ref, places, False, refs[4:])
        key_grad = heads_from_rows(key_sum_ref[...]).astype(bf16)
        value_grad = heads_from_rows(value_sum_ref[...]).astype(bf16)
        query_grad = grad_ref[...]
        proj_ref[:, :local] = query_grad
        proj_ref[:, local : 2 * local] = key_grad
        proj_ref[:, 2 * local :] = value_grad
        bias_ref[...] = jnp.zeros(bias_ref.shape, f32)
        bias_ref[0:1, :] = jnp.sum(query_grad.astype(f32), axis=0, keepdims=True)
        bias_ref[1:2, :] = jnp.sum(value_grad.astype(f32), axis=0, keepdims=True)
        part = dot_nt(query_grad, weight_ref[0, 0])
        part += dot_nt(key_grad, weight_ref[0, 1])
        part += dot_nt(value_grad, weight_ref[0, 2])
        low = part.astype(bf16)
        part_ref[...] = low.reshape(part_ref.shape)
        small_ref[...] = jnp.zeros(small_ref.shape, f32)
        if with_unit:
            into = low.astype(f32)
            small_ref[0:1, :] = jnp.sum(into * unit_ref[...], axis=0, keepdims=True)
            small_ref[1:2, :] = jnp.sum(into, axis=0, keepdims=True)

    inputs = [owner, lengths, far(queries), theirs, far(key_value)] + list(sums)
    inputs += [query_grad, far(qkv)]
    in_specs = scalars() + [plain(item) for item in inputs[2:8]] + [of_layer(qkv, layer)]
    if with_unit:
        inputs.append(far(unit))
        in_specs.append(plain(unit))
    return run_kernel(
        kernel,
        inputs,
        in_specs,
        [
            ((mp_count, rows // mp_count, width), bf16),
            ((rows, 3 * local), bf16, pltpu.HBM),
            ((8, local), f32, pltpu.HBM),
            ((8, width), f32, pltpu.HBM),
        ],
        flops=64 * rows * theirs.shape[0] * rows * local,
        limit=18,
        scratch=[
            pltpu.VMEM((2 * rows, local), bf16),
            pltpu.VMEM((2 * rows, local), bf16),
            pltpu.VMEM((2 * rows, local), f32),
            pltpu.VMEM((2 * rows, local), f32),
        ],
    )


def project(normed, qkv, bias, layer, first=None):
    rows, width = normed.shape
    local = qkv.shape[3]
    chips = lax.axis_size("dp") // 2
    own_rows = rows // lax.axis_size("mp")

    def kernel(normed_ref, weight_ref, bias_ref, *refs):
        if first is None:
            query_ref, pair_ref, spread_ref, kept_ref, sems = refs
            copies = keep_in_hbm([(normed_ref, kept_ref)], sems)
            normed = normed_ref[...]
        else:
            gain_ref, shift_ref, query_ref, pair_ref, spread_ref = refs[:5]
            own_ref, low_ref, unit_ref = refs[5:]
            centered, inverse = row_stats(normed_ref[...])
            unit = centered * inverse
            unit_ref[...] = unit
            normed = (unit * gain_ref[0:1, :] + shift_ref[0:1, :]).astype(bf16)
            low_ref[...] = normed
            own = pl.multiple_of(lax.axis_index("mp") * own_rows, own_rows)
            own_ref[...] = normed_ref[pl.ds(own, own_rows), :]
        query_bias, value_bias = (
            jnp.concatenate([bias_ref[0, at, 0:1, :], bias_ref[0, at, 1:2, :]], axis=1)
            for at in range(2)
        )
        query = dot_nn(normed, weight_ref[0, 0]) + query_bias
        query_ref[...] = query.astype(bf16)
        keys = dot_nn(normed, weight_ref[0, 1]).astype(bf16)
        values = (dot_nn(normed, weight_ref[0, 2]) + value_bias).astype(bf16)
        pair_ref[:, :local] = keys
        pair_ref[:, local:] = values
        for chip in range(chips):
            spread_ref[chip, :, :local] = keys
            spread_ref[chip, :, local:] = values
        if first is None:
            copies[0].wait()

    inputs = [normed, qkv, bias] if first is None else [far(normed), far(qkv), far(bias)]
    in_specs = [plain(normed), of_layer(qkv, layer), of_layer(bias, layer)]
    outputs = [
        ((rows, local), bf16),
        ((rows, 2 * local), bf16, pltpu.HBM),
        ((chips, rows, 2 * local), bf16),
    ]
    scratch = []
    if first is None:
        outputs.append((normed.shape, bf16, pltpu.HBM, True))
        scratch.append(pltpu.SemaphoreType.DMA((1,)))
    else:
        inputs += [far(item) for item in first]
        in_specs += [plain(item) for item in first]
        outputs += [
            ((own_rows, width), f32, pltpu.HBM),
            ((rows, width), bf16, pltpu.HBM),
            ((rows, width), f32, pltpu.HBM),
        ]
    return run_kernel(
        kernel, inputs, in_specs, outputs, flops=6 * rows * width * local, scratch=scratch
    )


def mlp_forward(normed, inner, inner_bias, down, layer):
    parts, part_rows, width = normed.shape
    rows, units = parts * part_rows, inner.shape[2]

    def kernel(
        normed_ref,
        inner_ref,
        bias_ref,
        down_ref,
        before_ref,
        active_ref,
        part_ref,
        kept_ref,
        sems,
    ):
        copies = keep_in_hbm([(normed_ref, kept_ref)], sems)
        own = normed_ref[...].reshape(rows, width)
        before = dot_nn(own, inner_ref[0]) + bias_ref[layer : layer + 1, :]
        before_ref[...] = before
        active = gelu(before).astype(bf16)
        active_ref[...] = active
        part_ref[...] = dot_nn(active, down_ref[0]).astype(bf16).reshape(part_ref.shape)
        copies[0].wait()

    inputs = [normed, far(inner), inner_bias, far(down)]
    return run_kernel(
        kernel,
        inputs,
        [plain(normed), of_layer(inner, layer), plain(inner_bias), of_layer(down, layer)],
        [
            ((rows, units), f32, pltpu.HBM),
            ((rows, units), bf16, pltpu.HBM),
            ((parts, part_rows, width), bf16),
            (normed.shape, bf16, pltpu.HBM, True),
        ],
        flops=4 * rows * width * units,
        scratch=[pltpu.SemaphoreType.DMA((1,))],
    )


def gelu(before):
    return 0.5 * before * (1.0 + lax.erf(before * math.sqrt(0.5)))


def gelu_slope(before):
    slope = 0.5 * (1.0 + lax.erf(before * math.sqrt(0.5)))
    return slope + before * jnp.exp(-0.5 * before * before) * (1.0 / math.sqrt(2.0 * math.pi))


def mlp_last(normed, cotangent, inner, inner_bias, down):
    parts, part_rows, width = normed.shape
    layer = inner.shape[0] - 1
    rows, units = parts * part_rows, inner.shape[2]

    def kernel(
        normed_ref,
        cotangent_ref,
        inner_ref,
        inner_bias_ref,
        down_ref,
        active_ref,
        out_ref,
        bias_ref,
        part_ref,
        own_ref,
        full_ref,
        kept_ref,
        sems,
    ):
        copies = keep_in_hbm([(normed_ref, kept_ref)], sems)
        grad = cotangent_ref[...].astype(bf16)
        full_ref[...] = grad.reshape(full_ref.shape)
        own = pl.multiple_of(lax.axis_index("mp") * part_rows, part_rows)
        own_ref[...] = cotangent_ref[pl.ds(own, part_rows), :]
        before = dot_nn(normed_ref[...].reshape(rows, width), inner_ref[0])
        before += inner_bias_ref[layer : layer + 1, :]
        out = (dot_nt(grad, down_ref[0]) * gelu_slope(before)).astype(bf16)
        out_ref[...] = out
        bias_ref[...] = jnp.broadcast_to(
            jnp.sum(out.astype(f32), axis=0, keepdims=True), bias_ref.shape
        )
        part = dot_nt(out, inner_ref[0]).astype(bf16)
        part_ref[:, :part_rows, :] = part.reshape(parts, part_rows, width)
        active = gelu(before).astype(bf16)
        active_ref[...] = active
        part = dot_nn(active, down_ref[0]).astype(bf16)
        part_ref[:, part_rows:, :] = part.reshape(parts, part_rows, width)
        copies[0].wait()

    inputs = [normed, far(cotangent), far(inner), inner_bias, far(down)]
    return run_kernel(
        kernel,
        inputs,
        [
            plain(normed),
            plain(cotangent),
            of_layer(inner, layer),
            plain(inner_bias),
            of_layer(down, layer),
        ],
        [
            ((rows, units), bf16, pltpu.HBM),
            ((rows, units), bf16, pltpu.HBM),
            ((8, units), f32, pltpu.HBM),
            ((parts, 2 * part_rows, width), bf16),
            ((part_rows, width), f32, pltpu.HBM),
            ((parts, part_rows, width), bf16, pltpu.HBM),
            (normed.shape, bf16, pltpu.HBM, True),
        ],
        flops=8 * rows * width * units,
        scratch=[pltpu.SemaphoreType.DMA((1,))],
    )


def mlp_backward(grad, before, inner, down, layer):
    parts, part_rows, width = grad.shape
    rows, units = parts * part_rows, inner.shape[2]

    def kernel(
        grad_ref, before_ref, inner_ref, down_ref, out_ref, bias_ref, part_ref, kept_ref, sems
    ):
        copies = keep_in_hbm([(grad_ref, kept_ref)], sems)
        into = dot_nt(grad_ref[...].reshape(rows, width), down_ref[0])
        out = (into * gelu_slope(before_ref[...])).astype(bf16)
        out_ref[...] = out
        bias_ref[...] = jnp.broadcast_to(
            jnp.sum(out.astype(f32), axis=0, keepdims=True), bias_ref.shape
        )
        part_ref[...] = dot_nt(out, inner_ref[0]).astype(bf16).reshape(part_ref.shape)
        copies[0].wait()

    inputs = [grad, before, inner, down]
    return run_kernel(
        kernel,
        inputs,
        [plain(grad), plain(before), of_layer(inner, layer), of_layer(down, layer)],
        [
            ((rows, units), bf16, pltpu.HBM),
            ((8, units), f32, pltpu.HBM),
            ((parts, part_rows, width), bf16),
            (grad.shape, bf16, pltpu.HBM, True),
        ],
        flops=4 * rows * width * units,
        scratch=[pltpu.SemaphoreType.DMA((1,))],
    )


def token_products(pairs):
    columns = [right.shape[-1] for left, right in pairs]
    width = pairs[0][0].shape[-1]
    rows = pairs[0][1].shape[0]
    items = [item for pair in pairs for item in pair]
    count = len(items)
    dp_count = lax.axis_size("dp")
    split = (dp_count // 4, 2, 2, width // dp_count)

    def kernel(*refs):
        sources, out_ref, held, parts = refs[:count], refs[count], refs[count + 1 : -2], refs[-2:]
        results, sems = held[count:], parts[0]
        out_sems = parts[1]
        copies = keep_in_hbm(zip(sources, held[:count]), sems)
        writes = []
        at = 0
        for index, size in enumerate(columns):
            copies[2 * index].wait()
            copies[2 * index + 1].wait()
            left = held[2 * index][...].reshape(rows, width)
            result = dot_tn(left, held[2 * index + 1][...]).astype(bf16)
            results[index][...] = result.reshape(split + (size,))
            for x in range(2):
                for core in range(2):
                    write = pltpu.make_async_copy(
                        results[index].at[:, x, core],
                        out_ref.at[:, core, x, :, pl.ds(at, size)],
                        out_sems.at[4 * index + 2 * x + core],
                    )
                    write.start()
                    writes.append(write)
            at += size
        for write in writes:
            write.wait()

    return run_kernel(
        kernel,
        [far(item) for item in items],
        [whole(pltpu.HBM)] * count,
        [(split + (sum(columns),), bf16, pltpu.HBM, True)],
        flops=2 * rows * width * sum(columns),
        scratch=[pltpu.VMEM(item.shape, item.dtype) for item in items]
        + [pltpu.VMEM(split + (size,), bf16) for size in columns]
        + [pltpu.SemaphoreType.DMA((count,)), pltpu.SemaphoreType.DMA((4 * len(pairs),))],
    )[0].reshape(width, sum(columns))


def last_products(pairs, norm_one, norm_two, key_small, own_cotangent, proj_bias, inner_bias):
    width = own_cotangent.shape[1]
    dp_count = lax.axis_size("dp")
    columns = width // dp_count
    token_rows = pairs[0][1].shape[0]
    total = sum(right.shape[-1] for left, right in pairs)
    items = [item for pair in pairs for item in pair]
    inputs = items + [norm_one, norm_two[0], norm_two[1], key_small, own_cotangent]
    inputs = [far(item) for item in inputs + proj_bias + inner_bias]

    def kernel(*refs):
        item_refs, refs = refs[: len(items)], refs[len(items) :]
        one_ref, two_a_ref, two_b_ref, key_ref, grad_ref = refs[:5]
        proj_refs, inner_refs = refs[5:7], refs[7:9]
        mine_ref, away_ref, first_ref, second_ref, product_ref = refs[9:]
        at = 0
        for left_ref, right_ref in zip(item_refs[0::2], item_refs[1::2]):
            left = left_ref[...].reshape(token_rows, width)
            size = right_ref.shape[-1]
            product_ref[:, at : at + size] = dot_tn(left, right_ref[...]).astype(bf16)
            at += size
        last = jnp.sum(grad_ref[...].astype(bf16).astype(f32), axis=0, keepdims=True)
        zero = jnp.zeros((2, width), f32)
        for target, two_ref, gains, bias in (
            (first_ref, two_a_ref, key_ref, one_ref[2:3, :]),
            (second_ref, two_b_ref, one_ref, last),
        ):
            target[0:2, :] = gains[0:2, :]
            target[2:3, :] = two_ref[2:3, :]
            target[3:5, :] = two_ref[0:2, :]
            target[5:6, :] = bias
            target[6:8, :] = zero
        lines = [proj_refs[layer][row : row + 1, :] for layer in range(2) for row in range(2)]
        for layer in range(2):
            lines += [inner_refs[layer][0:1, 128 * at : 128 * at + 128] for at in range(4)]
        row_index = lax.broadcasted_iota(jnp.int32, (8, 128), 0)
        shared = []
        for group in (lines[:8], lines[8:]):
            tile = jnp.zeros((8, 128), f32)
            for row, line in enumerate(group):
                tile = jnp.where(row_index == row, jnp.broadcast_to(line, (8, 128)), tile)
            shared.append(tile)
        core = lax.rem(lax.axis_index("dp"), 2)
        for device in range(dp_count):
            at = slice(device * columns, (device + 1) * columns)
            small = jnp.concatenate([first_ref[:, at], second_ref[:, at]] + shared, axis=1)
            high = small.astype(bf16).astype(f32)
            tail = jnp.concatenate([high, small - high], axis=0).astype(bf16)
            for flag, ref in ((core == device % 2, mine_ref), (core != device % 2, away_ref)):

                @pl.when(flag)
                def _(ref=ref, tail=tail, device=device, at=at):
                    ref[device // 2, :columns, :] = product_ref[at, :]
                    ref[device // 2, columns:, :] = tail

    shape = ((dp_count // 2, columns + 16, total), bf16)
    return run_kernel(
        kernel,
        inputs,
        [plain(item) for item in inputs],
        [shape, shape],
        flops=2 * token_rows * width * total,
        scratch=[
            pltpu.VMEM((8, width), f32),
            pltpu.VMEM((8, width), f32),
            pltpu.VMEM((width, total), bf16),
        ],
    )


def add_cores(mine, other, columns, output):
    parts, part_rows, width = output.shape

    def kernel(mine_ref, other_ref, low_ref, out_ref, output_ref):
        for chip in range(mine.shape[0]):
            both = mine_ref[chip].astype(f32) + other_ref[chip].astype(f32)
            out_ref[chip, :columns, :] = both[:columns].astype(bf16)
            small = both[columns : columns + 8] + both[columns + 8 :]
            high = small.astype(bf16).astype(f32)
            out_ref[chip, columns:, :] = jnp.concatenate([high, small - high], axis=0).astype(bf16)
        output_ref[...] = low_ref[...].astype(f32).reshape(parts * part_rows, width)

    return run_kernel(
        kernel,
        [mine, other, far(output)],
        [plain(mine), plain(other), plain(output)],
        [(mine.shape, bf16), ((parts * part_rows, width), f32, pltpu.HBM)],
    )


def own_half(pieces):
    shape = pieces.shape[1:]

    def kernel(pieces_ref, mine_ref, away_ref):
        x = lax.rem(lax.div(lax.axis_index("dp"), 2), 2)
        mine_ref[...] = pieces_ref[x]
        away_ref[...] = pieces_ref[1 - x]

    return run_kernel(
        kernel, [far(pieces)], [plain(pieces)], [(shape, bf16, pltpu.HBM), (shape, bf16)]
    )


def scatter_sum(pairs):
    count = lax.axis_size("dp")
    groups = [[4 * z + 2 * x + core for z in range(count // 4) for core in range(2)] for x in range(2)]
    pieces = lax.psum_scatter(
        token_products(pairs), "dp", scatter_dimension=0, tiled=True, axis_index_groups=groups
    )
    mine, away = own_half(pieces.reshape(2, -1, pieces.shape[1]))
    return mine, lax.ppermute(away, "dp", [(index, index ^ 2) for index in range(count)])


def finish_rows(got, width):
    parts, own_rows = got.shape[:2]

    def kernel(got_ref, out_ref, *small_refs):
        total = jnp.zeros((8, 128), f32)
        for part in range(parts):
            at = slice(part * own_rows, (part + 1) * own_rows)
            out_ref[at, :] = got_ref[part, :, :width].astype(f32)
            both = got_ref[part, :16, width:].astype(f32)
            total += both[:8] + both[8:]
        for index, small_ref in enumerate(small_refs):
            small_ref[0:1, :] = total[index : index + 1, :64]
            small_ref[1:2, :] = total[index : index + 1, 64:]

    return run_kernel(
        kernel,
        [got],
        [plain(got)],
        [((parts * own_rows, width), f32, pltpu.HBM)] + [((2, 64), f32, pltpu.HBM)] * 6,
    )


def finish_biases(third, columns):
    bias_columns = columns // lax.axis_size("dp")

    def kernel(third_ref, small_ref):
        small = jnp.zeros((8, third.shape[2]), f32)
        for chip in range(third.shape[0]):
            piece = third_ref[chip, columns:, :].astype(f32)
            small += piece[:8] + piece[8:]
        small = jnp.concatenate([small[:, 128:256], small[:, 256:384]], axis=0)
        lane = lax.broadcasted_iota(jnp.int32, small.shape, 1)
        own = lax.axis_index("dp") * bias_columns
        picked = jnp.zeros(small.shape, f32)
        for half in range(2):
            for column in range(bias_columns):
                at = half * 64 + own + column
                value = jnp.sum(jnp.where(lane == at, small, 0.0), axis=1, keepdims=True)
                picked = jnp.where(lane == half * bias_columns + column, value, picked)
        small_ref[...] = picked

    return run_kernel(kernel, [third], [plain(third)], [((16, 128), f32)])[0]


def finish_weights(first, second, third, local, units):
    columns = first[0].shape[0]

    def kernel(first_ref, first_other_ref, second_ref, second_other_ref, third_ref, qkv_ref, out_ref, inner_ref, down_ref):
        last = add_parts(third_ref)
        middle = first_ref[...].astype(f32) + first_other_ref[...].astype(f32)
        late = second_ref[...].astype(f32) + second_other_ref[...].astype(f32)
        for layer, sums in ((1, middle), (0, late)):
            inner_ref[layer] = sums[:, :units]
            down_ref[layer] = sums[:, units : 2 * units]
            out_ref[layer] = sums[:, 2 * units : 2 * units + local]
        for piece in range(3):
            at = 2 * units + local * (piece + 1)
            qkv_ref[1, piece] = middle[:, at : at + local]
            qkv_ref[0, piece] = last[:columns, local * piece : local * (piece + 1)]

    inputs = list(first) + list(second) + [third]
    return run_kernel(
        kernel,
        inputs,
        [plain(item) for item in inputs],
        [
            ((2, 3, columns, local), f32, pltpu.HBM),
            ((2, columns, local), f32, pltpu.HBM),
            ((2, columns, units), f32, pltpu.HBM),
            ((2, columns, units), f32, pltpu.HBM),
        ],
    )


def body(
    hidden_in,
    cotangent,
    scene_lengths,
    block_owner,
    attn_gain,
    attn_shift,
    qkv_weight,
    qv_bias,
    out_weight,
    out_bias,
    mlp_gain,
    mlp_shift,
    mlp_in_weight,
    mlp_in_bias,
    mlp_out_weight,
    mlp_out_bias,
):
    rows, width = hidden_in.shape
    layers = attn_gain.shape[0]
    local = qv_bias.shape[2] * qv_bias.shape[3]
    units = mlp_in_bias.shape[1]
    dp_count, mp_count = lax.axis_size("dp"), lax.axis_size("mp")
    own_rows = rows // mp_count
    qkv = qkv_weight.transpose(0, 2, 1, 3)
    where = (block_owner, scene_lengths)
    Cost.weight = 0.0

    kept = []
    for layer in range(layers):
        if layer:
            query, pair, spread, normed = project(normed, qkv, qv_bias, layer)
            spread = after(spread, queries)
        else:
            query, pair, spread, hidden, normed, unit = project(
                hidden_in, qkv, qv_bias, layer, (attn_gain, attn_shift)
            )
        mine = gather_chips(spread)
        theirs = from_other_core(mine)
        *state, mine = attention_begin(query, mine, *where)
        part, attended_low, flat, log_total, message, theirs = attention_end(
            query, theirs, state, out_weight, layer, *where
        )
        got = exchange_mp(part)
        queries = lax.all_gather(after(message, got), "dp", axis=0, tiled=True)
        queries = queries.reshape((dp_count,) + message.shape)
        middle, spread = residual_norm(
            got, hidden, out_bias, layer, mlp_gain, mlp_shift, layer
        )
        normed_mlp = exchange_mp(spread)
        if layer + 1 < layers:
            before, active, part, normed_mlp = mlp_forward(
                normed_mlp, mlp_in_weight, mlp_in_bias, mlp_out_weight, layer
            )
        kept.append(
            dict(
                hidden=hidden,
                normed=normed,
                pair=pair,
                mine=mine,
                theirs=theirs,
                attended_low=attended_low,
                flat=flat,
                log_total=log_total,
                message=message,
                queries=queries,
                middle=middle,
                normed_mlp=normed_mlp,
                before=before,
                active=active,
            )
        )
        if layer + 1 < layers:
            hidden, spread = residual_norm(
                exchange_mp(part), middle, mlp_out_bias, layer, attn_gain, attn_shift, layer + 1
            )
            normed = exchange_mp(spread).reshape(rows, width)
    norm_one, norm_two, bias_proj, bias_inner = {}, {}, {}, {}
    for layer in reversed(range(layers)):
        now = kept[layer]
        if layer == layers - 1:
            (
                now["active"],
                grad_before,
                bias_inner[layer],
                part,
                grad_own,
                grad_full,
                now["normed_mlp"],
            ) = mlp_last(now["normed_mlp"], cotangent, mlp_in_weight, mlp_in_bias, mlp_out_weight)
            own_cotangent = grad_own
        else:
            grad_before, bias_inner[layer], part, grad_full = mlp_backward(
                grad_full, now["before"], mlp_in_weight, mlp_out_weight, layer
            )
        mlp_pairs = [(now["normed_mlp"], grad_before), (grad_full, now["active"])]
        middle_grad, spread, norm_two[layer] = norm_backward(
            exchange_mp(part),
            now["middle"],
            mlp_gain,
            layer,
            grad_own,
            bias=mlp_out_bias if layer == layers - 1 else None,
        )
        if layer == layers - 1:
            spread = after(spread, now["queries"])
        spread, grad_rows, delta, branch, *ridden = grad_attended(
            exchange_mp(spread), out_weight, layer, now["flat"]
        )
        if ridden:
            output = ridden[0]
        grad_mine = gather_chips(spread)
        query_grad = query_side(
            now["message"], now["log_total"], delta, now["mine"], now["theirs"], grad_rows, *where
        )
        grad_theirs = from_other_core(after(grad_mine, query_grad))
        sums = key_begin(now["queries"], grad_mine, now["pair"], *where)
        part, proj_grad, bias_proj[layer], key_small = key_end(
            now["queries"],
            grad_theirs,
            now["pair"],
            sums,
            query_grad,
            qkv,
            layer,
            *where,
            unit if layer == 0 else None,
        )
        if layer:
            Cost.weight = 9.5
        out_pairs = [(branch, now["attended_low"])]
        proj_pairs = [(now["normed"], proj_grad)]
        if layer:
            grad_own, spread, norm_one[layer] = norm_backward(
                exchange_mp(part), now["hidden"], attn_gain, layer, middle_grad
            )
            grad_full = exchange_mp(spread)
            first = scatter_sum(mlp_pairs + out_pairs + proj_pairs)
        else:
            second = scatter_sum(mlp_pairs + out_pairs)
            mine, away = last_products(
                proj_pairs,
                norm_one[1],
                norm_two,
                key_small,
                own_cotangent,
                [bias_proj[0], bias_proj[1]],
                [bias_inner[0], bias_inner[1]],
            )
            both, output = add_cores(mine, from_other_core(away), width // dp_count, output)
            got = exchange_mp(part)
            third = gather_chips(after(both, got, first[1]))
            ignored, spread, ignored = norm_backward(
                got, now["hidden"], attn_gain, layer, middle_grad, third
            )
            tail = exchange_mp(spread)

    small = finish_biases(third, width // dp_count)
    qkv_grad, out_grad, inner_grad, down_grad = finish_weights(
        first, second, third, local, units
    )
    (
        input_grad,
        gain_one,
        shift_one,
        out_bias_grad,
        gain_two,
        shift_two,
        down_bias_grad,
    ) = finish_rows(tail, width)
    bias_columns = qv_bias.shape[3] // dp_count
    qv_grad = small[:4, : 2 * bias_columns].reshape(layers, 2, 2, bias_columns)
    inner_bias_grad = small[4:12, : 2 * bias_columns].reshape(layers, units // 64, bias_columns)
    return (
        output,
        input_grad,
        gain_one,
        shift_one,
        qkv_grad.transpose(0, 2, 1, 3),
        qv_grad,
        out_grad.transpose(0, 2, 1),
        out_bias_grad,
        gain_two,
        shift_two,
        inner_grad,
        inner_bias_grad,
        down_grad.transpose(0, 2, 1),
        down_bias_grad,
    )


def solution(mesh):
    in_specs = (
        P("dp", None),
        P("dp", None),
        P(),
        P(),
        P(),
        P(),
        P(None, None, None, "mp"),
        P(None, None, "mp", None),
        P(None, "mp", None),
        P(),
        P(),
        P(),
        P(None, None, "mp"),
        P(None, "mp"),
        P(None, "mp", None),
        P(),
    )
    out_specs = (
        P("dp", None),
        P("dp", None),
        P(None, "dp"),
        P(None, "dp"),
        P(None, "dp", None, "mp"),
        P(None, None, "mp", "dp"),
        P(None, "mp", "dp"),
        P(None, "dp"),
        P(None, "dp"),
        P(None, "dp"),
        P(None, "dp", "mp"),
        P(None, "mp", "dp"),
        P(None, "mp", "dp"),
        P(None, "dp"),
    )
    return jax.shard_map(body, mesh=mesh, in_specs=in_specs, out_specs=out_specs, check_vma=False)
```
